128 devices in a mesh: batch: 32 (over y, z, core), tp: 4 (over x).
Axes of the slice: x: 4, y: 4, z: 4, core: 2. Of those that a mesh axis runs over, the one named last changes fastest.
Arguments:
- inputs: bfloat16 [32768, 768], P(('batch', 'tp')), may hold values from -6 to 6
- side_start: float32 [32768, 96], P('batch'), may hold values from -6 to 6
- lengths: int32 [64], P('batch'), may hold values from 1 to 512, as said below
- offset_bias: bfloat16 [12, 1023], replicated, may hold values from -4 to 4
- gain_attn: bfloat16 [2, 768], replicated, may hold values from 0.099609375 to 1.8984375
- w_query: bfloat16 [2, 768, 768], P(None, None, 'tp'), may hold values from -0.21875 to 0.21875
- w_key: bfloat16 [2, 768, 768], P(None, None, 'tp'), may hold values from -0.21875 to 0.21875
- w_value: bfloat16 [2, 768, 768], P(None, None, 'tp'), may hold values from -0.21875 to 0.21875
- w_out: bfloat16 [2, 768, 768], P(None, 'tp'), may hold values from -0.875 to 0.875
- gain_ffn: bfloat16 [2, 768], replicated, may hold values from 0.099609375 to 1.8984375
- w_inner: bfloat16 [2, 768, 3072], P(None, None, 'tp'), may hold values from -0.21875 to 0.21875
- w_outer: bfloat16 [2, 3072, 768], P(None, 'tp'), may hold values from -0.109375 to 0.109375
- narrowing_weight: bfloat16 [2, 768, 96], replicated, may hold values from -0.21875 to 0.21875
- gate_logit: float32 [2, 96], replicated, may hold values from -5 to 5
- side_gain1: float32 [2, 96], replicated, may hold values from 0.1 to 1.9
- side_qkv: float32 [2, 96, 288], replicated, may hold values from -0.625 to 0.625
- side_proj: float32 [2, 96, 96], replicated, may hold values from -2.5 to 2.5
- side_gain2: float32 [2, 96], replicated, may hold values from 0.1 to 1.9
- side_inner: float32 [2, 96, 384], replicated, may hold values from -0.625 to 0.625
- side_outer: float32 [2, 384, 96], replicated, may hold values from -0.3125 to 0.3125
- side_cotangent: float32 [32768, 96], P('batch'), may hold values from -6 to 6
Outputs:
- backbone_out: bfloat16 [32768, 768], P(('batch', 'tp'))
- side_out: float32 [32768, 96], P('batch')
- grad_inputs: float32 [32768, 768], P(('batch', 'tp'))
- grad_side_start: float32 [32768, 96], P('batch')
- grad_w_down: float32 [2, 768, 96], replicated
- grad_gate_logit: float32 [2, 96], replicated
- grad_side_gain1: float32 [2, 96], replicated
- grad_side_qkv: float32 [2, 96, 288], replicated
- grad_side_proj: float32 [2, 96, 96], replicated
- grad_side_gain2: float32 [2, 96], replicated
- grad_side_inner: float32 [2, 96, 384], replicated
- grad_side_outer: float32 [2, 384, 96], replicated
The draws below stay inside these ranges and needn't reach their ends.
Inputs may be any that keep to these rules, and one draw needn't show every extreme that they name: `lengths`: of the 2 sequences of each index of batch, one, drawn from the seed, has length 512.
All inputs are finite; a program needn't handle non-finite values.
Results may differ from the reference program's by a relative error of at most 0.035.
Values may be sent and summed in bfloat16 or wider, within the bound.
A program may use at most 256 MiB of HBM per device.

```python
import math
from functools import partial
import jax
import jax.numpy as jnp
from jax import lax

D = 768
HEADS = 12
FF = 3072
SIDE_W = 96
SIDE_FF = 384
LAYERS = 2
SEQ_LEN = 512
SEQ_DEV = 2
SEQS = 64
TOKENS = 32768


def draw_lengths(key, part):
    key = jax.random.fold_in(key, 7)
    first_key, second_key, third_key, fourth_key = jax.random.split(key, 4)
    first_draw = jax.random.randint(first_key, (SEQS,), 0, SEQ_LEN)
    second_draw = jax.random.randint(second_key, (SEQS,), 0, SEQ_LEN)
    third_draw = jax.random.randint(third_key, (SEQS,), 0, SEQ_LEN)
    short_length = 1 + first_draw * second_draw // SEQ_LEN * third_draw // SEQ_LEN
    chosen = jax.random.randint(fourth_key, (SEQS // SEQ_DEV,), 0, SEQ_DEV)
    longest = jnp.arange(SEQS) % SEQ_DEV == jnp.repeat(chosen, SEQ_DEV)
    return jnp.where(longest, SEQ_LEN, short_length).astype(jnp.int32)


def levels(rng, extent, pieces, least, largest):
    gain = 1.0
    for dim, shards_of in pieces:
        draws = jax.random.uniform(jax.random.fold_in(jax.random.fold_in(rng, 6), dim), (shards_of,), jnp.float32, least / len(pieces), largest / len(pieces))
        gain = gain * jnp.repeat(jnp.exp(draws), extent[dim] // shards_of).reshape((-1,) + (1,) * (len(extent) - 1 - dim))
    return gain


def centred(stream_key, extent, spread, limit, cuts=(), held_as=jnp.bfloat16):
    drawn = jax.random.normal(stream_key, extent, jnp.float32) * spread
    if len(cuts) > 0:
        drawn = levels(stream_key, extent, cuts, -0.22, 0.18) * drawn
    return jnp.clip(drawn, min=-limit, max=limit).astype(held_as)


def setup_inputs(seed: int = 0) -> dict:
    arg_keys = jax.random.split(jax.random.key(seed), 22)
    inputs = centred(arg_keys[0], (TOKENS, D), 1.0, 6.0, ((0, 128),))
    side_start = centred(arg_keys[1], (TOKENS, SIDE_W), 1.0, 6.0, ((0, 32),), jnp.float32)
    lengths = draw_lengths(jax.random.fold_in(arg_keys[21], 71), 0)
    offset_bias = centred(arg_keys[3], (HEADS, 2 * SEQ_LEN - 1), 1.0, 4.0)
    gain_attn = jnp.clip(1.0 + 0.18 * jax.random.normal(arg_keys[4], (LAYERS, D), jnp.float32), 0.099609375, 1.8984375).astype(jnp.bfloat16)
    w_query = centred(arg_keys[5], (LAYERS, D, D), D ** -0.5, 0.21875, ((2, 4),))
    w_key = centred(arg_keys[6], (LAYERS, D, D), D ** -0.5, 0.21875, ((2, 4),))
    w_value = centred(arg_keys[7], (LAYERS, D, D), D ** -0.5, 0.21875, ((2, 4),))
    w_out = centred(arg_keys[8], (LAYERS, D, D), (D // 16) ** -0.5, 0.875, ((1, 4),))
    gain_ffn = jnp.clip(1.0 + 0.18 * jax.random.normal(arg_keys[9], (LAYERS, D), jnp.float32), 0.099609375, 1.8984375).astype(jnp.bfloat16)
    w_inner = centred(arg_keys[10], (LAYERS, D, FF), D ** -0.5, 0.21875, ((2, 4),))
    w_outer = centred(arg_keys[11], (LAYERS, FF, D), FF ** -0.5, 0.109375, ((1, 4),))
    narrowing_weight = centred(arg_keys[12], (LAYERS, D, SIDE_W), D ** -0.5, 0.21875)
    gate_logit = centred(arg_keys[13], (LAYERS, SIDE_W), 1.5, 5.0, (), jnp.float32)
    side_gain1 = jnp.clip(1.0 + 0.18 * jax.random.normal(arg_keys[14], (LAYERS, SIDE_W), jnp.float32), 0.1, 1.9)
    side_qkv = centred(arg_keys[15], (LAYERS, SIDE_W, 3 * SIDE_W), SIDE_W ** -0.5, 0.625, (), jnp.float32)
    side_proj = centred(arg_keys[16], (LAYERS, SIDE_W, SIDE_W), (SIDE_W // 16) ** -0.5, 2.5, (), jnp.float32)
    side_gain2 = jnp.clip(1.0 + 0.18 * jax.random.normal(arg_keys[17], (LAYERS, SIDE_W), jnp.float32), 0.1, 1.9)
    side_inner = centred(arg_keys[18], (LAYERS, SIDE_W, SIDE_FF), SIDE_W ** -0.5, 0.625, (), jnp.float32)
    side_outer = centred(arg_keys[19], (LAYERS, SIDE_FF, SIDE_W), SIDE_FF ** -0.5, 0.3125, (), jnp.float32)
    side_cotangent = centred(arg_keys[20], (TOKENS, SIDE_W), 1.0, 6.0, ((0, 32),), jnp.float32)
    return dict(inputs=inputs, side_start=side_start, lengths=lengths, offset_bias=offset_bias, gain_attn=gain_attn, w_query=w_query, w_key=w_key, w_value=w_value, w_out=w_out, gain_ffn=gain_ffn, w_inner=w_inner, w_outer=w_outer, narrowing_weight=narrowing_weight, gate_logit=gate_logit, side_gain1=side_gain1, side_qkv=side_qkv, side_proj=side_proj, side_gain2=side_gain2, side_inner=side_inner, side_outer=side_outer, side_cotangent=side_cotangent)


EPSILON = 1e-06
BACKBONE_SCALE = 0.125
HIGHEST = lax.Precision.HIGHEST
NEGATIVE = -1e+30

@jax.custom_vjp
def low(v):
    return lax.optimization_barrier(v.astype(jnp.bfloat16)).astype(jnp.float32)

@jax.custom_vjp
def low_back(v):
    return v

def low_keep(v):
    return (low(v), None)

def low_pass(kept, grad):
    return (grad,)

def back_keep(v):
    return (v, None)

def back_low(kept, grad):
    return (low(grad),)
low.defvjp(low_keep, low_pass)
low_back.defvjp(back_keep, back_low)

def rms_norm(values, gain_row):
    return values * lax.rsqrt(lax.optimization_barrier(jnp.mean(values * values, axis=-1, keepdims=True)) + EPSILON) * gain_row

def gelu_tanh(values):
    return jax.nn.gelu(values, approximate=True)

def offset_table(offset_bias, positions):
    head_count = offset_bias.shape[0]
    span = 2 * positions - 1
    tiled = jnp.tile(offset_bias, (1, positions + 1))
    window = tiled[:, positions - 1:positions - 1 + positions * (span - 1)]
    return window.reshape(head_count, positions, span - 1)[:, :, :positions]

def side_attend(bias_table, score_scale, side_packed):
    side_queries, side_keys, side_values, side_length = side_packed
    side_scores = jnp.einsum('qhd,khd->hqk', side_queries, side_keys, precision=HIGHEST) * score_scale + bias_table
    side_valid = jnp.arange(side_keys.shape[0]) < side_length
    side_scores = jnp.where(side_valid[None, None, :], side_scores, NEGATIVE)
    side_max = lax.optimization_barrier(jnp.max(side_scores, axis=-1, keepdims=True))
    side_exp = jnp.exp(side_scores - side_max)
    side_probs = side_exp / lax.optimization_barrier(jnp.sum(side_exp, axis=-1, keepdims=True))
    return jnp.einsum('hqk,khd->qhd', side_probs, side_values, precision=HIGHEST)

def side_layer(side_weights, narrowed_rows, prior_state, bias_table, lengths):
    gate_row, first_gain, triple_weight, mixer_weight, second_gain, expand_weight, shrink_weight = side_weights
    mixing = jax.nn.sigmoid(gate_row)
    side_joined = mixing * narrowed_rows + (1.0 - mixing) * prior_state
    side_normed = rms_norm(side_joined, first_gain)
    sequences = lengths.shape[0]
    token_rows = side_joined.shape[0]
    side_width = side_joined.shape[1]
    head_count = bias_table.shape[0]
    head_size = side_width // head_count
    side_projected = jnp.dot(side_normed, triple_weight, precision=HIGHEST).reshape(sequences, token_rows // sequences, 3, head_count, head_size)
    attend_one = jax.checkpoint(partial(side_attend, bias_table, 1.0 / math.sqrt(head_size)))
    side_mixed = lax.map(attend_one, (side_projected[:, :, 0], side_projected[:, :, 1], side_projected[:, :, 2], lengths))
    side_joined = side_joined + jnp.dot(side_mixed.reshape(token_rows, side_width), mixer_weight, precision=HIGHEST)
    side_second = rms_norm(side_joined, second_gain)
    side_expanded = gelu_tanh(jnp.dot(side_second, expand_weight, precision=HIGHEST))
    return side_joined + jnp.dot(side_expanded, shrink_weight, precision=HIGHEST)

def backbone_attend(bias_table, packed):
    queries, key_rows, values, seq_length = packed
    scores = low_back(jnp.einsum('qhd,khd->hqk', queries, key_rows, precision=HIGHEST) * BACKBONE_SCALE + bias_table)
    valid_keys = jnp.arange(key_rows.shape[0]) < seq_length
    scores = jnp.where(valid_keys[None, None, :], scores, NEGATIVE)
    row_max = lax.optimization_barrier(jnp.max(scores, axis=-1, keepdims=True))
    weights_exp = jnp.exp(scores - row_max)
    probabilities = low(weights_exp / lax.optimization_barrier(jnp.sum(weights_exp, axis=-1, keepdims=True)))
    mixed_heads = jnp.einsum('hqk,khd->qhd', probabilities, values, precision=HIGHEST)
    return low(low_back(mixed_heads))

def backbone(residual, frozen_layer, bias_table, lengths):
    gain_one, query_weight, key_weight, value_weight, out_weight, gain_two, inner_weight, outer_weight = frozen_layer
    sequences = lengths.shape[0]
    token_rows = residual.shape[0]
    width = residual.shape[1]
    head_count = bias_table.shape[0]
    head_size = width // head_count
    normed = low(rms_norm(residual, gain_one))
    shape_heads = (sequences, token_rows // sequences, head_count, head_size)
    queries = low(low_back(jnp.dot(normed, query_weight, precision=HIGHEST))).reshape(shape_heads)
    key_rows = low(low_back(jnp.dot(normed, key_weight, precision=HIGHEST))).reshape(shape_heads)
    values = low(low_back(jnp.dot(normed, value_weight, precision=HIGHEST))).reshape(shape_heads)
    attend_one = jax.checkpoint(partial(backbone_attend, bias_table))
    mixed_heads = lax.map(attend_one, (queries, key_rows, values, lengths)).reshape(token_rows, width)
    residual = residual + low_back(jnp.dot(mixed_heads, out_weight, precision=HIGHEST))
    normed = low(rms_norm(residual, gain_two))
    hidden = low_back(jnp.dot(normed, inner_weight, precision=HIGHEST))
    active = low(gelu_tanh(hidden))
    return residual + low_back(jnp.dot(active, outer_weight, precision=HIGHEST))

def reference(inputs, side_start, lengths, offset_bias, gain_attn, w_query, w_key, w_value, w_out, gain_ffn, w_inner, w_outer, narrowing_weight, gate_logit, side_gain1, side_qkv, side_proj, side_gain2, side_inner, side_outer, side_cotangent):
    bias_table = offset_table(offset_bias.astype(jnp.float32), SEQ_LEN)
    frozen = [gain_attn, w_query, w_key, w_value, w_out, gain_ffn, w_inner, w_outer]
    frozen = [weight.astype(jnp.float32) for weight in frozen]

    def forward(residual, side_state, reduce_matrix, gates, gains_first, triple_all, mixer_all, gains_second, expand_all, shrink_all):
        for layer_position in range(LAYERS):
            frozen_layer = [weight[layer_position] for weight in frozen]
            residual = backbone(residual, frozen_layer, bias_table, lengths)
            narrowed_rows = low(low_back(jnp.dot(low(residual), reduce_matrix[layer_position], precision=HIGHEST)))
            side_weights = (gates[layer_position], gains_first[layer_position], triple_all[layer_position], mixer_all[layer_position], gains_second[layer_position], expand_all[layer_position], shrink_all[layer_position])
            side_state = side_layer(side_weights, narrowed_rows, side_state, bias_table, lengths)
        return (side_state, residual)
    side_out, pullback, backbone_last = jax.vjp(forward, inputs.astype(jnp.float32), side_start, narrowing_weight.astype(jnp.float32), gate_logit, side_gain1, side_qkv, side_proj, side_gain2, side_inner, side_outer, has_aux=True)
    grads = pullback(side_cotangent)
    return (backbone_last.astype(jnp.bfloat16), side_out, grads[0], grads[1], grads[2], grads[3], grads[4], grads[5], grads[6], grads[7], grads[8], grads[9])
```

```python
from functools import partial
import math

import jax
import jax.numpy as jnp
from jax import lax
from jax.experimental import pallas as pl
from jax.experimental.pallas import tpu as pltpu
from jax.sharding import PartitionSpec as P


BF = jnp.bfloat16
F32 = jnp.float32
EPSILON = 1e-06
NEGATIVE = -1e30
HIGHEST = lax.Precision.HIGHEST
MESH = pl.DeviceIdType.MESH
TP = 4
SIDES = 4
HALF = 256
WIDTH = 768
SIDE_W = 96
SIDE_FF = 384
SIDE_SCALE = 1.0 / math.sqrt(8)
GELU_K = math.sqrt(2.0 / math.pi)
VMEM_BYTES = 56 * 1024 * 1024

A_PROJ, A_INNER, A_OUTER, A_SMALL, A_ROWS = 0, 96, 384, 672, 688
B_QKV, B_DOWN, B_SMALL, B_ROWS = 0, 288, 864, 880
LAYER_ROWS = A_ROWS + B_ROWS
SUM_ROWS = 3584


def dot(a, b, ca, cb, precision=None):
    return lax.dot_general(
        a, b, (((ca,), (cb,)), ((), ())), preferred_element_type=F32, precision=precision
    )


def nn(a, b, precision=None):
    return dot(a, b, 1, 0, precision)


def nt(a, b, precision=None):
    return dot(a, b, 1, 1, precision)


def tn(a, b, precision=None):
    return dot(a, b, 0, 0, precision)


def rms_scale(values):
    return lax.rsqrt(jnp.mean(values * values, axis=-1, keepdims=True) + EPSILON)


def rms_back(values, gain_row, grad):
    scale = rms_scale(values)
    scaled = grad * gain_row
    inner = jnp.mean(scaled * values, axis=-1, keepdims=True)
    return scale * scaled - values * (scale * scale * scale * inner)


def gelu_parts(hidden):
    square = hidden * hidden
    tanh = jnp.tanh(GELU_K * hidden * (1.0 + 0.044715 * square))
    plus = 0.5 * (1.0 + tanh)
    slope = plus + (0.5 * GELU_K) * hidden * (1.0 - tanh * tanh) * (1.0 + (3 * 0.044715) * square)
    return hidden * plus, slope


def lane_mask(test):
    lanes = lax.broadcasted_iota(jnp.int32, (HALF, 128), 1)
    return jnp.where(test(lanes), 1.0, 0.0).astype(BF)


def row_block(shape, index_map):
    return pl.BlockSpec(shape, index_map)


def whole(shape):
    return pl.BlockSpec(shape, lambda *_: (0,) * len(shape))


def call(kernel, grid, in_specs, out_specs, out_shape, scratch=(), prefetch=0, flops=0, nbytes=0):
    return pl.pallas_call(
        kernel,
        grid_spec=pltpu.PrefetchScalarGridSpec(
            num_scalar_prefetch=prefetch,
            grid=grid,
            in_specs=in_specs,
            out_specs=out_specs,
            scratch_shapes=scratch,
        ),
        out_shape=out_shape,
        compiler_params=pltpu.CompilerParams(vmem_limit_bytes=VMEM_BYTES),
        cost_estimate=pl.CostEstimate(flops=flops, bytes_accessed=nbytes, transcendentals=0),
    )


def shape(dims, dtype):
    return jax.ShapeDtypeStruct(dims, dtype)


def gather_kernel(qkv, inner, outer, wo, gq, gi, gu, go, xs, xr, ss, sr, ds, dr, ws, wr, cs):
    x = lax.axis_index("tp")
    b = lax.axis_index("batch")
    c = lax.rem(b, 2)
    z = lax.rem(b // 2, SIDES)
    y = b // (2 * SIDES)
    left, right = {"tp": lax.rem(x + TP - 1, TP)}, {"tp": lax.rem(x + 1, TP)}

    def at(y_now, z_now, c_now):
        return {"batch": (y_now * SIDES + z_now) * 2 + c_now}

    up = (at(lax.rem(y + 1, SIDES), z, c), at(y, lax.rem(z + 1, SIDES), c))
    down = (at(lax.rem(y + SIDES - 1, SIDES), z, c), at(y, lax.rem(z + SIDES - 1, SIDES), c))
    partner = at(y, z, 1 - c)

    barrier = pltpu.get_barrier_semaphore()
    for device in (left, right, up[0], up[1], down[0], down[1], partner):
        pl.semaphore_signal(barrier, inc=1, device_id=device, device_id_type=MESH)
    pl.semaphore_wait(barrier, 7)

    def send(src, dst, send_sem, recv_sem, device):
        return pltpu.make_async_remote_copy(
            src_ref=src,
            dst_ref=dst,
            send_sem=send_sem,
            recv_sem=recv_sem,
            device_id=device,
            device_id_type=MESH,
        )

    def rows(start, count):
        return pl.ds(pl.multiple_of(start, 16), count)

    mine = rows(c * 384, 384)
    blocks = (rows(c * 384 + y * 48, 48), rows(c * 384 + 192 + z * 48, 48))
    back = (
        rows(c * 384 + lax.rem(y + SIDES - 1, SIDES) * 48, 48),
        rows(c * 384 + 192 + lax.rem(z + SIDES - 1, SIDES) * 48, 48),
    )
    ahead = (
        rows(c * 384 + lax.rem(y + 1, SIDES) * 48, 48),
        rows(c * 384 + 192 + lax.rem(z + 1, SIDES) * 48, 48),
    )
    chunks = [(source, target, layer) for layer in range(2) for source, target in ((qkv, gq), (inner, gi), (outer, gu))]
    count = len(chunks)

    def first(k):
        source, target, layer = chunks[k]
        out = []
        for path in range(2):
            block = blocks[path]
            for way, (device, slot) in enumerate(((right, 3), (left, 1))):
                n = path * 2 + way
                out.append(
                    send(source.at[layer, block], target.at[layer, slot, block], xs.at[k, n], xr.at[k, n], device)
                )
        return out

    def relay(k):
        _, target, layer = chunks[k]
        y_block, z_block = blocks
        return [
            send(target.at[layer, 3, y_block], target.at[layer, 2, y_block], xs.at[k, 4], xr.at[k, 4], right),
            send(target.at[layer, 1, z_block], target.at[layer, 2, z_block], xs.at[k, 5], xr.at[k, 5], left),
        ]

    def spread(k):
        _, target, layer = chunks[k]
        out = []
        for path in range(2):
            block = target.at[layer, pl.ds(1, 3), blocks[path]]
            for way, device in enumerate((up[path], down[path])):
                n = path * 2 + way
                out.append(send(block, block, ss.at[k, n], sr.at[k, n], device))
        return out

    def spread_relay(k):
        _, target, layer = chunks[k]
        out = []
        for path in range(2):
            if (k + path) % 2 == 0:
                block, device = target.at[layer, pl.ds(1, 3), back[path]], up[path]
            else:
                block, device = target.at[layer, pl.ds(1, 3), ahead[path]], down[path]
            out.append(send(block, block, ss.at[k, 4 + path], sr.at[k, 4 + path], device))
        return out

    def swap(k):
        _, target, layer = chunks[k]
        block = target.at[layer, pl.ds(1, 3), mine]
        return [send(block, block, ds.at[k], dr.at[k], partner)]

    started = []

    def start(copies):
        for copy in copies:
            copy.start()
        started.extend(copies)
        return copies

    def arrived(copies):
        for copy in copies:
            copy.wait_recv()

    local = [
        pltpu.make_async_copy(source, target.at[:, 0], cs.at[n])
        for n, (source, target) in enumerate(((qkv, gq), (inner, gi), (outer, gu), (wo, go)))
    ]
    firsts = {0: start(first(0))}
    for copy in local:
        copy.start()
    relays, spreads, second, last = {}, {}, {}, {}

    wo_rows = rows(c * 96, 96)
    wo_low, wo_high = rows(c * 96, 48), rows(c * 96 + 48, 48)

    for k in range(count):
        arrived(firsts[k])
        relays[k] = start(relay(k))
        if k + 1 < count:
            firsts[k + 1] = start(first(k + 1))
        else:
            wo_first = start([
                send(wo.at[:, wo_rows], go.at[:, 3, wo_rows], ws.at[0], wr.at[0], right),
                send(wo.at[:, wo_rows], go.at[:, 1, wo_rows], ws.at[1], wr.at[1], left),
            ])
        arrived(relays[k])
        spreads[k] = start(spread(k))
        if k >= 1:
            arrived(spreads[k - 1])
            second[k - 1] = start(spread_relay(k - 1))
        if k >= 2:
            arrived(second[k - 2])
            last[k - 2] = start(swap(k - 2))
    arrived(wo_first)
    wo_relay = start([
        send(go.at[:, 3, wo_low], go.at[:, 2, wo_low], ws.at[2], wr.at[2], right),
        send(go.at[:, 1, wo_high], go.at[:, 2, wo_high], ws.at[3], wr.at[3], left),
    ])
    arrived(spreads[count - 1])
    second[count - 1] = start(spread_relay(count - 1))
    arrived(second[count - 2])
    last[count - 2] = start(swap(count - 2))
    arrived(wo_relay)
    wo_block = go.at[:, pl.ds(1, 3), wo_rows]
    wo_last = start([send(wo_block, wo_block, ws.at[4], wr.at[4], partner)])
    arrived(second[count - 1])
    last[count - 1] = start(swap(count - 1))
    for k in range(count):
        arrived(last[k])
    arrived(wo_last)
    for copy in started:
        copy.wait_send()
    for copy in local:
        copy.wait()


def gather_weights(qkv, inner, outer, wo):
    layers = qkv.shape[0]
    dma = pltpu.SemaphoreType.DMA
    anywhere = pl.BlockSpec(memory_space=pl.ANY)
    arrays = (qkv, inner, outer, wo)
    return pl.pallas_call(
        gather_kernel,
        out_shape=[shape((layers, TP) + a.shape[1:], a.dtype) for a in arrays],
        in_specs=[anywhere] * 4,
        out_specs=[anywhere] * 4,
        scratch_shapes=[
            dma((6, 6)), dma((6, 6)), dma((6, 6)), dma((6, 6)), dma((6,)), dma((6,)), dma((5,)), dma((5,)), dma((4,)),
        ],
        compiler_params=pltpu.CompilerParams(collective_id=0, has_side_effects=True),
    )(*arrays)


def sum_kernel(
    a0, b0, a1, b1, down_out, gate_out, gain1_out, qkv_out, proj_out, gain2_out, inner_out, outer_out,
    packed, from_core, half, from_x, piece, from_y, small, from_z, total, send_sems, recv_sems,
):
    x = lax.axis_index("tp")
    b = lax.axis_index("batch")
    c = lax.rem(b, 2)
    z = lax.rem(b // 2, SIDES)
    y = b // (2 * SIDES)

    def at(y_now, z_now, c_now):
        return {"batch": (y_now * SIDES + z_now) * 2 + c_now}

    partner = at(y, z, 1 - c)
    x_devices = [{"tp": lax.rem(x + d, TP)} for d in (1, 2, 3)]
    y_devices = [at(lax.rem(y + d, SIDES), z, c) for d in (1, 2, 3)]
    z_devices = [at(y, lax.rem(z + d, SIDES), c) for d in (1, 2, 3)]
    barrier = pltpu.get_barrier_semaphore()
    for device in [partner] + x_devices + y_devices + z_devices:
        pl.semaphore_signal(barrier, inc=1, device_id=device, device_id_type=MESH)

    packed[0:A_ROWS] = a0[...]
    packed[A_ROWS:LAYER_ROWS] = b0[...]
    packed[LAYER_ROWS : LAYER_ROWS + A_ROWS] = a1[...]
    packed[LAYER_ROWS + A_ROWS : 2 * LAYER_ROWS] = b1[...]
    packed[2 * LAYER_ROWS :] = jnp.zeros((SUM_ROWS - 2 * LAYER_ROWS, 128), BF)
    pl.semaphore_wait(barrier, 10)

    def send(n, src, dst, device):
        copy = pltpu.make_async_remote_copy(
            src_ref=src,
            dst_ref=dst,
            send_sem=send_sems.at[n],
            recv_sem=recv_sems.at[n],
            device_id=device,
            device_id_type=MESH,
        )
        copy.start()
        return copy

    def rows(start, count):
        return pl.ds(pl.multiple_of(start, 16), count)

    half_rows, x_rows, y_rows = SUM_ROWS // 2, SUM_ROWS // 8, SUM_ROWS // 32
    copies = [send(0, packed.at[rows((1 - c) * half_rows, half_rows)], from_core, partner)]
    copies[0].wait_recv()
    half[...] = (packed[rows(c * half_rows, half_rows)].astype(F32) + from_core[...].astype(F32)).astype(BF)

    now = [
        send(1 + d, half.at[rows(lax.rem(x + d + 1, TP) * x_rows, x_rows)], from_x.at[d], x_devices[d])
        for d in range(3)
    ]
    for copy in now:
        copy.wait_recv()
    copies += now
    piece[...] = (
        half[rows(x * x_rows, x_rows)].astype(F32)
        + from_x[0].astype(F32)
        + from_x[1].astype(F32)
        + from_x[2].astype(F32)
    ).astype(BF)

    now = [
        send(4 + d, piece.at[rows(lax.rem(y + d + 1, SIDES) * y_rows, y_rows)], from_y.at[d], y_devices[d])
        for d in range(3)
    ]
    for copy in now:
        copy.wait_recv()
    copies += now
    small[...] = (
        piece[rows(y * y_rows, y_rows)].astype(F32)
        + from_y[0].astype(F32)
        + from_y[1].astype(F32)
        + from_y[2].astype(F32)
    ).astype(BF)

    now = [send(7 + d, small, from_z.at[z], z_devices[d]) for d in range(3)]
    from_z[z] = small[...]
    for copy in now:
        copy.wait_recv()
    copies += now
    mine = rows(c * half_rows + x * x_rows + y * y_rows, y_rows)
    total[mine] = (
        from_z[0].astype(F32) + from_z[1].astype(F32) + from_z[2].astype(F32) + from_z[3].astype(F32)
    ).astype(BF)

    now = [send(10 + d, total.at[mine], total.at[mine], y_devices[d]) for d in range(3)]
    for copy in now:
        copy.wait_recv()
    copies += now
    mine = rows(c * half_rows + x * x_rows, x_rows)
    now = [send(13 + d, total.at[mine], total.at[mine], x_devices[d]) for d in range(3)]
    for copy in now:
        copy.wait_recv()
    copies += now
    mine = rows(c * half_rows, half_rows)
    now = [send(16, total.at[mine], total.at[mine], partner)]
    for copy in now:
        copy.wait_recv()
    copies += now
    for copy in copies:
        copy.wait_send()

    for layer in range(2):
        base = layer * LAYER_ROWS

        def part(start, count, base=base):
            return total[base + start : base + start + count].astype(F32)

        proj_out[layer] = part(A_PROJ, 96)[:, :SIDE_W]
        for n in range(3):
            inner_out[layer, :, n * 128 : (n + 1) * 128] = part(A_INNER + n * 96, 96)
            block = part(A_OUTER + n * 96, 128).T
            outer_out[layer, n * 128 : (n + 1) * 128] = block[:, :SIDE_W]
            qkv_out[layer, n] = part(A_ROWS + B_QKV + n * 96, 96)[:, :SIDE_W]
        for n in range(6):
            block = part(A_ROWS + B_DOWN + n * 96, 128).T
            down_out[layer, n * 128 : (n + 1) * 128] = block[:, :SIDE_W]
        gain2_out[layer : layer + 1] = part(A_SMALL, 16)[0:1, :SIDE_W]
        rest = part(A_ROWS + B_SMALL, 16)
        gate_out[layer : layer + 1] = rest[0:1, :SIDE_W]
        gain1_out[layer : layer + 1] = rest[1:2, :SIDE_W]


def sum_gradients(parts):
    vmem = pl.BlockSpec(memory_space=pltpu.VMEM)
    dma = pltpu.SemaphoreType.DMA
    outs = [
        shape((2, WIDTH, SIDE_W), F32),
        shape((2, SIDE_W), F32),
        shape((2, SIDE_W), F32),
        shape((2, 3, SIDE_W, SIDE_W), F32),
        shape((2, SIDE_W, SIDE_W), F32),
        shape((2, SIDE_W), F32),
        shape((2, SIDE_W, SIDE_FF), F32),
        shape((2, SIDE_FF, SIDE_W), F32),
    ]
    down, gate, gain1, qkv, proj, gain2, inner, outer = pl.pallas_call(
        sum_kernel,
        out_shape=outs,
        in_specs=[vmem] * 4,
        out_specs=[vmem] * 8,
        scratch_shapes=[
            pltpu.VMEM((SUM_ROWS, 128), BF),
            pltpu.VMEM((SUM_ROWS // 2, 128), BF),
            pltpu.VMEM((SUM_ROWS // 2, 128), BF),
            pltpu.VMEM((3, SUM_ROWS // 8, 128), BF),
            pltpu.VMEM((SUM_ROWS // 8, 128), BF),
            pltpu.VMEM((3, SUM_ROWS // 32, 128), BF),
            pltpu.VMEM((SUM_ROWS // 32, 128), BF),
            pltpu.VMEM((4, SUM_ROWS // 32, 128), BF),
            pltpu.VMEM((SUM_ROWS, 128), BF),
            dma((17,)),
            dma((17,)),
        ],
        compiler_params=pltpu.CompilerParams(
            collective_id=1, has_side_effects=True, vmem_limit_bytes=VMEM_BYTES
        ),
    )(*parts)
    qkv = jnp.concatenate([qkv[:, 0], qkv[:, 1], qkv[:, 2]], axis=-1)
    return down, gate, gain1, qkv, proj, gain2, inner, outer


def table_kernel(ends, base, out):
    for side in range(2):
        spread = jnp.broadcast_to(base[0, side : side + 1], (HALF, 2 * HALF))
        rolled = pltpu.roll(spread, 0, 1, stride=1, stride_axis=0)[:, :HALF]
        keys = lax.broadcasted_iota(jnp.int32, (HALF, HALF), 0)
        out[0, side * HALF : (side + 1) * HALF] = jnp.where(keys < ends[side], rolled, NEGATIVE).astype(BF)


def offset_tables(offset_bias, core, first_head, length):
    heads = offset_bias.shape[0]
    bias = jnp.pad(offset_bias.astype(F32), ((0, 0), (0, 1)))
    bias = lax.dynamic_slice_in_dim(jnp.concatenate([bias, bias]), first_head, heads, 0)

    def flipped(low, high):
        return jnp.concatenate([bias[:, low : low + HALF][:, ::-1], bias[:, high : high + HALF][:, ::-1]], axis=1)

    other = jnp.where(core == 0, flipped(512, 768), flipped(0, 256))
    base = jnp.stack([flipped(256, 512), other], axis=1)
    ends = jnp.stack([length - core * HALF, length - (1 - core) * HALF])
    return call(
        table_kernel,
        (heads,),
        [row_block((1, 2, 2 * HALF), lambda h, ends: (h, 0, 0))],
        row_block((1, 2 * HALF, HALF), lambda h, ends: (h, 0, 0)),
        shape((heads, 2 * HALF, HALF), BF),
        prefetch=1,
    )(ends, base)


def project_kernel(b_ref, gain_ref, w_ref, q_ref, kv_ref, normed):
    @pl.when(pl.program_id(0) == 0)
    def _():
        b = b_ref[...]
        normed[...] = (b * rms_scale(b) * gain_ref[...]).astype(BF)

    out = nn(normed[...], w_ref[0, 0])
    q_ref[0] = (out[:, :256] * 0.125).astype(BF)
    kv_ref[0] = out[:, 256:].astype(BF)


def project(layer, b, gain, weights):
    return call(
        project_kernel,
        (TP,),
        [
            whole((HALF, WIDTH)),
            whole((1, WIDTH)),
            row_block((1, 1, WIDTH, 640), lambda s: (layer, s, 0, 0)),
        ],
        [row_block((1, HALF, 256), lambda s: (s, 0, 0)), row_block((1, HALF, 384), lambda s: (s, 0, 0))],
        [shape((TP, HALF, 256), BF), shape((TP, HALF, 384), BF)],
        [pltpu.VMEM((HALF, WIDTH), BF)],
        flops=2 * HALF * WIDTH * 2560,
        nbytes=5 * 10**6,
    )(b, gain, weights)


def head_parts(q, dm=None):
    low = lane_mask(lambda lanes: lanes < 64)
    high = lane_mask(lambda lanes: lanes >= 64)
    queries = [q[:, :128] * low, q[:, :128] * high, q[:, 128:]]
    key_slabs = [slice(0, 128), slice(0, 128), slice(256, 384)]
    value_slabs = [slice(128, 256), slice(128, 256), slice(256, 384)]
    if dm is None:
        return queries, key_slabs, value_slabs
    return queries, key_slabs, value_slabs, [dm[:, :128] * low, dm[:, :128] * high, dm[:, 128:]]


def softmax_parts(scores_own, scores_other):
    top = jnp.maximum(
        jnp.max(scores_own, axis=0, keepdims=True), jnp.max(scores_other, axis=0, keepdims=True)
    )
    exp_own = jnp.exp(scores_own - top)
    exp_other = jnp.exp(scores_other - top)
    total = jnp.sum(exp_own, axis=0, keepdims=True) + jnp.sum(exp_other, axis=0, keepdims=True)
    return exp_own, exp_other, 1.0 / total, top + jnp.log(total)


def attend_kernel(q_ref, own_ref, other_ref, table_ref, mixed_ref, lse_ref):
    queries, key_slabs, value_slabs = head_parts(q_ref[0])
    rows = []
    for j in range(3):
        own, other = own_ref[0, :, key_slabs[j]], other_ref[0, :, key_slabs[j]]
        scores_own = nt(own, queries[j]) + table_ref[j, :HALF].astype(F32)
        scores_other = nt(other, queries[j]) + table_ref[j, HALF:].astype(F32)
        exp_own, exp_other, inverse, lse = softmax_parts(scores_own, scores_other)
        mixed = tn(own_ref[0, :, value_slabs[j]], exp_own.astype(BF)) + tn(
            other_ref[0, :, value_slabs[j]], exp_other.astype(BF)
        )
        rows.append((mixed[:64] if j == 0 else mixed[64:]) * inverse)
        lse_ref[0, j : j + 1] = lse
    mixed_ref[0, :, :128] = jnp.concatenate(rows[:2], axis=0).T.astype(BF)
    third = jnp.concatenate([rows[2], jnp.zeros_like(rows[2])], axis=0).T
    mixed_ref[0, :, 128:] = third[:, :64].astype(BF)


def attend(q, own, other, table):
    return call(
        attend_kernel,
        (TP,),
        [
            row_block((1, HALF, 256), lambda s: (s, 0, 0)),
            row_block((1, HALF, 384), lambda s: (s, 0, 0)),
            row_block((1, HALF, 384), lambda s: (s, 0, 0)),
            row_block((3, 2 * HALF, HALF), lambda s: (s, 0, 0)),
        ],
        [row_block((1, HALF, 192), lambda s: (s, 0, 0)), row_block((1, 8, HALF), lambda s: (s, 0, 0))],
        [shape((TP, HALF, 192), BF), shape((TP, 8, HALF), F32)],
        flops=12 * 4 * 2 * HALF * HALF * 128,
        nbytes=5 * 10**6,
    )(q, own, other, table)


def feed_kernel(
    mixed_ref, b_ref, wo_ref, gain_ref, inner_ref, outer_ref, narrow_ref,
    mid_ref, slope_ref, out_ref, out_low_ref, down_ref, normed, acc,
):
    step = pl.program_id(0)

    @pl.when(step == 0)
    def _():
        mid = b_ref[...]
        for s in range(TP):
            mid = mid + nn(mixed_ref[s], wo_ref[0, s])
        mid_ref[...] = mid
        acc[...] = mid
        normed[...] = (mid * rms_scale(mid) * gain_ref[...]).astype(BF)

    active, slope = gelu_parts(nn(normed[...], inner_ref[0, 0]))
    slope_ref[0] = slope.astype(BF)
    acc[...] += nn(active.astype(BF), outer_ref[0, 0])

    @pl.when(step == TP - 1)
    def _():
        out = acc[...]
        low = out.astype(BF)
        out_ref[...] = out
        out_low_ref[...] = low
        down_ref[...] = nn(low, narrow_ref[...]).astype(BF)


def feed(layer, mixed, b, wo, gain, inner, outer, narrow):
    return call(
        feed_kernel,
        (TP,),
        [
            whole((TP, HALF, 192)),
            whole((HALF, WIDTH)),
            row_block((1, TP, 192, WIDTH), lambda s: (layer, 0, 0, 0)),
            whole((1, WIDTH)),
            row_block((1, 1, WIDTH, WIDTH), lambda s: (layer, s, 0, 0)),
            row_block((1, 1, WIDTH, WIDTH), lambda s: (layer, s, 0, 0)),
            whole((WIDTH, SIDE_W)),
        ],
        [
            whole((HALF, WIDTH)),
            row_block((1, HALF, WIDTH), lambda s: (s, 0, 0)),
            whole((HALF, WIDTH)),
            whole((HALF, WIDTH)),
            whole((HALF, SIDE_W)),
        ],
        [
            shape((HALF, WIDTH), F32),
            shape((TP, HALF, WIDTH), BF),
            shape((HALF, WIDTH), F32),
            shape((HALF, WIDTH), BF),
            shape((HALF, SIDE_W), BF),
        ],
        [pltpu.VMEM((HALF, WIDTH), BF), pltpu.VMEM((HALF, WIDTH), F32)],
        flops=2 * HALF * WIDTH * WIDTH * 9,
        nbytes=14 * 10**6,
    )(mixed, b, wo, gain, inner, outer, narrow)


def feed_back_kernel(
    grad_ref, ddown_ref, narrow_ref, mid_ref, gain_ref, slope_ref, outer_ref, inner_ref, wo_ref,
    gmid_ref, dmixed_ref, grad, grad_low, acc,
):
    step = pl.program_id(0)

    @pl.when(step == 0)
    def _():
        total = grad_ref[...] + nt(ddown_ref[...], narrow_ref[...])
        grad[...] = total
        grad_low[...] = total.astype(BF)
        acc[...] = jnp.zeros_like(acc)

    dactive = nt(grad_low[...], outer_ref[0, 0])
    dhidden = (dactive * slope_ref[0].astype(F32)).astype(BF)
    acc[...] += nt(dhidden, inner_ref[0, 0])

    @pl.when(step == TP - 1)
    def _():
        gmid = grad[...] + rms_back(mid_ref[...], gain_ref[...], acc[...])
        gmid_ref[...] = gmid
        low = gmid.astype(BF)
        for s in range(TP):
            dmixed_ref[s, :, :128] = nt(low, wo_ref[0, s, :128]).astype(BF)
            third = jnp.concatenate([jnp.zeros((64, WIDTH), BF), wo_ref[0, s, 128:]], axis=0)
            dmixed_ref[s, :, 128:] = nt(low, third).astype(BF)


def feed_back(layer, grad, ddown, narrow, mid, gain, slope, outer, inner, wo):
    return call(
        feed_back_kernel,
        (TP,),
        [
            whole((HALF, WIDTH)),
            whole((HALF, SIDE_W)),
            whole((WIDTH, SIDE_W)),
            whole((HALF, WIDTH)),
            whole((1, WIDTH)),
            row_block((1, HALF, WIDTH), lambda s: (s, 0, 0)),
            row_block((1, 1, WIDTH, WIDTH), lambda s: (layer, s, 0, 0)),
            row_block((1, 1, WIDTH, WIDTH), lambda s: (layer, s, 0, 0)),
            row_block((1, TP, 192, WIDTH), lambda s: (layer, 0, 0, 0)),
        ],
        [whole((HALF, WIDTH)), whole((TP, HALF, 256))],
        [shape((HALF, WIDTH), F32), shape((TP, HALF, 256), BF)],
        [pltpu.VMEM((HALF, WIDTH), F32), pltpu.VMEM((HALF, WIDTH), BF), pltpu.VMEM((HALF, WIDTH), F32)],
        flops=2 * HALF * WIDTH * WIDTH * 9,
        nbytes=14 * 10**6,
    )(grad, ddown, narrow, mid, gain, slope, outer, inner, wo)


def score_gradients(scores, lse, dprobs):
    probs = [jnp.exp(s - lse) for s in scores]
    inner = jnp.sum(probs[0] * dprobs[0], axis=0, keepdims=True) + jnp.sum(
        probs[1] * dprobs[1], axis=0, keepdims=True
    )
    dscores = [(p * (d - inner)).astype(BF) for p, d in zip(probs, dprobs)]
    return [p.astype(BF) for p in probs], dscores


def attend_back_kernel(
    q_ref, own_ref, other_ref, table_ref, lse_ref, dmixed_ref, dq_ref, dkv_own_ref, dkv_other_ref
):
    queries, key_slabs, value_slabs, dmixed = head_parts(q_ref[0], dmixed_ref[0])
    halves = (own_ref, other_ref)
    probs, dscores, dq_rows = [], [], []
    for j in range(3):
        keys = [ref[0, :, key_slabs[j]] for ref in halves]
        scores = [
            nt(k, queries[j]) + table_ref[j, n * HALF : (n + 1) * HALF].astype(F32) for n, k in enumerate(keys)
        ]
        dprobs = [nt(ref[0, :, value_slabs[j]], dmixed[j]) for ref in halves]
        p, ds = score_gradients(scores, lse_ref[0, j : j + 1], dprobs)
        probs.append(p)
        dscores.append(ds)
        dq = tn(keys[0], ds[0]) + tn(keys[1], ds[1])
        dq_rows.append(dq[64:] if j == 1 else dq[:64])
    dq_ref[0, :, :128] = (jnp.concatenate(dq_rows[:2], axis=0).T * 0.125).astype(BF)
    third = jnp.concatenate([dq_rows[2], jnp.zeros_like(dq_rows[2])], axis=0)
    dq_ref[0, :, 128:] = (third.T * 0.125).astype(BF)
    right = [
        jnp.concatenate(queries[:2], axis=0),
        jnp.concatenate(dmixed[:2], axis=0),
        jnp.concatenate([queries[2], dmixed[2]], axis=0),
    ]
    for n, ref in enumerate((dkv_own_ref, dkv_other_ref)):
        left = [
            jnp.concatenate([dscores[0][n], dscores[1][n]], axis=1),
            jnp.concatenate([probs[0][n], probs[1][n]], axis=1),
            jnp.concatenate([dscores[2][n], probs[2][n]], axis=1),
        ]
        for m in range(3):
            ref[0, :, m * 128 : (m + 1) * 128] = nn(left[m], right[m]).astype(ref.dtype)


def attend_back(q, own, other, table, lse, dmixed):
    return call(
        attend_back_kernel,
        (TP,),
        [
            row_block((1, HALF, 256), lambda s: (s, 0, 0)),
            row_block((1, HALF, 384), lambda s: (s, 0, 0)),
            row_block((1, HALF, 384), lambda s: (s, 0, 0)),
            row_block((3, 2 * HALF, HALF), lambda s: (s, 0, 0)),
            row_block((1, 8, HALF), lambda s: (s, 0, 0)),
            row_block((1, HALF, 256), lambda s: (s, 0, 0)),
        ],
        [
            row_block((1, HALF, 256), lambda s: (s, 0, 0)),
            row_block((1, HALF, 384), lambda s: (s, 0, 0)),
            row_block((1, HALF, 384), lambda s: (s, 0, 0)),
        ],
        [shape((TP, HALF, 256), BF), shape((TP, HALF, 384), F32), shape((TP, HALF, 384), BF)],
        flops=12 * 10 * 2 * HALF * HALF * 128,
        nbytes=9 * 10**6,
    )(q, own, other, table, lse, dmixed)


def project_back_kernel(dq_ref, own_ref, got_ref, w_ref, b_ref, gain_ref, gmid_ref, out_ref, acc):
    step = pl.program_id(0)

    @pl.when(step == 0)
    def _():
        acc[...] = jnp.zeros_like(acc)

    dkv = (own_ref[0] + got_ref[0].astype(F32)).astype(BF)
    acc[...] += nt(dq_ref[0], w_ref[0, 0, :, :256]) + nt(dkv, w_ref[0, 0, :, 256:])

    @pl.when(step == TP - 1)
    def _():
        out = gmid_ref[...] + rms_back(b_ref[...], gain_ref[...], acc[...])
        out_ref[...] = out.astype(out_ref.dtype)


def project_back(layer, dq, dkv_own, dkv_got, weights, b, gain, gmid, out_type):
    return call(
        project_back_kernel,
        (TP,),
        [
            row_block((1, HALF, 256), lambda s: (s, 0, 0)),
            row_block((1, HALF, 384), lambda s: (s, 0, 0)),
            row_block((1, HALF, 384), lambda s: (s, 0, 0)),
            row_block((1, 1, WIDTH, 640), lambda s: (layer, s, 0, 0)),
            whole((HALF, WIDTH)),
            whole((1, WIDTH)),
            whole((HALF, WIDTH)),
        ],
        whole((HALF, WIDTH)),
        shape((HALF, WIDTH), out_type),
        [pltpu.VMEM((HALF, WIDTH), F32)],
        flops=2 * HALF * WIDTH * 2560,
        nbytes=8 * 10**6,
    )(dq, dkv_own, dkv_got, weights, b, gain, gmid)


def split_pack(values, low_test):
    high = values.astype(BF)
    low = (values - high.astype(F32)).astype(BF)
    mask = lane_mask(low_test)
    return high * (1 - mask) + low * mask


def side_start_kernel(down_ref, prior_ref, gate_ref, gain_ref, wq_ref, wkv_ref, joined_ref, q_ref, kv_ref):
    mix = jax.nn.sigmoid(gate_ref[...])
    joined = mix * down_ref[...].astype(F32) + (1.0 - mix) * prior_ref[...]
    joined_ref[...] = joined
    normed = joined * rms_scale(joined) * gain_ref[...]
    q = nn(normed, wq_ref[...], HIGHEST)
    kv = nn(normed, wkv_ref[...], HIGHEST)
    for g in range(4):
        lanes = slice(g * 128, (g + 1) * 128)
        q_ref[g] = split_pack(q[:, lanes], lambda n: (n >= 24) & (n < 48))
        kv_ref[g] = split_pack(kv[:, lanes], lambda n: ((n >= 48) & (n < 72)) | (n >= 96))


def side_start_call(down, prior, gate, gain, wq, wkv):
    return call(
        side_start_kernel,
        (1,),
        [
            whole((HALF, SIDE_W)),
            whole((HALF, SIDE_W)),
            whole((1, SIDE_W)),
            whole((1, SIDE_W)),
            whole((SIDE_W, 512)),
            whole((SIDE_W, 512)),
        ],
        [whole((HALF, SIDE_W)), whole((4, HALF, 128)), whole((4, HALF, 128))],
        [shape((HALF, SIDE_W), F32), shape((4, HALF, 128), BF), shape((4, HALF, 128), BF)],
        flops=6 * 2 * HALF * SIDE_W * 1024,
        nbytes=2 * 10**6,
    )(down, prior, gate, gain, wq, wkv)


def of_head(j, blocks):
    def test(lanes):
        hit = (lanes >= blocks[0] * 24 + j * 8) & (lanes < blocks[0] * 24 + j * 8 + 8)
        for n in blocks[1:]:
            hit = hit | ((lanes >= n * 24 + j * 8) & (lanes < n * 24 + j * 8 + 8))
        return hit

    return lane_mask(test)


def transposed(rows):
    return jnp.concatenate([rows, jnp.zeros((32, rows.shape[1]), rows.dtype)], axis=0).T[:, :SIDE_W]


def side_attend_kernel(
    first, q_ref, own_ref, other_ref, table_ref, joined_ref, proj_ref, gain_ref, inner_ref, outer_ref,
    mixed_ref, lse_ref, out_ref, mixed_rows,
):
    group = pl.program_id(0)
    for j in range(3):
        q = q_ref[0] * of_head(j, (0, 1, 2))
        scores_own = nt(own_ref[0], q) + table_ref[j, :HALF].astype(F32)
        scores_other = nt(other_ref[0], q) + table_ref[j, HALF:].astype(F32)
        exp_own, exp_other, inverse, lse = softmax_parts(scores_own, scores_other)
        mixed = tn(own_ref[0], exp_own.astype(BF)) + tn(other_ref[0], exp_other.astype(BF))
        head = (mixed[72 + j * 8 : 80 + j * 8] + mixed[96 + j * 8 : 104 + j * 8]) * inverse
        mixed_rows[pl.ds(pl.multiple_of(group * 24 + j * 8, 8), 8)] = head
        lse_ref[0, j : j + 1] = lse

    @pl.when(group == 3)
    def _():
        mixed = transposed(mixed_rows[...])
        mixed_ref[...] = mixed
        joined = joined_ref[...] + nn(mixed, proj_ref[...], HIGHEST)
        normed = joined * rms_scale(joined) * gain_ref[...]
        active, _ = gelu_parts(nn(normed, inner_ref[...], HIGHEST))
        out_ref[...] = joined + nn(active, outer_ref[...], HIGHEST)


def group_table(g, first):
    return (lax.rem(g + 4 - first[0], 4), 0, 0)


def side_attend(first, q, own, other, table, joined, proj, gain, inner, outer):
    return call(
        side_attend_kernel,
        (4,),
        [
            row_block((1, HALF, 128), lambda g, first: (g, 0, 0)),
            row_block((1, HALF, 128), lambda g, first: (g, 0, 0)),
            row_block((1, HALF, 128), lambda g, first: (g, 0, 0)),
            row_block((3, 2 * HALF, HALF), group_table),
            whole((HALF, SIDE_W)),
            whole((SIDE_W, SIDE_W)),
            whole((1, SIDE_W)),
            whole((SIDE_W, SIDE_FF)),
            whole((SIDE_FF, SIDE_W)),
        ],
        [whole((HALF, SIDE_W)), row_block((1, 8, HALF), lambda g, first: (g, 0, 0)), whole((HALF, SIDE_W))],
        [shape((HALF, SIDE_W), F32), shape((4, 8, HALF), F32), shape((HALF, SIDE_W), F32)],
        [pltpu.VMEM((SIDE_W, HALF), F32)],
        prefetch=1,
        flops=12 * 4 * 2 * HALF * HALF * 128,
        nbytes=5 * 10**6,
    )(first, q, own, other, table, joined, proj, gain, inner, outer)


def side_back_kernel(
    first, grad_ref, joined_ref, mixed_ref, proj_ref, gain_ref, inner_ref, outer_ref, spread_ref,
    q_ref, own_ref, other_ref, table_ref, lse_ref,
    djoined_ref, dq_ref, dkv_own_ref, dkv_other_ref, sums_ref, dmixed,
):
    group = pl.program_id(0)

    @pl.when(group == 0)
    def _():
        grad = grad_ref[...]
        grad_low = grad.astype(BF)
        mixed = mixed_ref[...]
        joined = joined_ref[...] + nn(mixed, proj_ref[...], HIGHEST)
        unit = joined * rms_scale(joined)
        normed = unit * gain_ref[...]
        active, slope = gelu_parts(nn(normed, inner_ref[...], HIGHEST))
        dhidden = (nt(grad_low, outer_ref[...].astype(BF)) * slope).astype(BF)
        dnormed = nt(dhidden, inner_ref[...].astype(BF))
        djoined = grad + rms_back(joined, gain_ref[...], dnormed)
        djoined_ref[...] = djoined
        djoined_low = djoined.astype(BF)
        dmixed_low = nt(djoined_low, proj_ref[...].astype(BF)).astype(BF)
        for g in range(4):
            dmixed[g] = nn(dmixed_low, spread_ref[:, g * 128 : (g + 1) * 128]).astype(BF)
        sums_ref[...] = jnp.zeros_like(sums_ref)
        sums_ref[A_PROJ : A_PROJ + SIDE_W, :SIDE_W] = tn(mixed.astype(BF), djoined_low).astype(BF)
        inner_sum = tn(normed.astype(BF), dhidden).astype(BF)
        outer_sum = tn(grad_low, active.astype(BF)).astype(BF)
        for n in range(3):
            lanes = slice(n * 128, (n + 1) * 128)
            sums_ref[A_INNER + n * 96 : A_INNER + (n + 1) * 96] = inner_sum[:, lanes]
            sums_ref[A_OUTER + n * 96 : A_OUTER + (n + 1) * 96] = outer_sum[:, lanes]
        gain_sum = jnp.sum(dnormed * unit, axis=0, keepdims=True)
        sums_ref[A_SMALL:A_ROWS, :SIDE_W] = jnp.broadcast_to(gain_sum, (16, SIDE_W)).astype(BF)

    halves = (own_ref[0], other_ref[0])
    left, right = [[], []], []
    for j in range(3):
        q = q_ref[0] * of_head(j, (0, 1, 2))
        dm = dmixed[group] * of_head(j, (3, 4))
        scores = [nt(kv, q) + table_ref[j, n * HALF : (n + 1) * HALF].astype(F32) for n, kv in enumerate(halves)]
        dprobs = [nt(kv, dm) for kv in halves]
        p, ds = score_gradients(scores, lse_ref[0, j : j + 1], dprobs)
        dq = tn(halves[0], ds[0]) + tn(halves[1], ds[1])
        dq_ref[j * 8 : j * 8 + 8] = dq[j * 8 : j * 8 + 8] + dq[48 + j * 8 : 56 + j * 8]
        for n in range(2):
            left[n] += [ds[n], p[n]]
        right += [q_ref[0] * of_head(j, (0,)), dmixed[group] * of_head(j, (3,))]
    right = jnp.concatenate(right, axis=0)
    for n, ref in enumerate((dkv_own_ref, dkv_other_ref)):
        ref[0] = nn(jnp.concatenate(left[n], axis=1), right).astype(ref.dtype)


def side_back(first, grad, joined, mixed, proj, gain, inner, outer, spread, q, own, other, table, lse):
    return call(
        side_back_kernel,
        (4,),
        [
            whole((HALF, SIDE_W)),
            whole((HALF, SIDE_W)),
            whole((HALF, SIDE_W)),
            whole((SIDE_W, SIDE_W)),
            whole((1, SIDE_W)),
            whole((SIDE_W, SIDE_FF)),
            whole((SIDE_FF, SIDE_W)),
            whole((SIDE_W, 512)),
            row_block((1, HALF, 128), lambda g, first: (g, 0, 0)),
            row_block((1, HALF, 128), lambda g, first: (g, 0, 0)),
            row_block((1, HALF, 128), lambda g, first: (g, 0, 0)),
            row_block((3, 2 * HALF, HALF), group_table),
            row_block((1, 8, HALF), lambda g, first: (g, 0, 0)),
        ],
        [
            whole((HALF, SIDE_W)),
            row_block((24, HALF), lambda g, first: (g, 0)),
            row_block((1, HALF, 128), lambda g, first: (g, 0, 0)),
            row_block((1, HALF, 128), lambda g, first: (g, 0, 0)),
            whole((A_ROWS, 128)),
        ],
        [
            shape((HALF, SIDE_W), F32),
            shape((SIDE_W, HALF), F32),
            shape((4, HALF, 128), F32),
            shape((4, HALF, 128), BF),
            shape((A_ROWS, 128), BF),
        ],
        [pltpu.VMEM((4, HALF, 128), BF)],
        prefetch=1,
        flops=12 * 10 * 2 * HALF * HALF * 128,
        nbytes=6 * 10**6,
    )(first, grad, joined, mixed, proj, gain, inner, outer, spread, q, own, other, table, lse)


def side_end_kernel(
    joined_ref, djoined_ref, dq_ref, own_ref, got_ref, gate_ref, gain_ref, down_ref, prior_ref,
    wq_ref, wkv_ref, gather_ref, out_low_ref, ddown_ref, dprior_ref, sums_ref,
):
    joined = joined_ref[...]
    unit = joined * rms_scale(joined)
    normed_low = (unit * gain_ref[...]).astype(BF)
    dq = transposed(dq_ref[...]).astype(BF)
    dkv = jnp.zeros((HALF, 256), F32)
    for g in range(4):
        both = (own_ref[g] + got_ref[g].astype(F32)).astype(BF)
        dkv = dkv + nn(both, gather_ref[g * 128 : (g + 1) * 128])
    dkv = dkv.astype(BF)
    dnormed = nt(dq, wq_ref[...]) + nt(dkv, wkv_ref[...])
    djoined = djoined_ref[...] + rms_back(joined, gain_ref[...], dnormed)
    mix = jax.nn.sigmoid(gate_ref[...])
    down = down_ref[...].astype(F32)
    ddown = (mix * djoined).astype(BF)
    ddown_ref[...] = ddown
    dprior_ref[...] = (1.0 - mix) * djoined
    gate_sum = jnp.sum(djoined * (down - prior_ref[...]), axis=0, keepdims=True) * mix * (1.0 - mix)
    gain_sum = jnp.sum(dnormed * unit, axis=0, keepdims=True)
    sums_ref[...] = jnp.zeros_like(sums_ref)
    sums_ref[B_QKV : B_QKV + 96, :SIDE_W] = (tn(normed_low, dq) * SIDE_SCALE).astype(BF)
    kv_sum = tn(normed_low, dkv).astype(BF)
    sums_ref[B_QKV + 96 : B_QKV + 192] = kv_sum[:, :128]
    sums_ref[B_QKV + 192 : B_QKV + 288] = kv_sum[:, 128:]
    down_sum = tn(ddown, out_low_ref[...]).astype(BF)
    for n in range(6):
        sums_ref[B_DOWN + n * 96 : B_DOWN + (n + 1) * 96] = down_sum[:, n * 128 : (n + 1) * 128]
    row = lax.broadcasted_iota(jnp.int32, (16, SIDE_W), 0)
    sums_ref[B_SMALL:B_ROWS, :SIDE_W] = jnp.where(row == 0, gate_sum, gain_sum).astype(BF)


def side_end(joined, djoined, dq, dkv_own, dkv_got, gate, gain, down, prior, wq, wkv, gather, out_low):
    return call(
        side_end_kernel,
        (1,),
        [
            whole((HALF, SIDE_W)),
            whole((HALF, SIDE_W)),
            whole((SIDE_W, HALF)),
            whole((4, HALF, 128)),
            whole((4, HALF, 128)),
            whole((1, SIDE_W)),
            whole((1, SIDE_W)),
            whole((HALF, SIDE_W)),
            whole((HALF, SIDE_W)),
            whole((SIDE_W, SIDE_W)),
            whole((SIDE_W, 256)),
            whole((512, 256)),
            whole((HALF, WIDTH)),
        ],
        [whole((HALF, SIDE_W)), whole((HALF, SIDE_W)), whole((B_ROWS, 128))],
        [shape((HALF, SIDE_W), BF), shape((HALF, SIDE_W), F32), shape((B_ROWS, 128), BF)],
        flops=2 * HALF * 96 * 2048,
        nbytes=2 * 10**6,
    )(joined, djoined, dq, dkv_own, dkv_got, gate, gain, down, prior, wq, wkv, gather, out_low)


def grouped(weight, copies, offset):
    lead = weight.shape[:-1]
    groups = weight.reshape(lead + (4, 1, 24))
    groups = jnp.broadcast_to(groups, lead + (4, copies, 24)).reshape(lead + (4, copies * 24))
    pad = [(0, 0)] * (len(lead) + 1) + [(offset, 128 - offset - copies * 24)]
    return jnp.pad(groups, pad).reshape(lead + (512,))


def permutations(batch_size):
    move, flip = [], []
    for b in range(batch_size):
        core = b % 2
        flip.append((b, b - core + 1 - core))
        for x in range(TP):
            if x % 2 == core:
                target = b * TP + x
            elif core == 1:
                target = (b - 1) * TP + x + 1
            else:
                target = (b + 1) * TP + x - 1
            move.append((b * TP + x, target))
    return move, flip


def per_device(
    inputs, side_start, lengths, offset_bias, gain_attn, w_query, w_key, w_value, w_out, gain_ffn, w_inner,
    w_outer, narrowing_weight, gate_logit, side_gain1, side_qkv, side_proj, side_gain2, side_inner, side_outer,
    side_cotangent,
):
    x = lax.axis_index("tp")
    core = lax.rem(lax.axis_index("batch"), 2)
    move, flip = permutations(lax.axis_size("batch"))

    def moved(rows):
        return lax.ppermute(rows, ("batch", "tp"), move)

    def flipped(rows):
        return lax.ppermute(rows, "batch", flip)

    joined_qkv = jnp.concatenate(
        [
            w_query,
            jnp.zeros(w_query.shape[:2] + (64,), BF),
            w_key[..., :128],
            w_value[..., :128],
            w_key[..., 128:],
            w_value[..., 128:],
        ],
        axis=-1,
    )
    all_qkv, all_inner, all_outer, all_out = gather_weights(joined_qkv, w_inner, w_outer, w_out)
    side_query = side_qkv[..., :SIDE_W] * SIDE_SCALE
    side_key, side_value = side_qkv[..., SIDE_W : 2 * SIDE_W], side_qkv[..., 2 * SIDE_W :]
    wide_query = grouped(side_query, 3, 0)
    wide_kv = grouped(side_key, 3, 0) + grouped(side_value, 2, 72)
    back_query = side_query.astype(BF)
    lane_pad = [(0, 0), (0, 0), (0, 32)]
    back_kv = jnp.concatenate([jnp.pad(side_key, lane_pad), jnp.pad(side_value, lane_pad)], axis=-1).astype(BF)
    eye = jnp.eye(SIDE_W, dtype=F32)
    spread_sel = grouped(eye, 2, 72).astype(BF)
    row_pad = [(0, 0), (0, 32)]
    gather_sel = jnp.concatenate(
        [jnp.pad(grouped(eye, 1, 0).T, row_pad), jnp.pad(grouped(eye, 1, 72).T, row_pad)], axis=1
    ).astype(BF)

    start = lax.div(x, 2) * (2 * HALF)

    def side_rows(half):
        return jnp.concatenate(
            [
                lax.dynamic_slice_in_dim(side_start, start + half * HALF, HALF, 0),
                lax.dynamic_slice_in_dim(side_cotangent, start + half * HALF, HALF, 0),
                jnp.broadcast_to(lax.dynamic_slice_in_dim(lengths, lax.div(x, 2), 1, 0).astype(F32), (8, SIDE_W)),
            ]
        )

    got = flipped(side_rows(1 - core))
    here = jnp.where(lax.rem(x, 2) == core, side_rows(core), got)
    state, cotangent, length = here[:HALF], here[HALF : 2 * HALF], here[2 * HALF, 0].astype(jnp.int32)
    table = offset_tables(offset_bias, core, 3 * x, length)
    first = x.reshape(1)

    b = moved(inputs).astype(F32)
    gains = [gain_attn.astype(F32), gain_ffn.astype(F32)]
    saved, side_saved = [], []
    for layer in range(2):
        gain_one, gain_two = gains[0][layer : layer + 1], gains[1][layer : layer + 1]
        q, own = project(layer, b, gain_one, all_qkv)
        other = flipped(own)
        mixed, lse = attend(q, own, other, table)
        mid, slope, out, out_low, down = feed(
            layer, mixed, b, all_out, gain_two, all_inner, all_outer, narrowing_weight[layer]
        )
        saved.append((b, q, own, other, lse, mid, slope, gain_one, gain_two))
        b = out
        gate, side_gain = gate_logit[layer : layer + 1], side_gain1[layer : layer + 1]
        joined, side_q, side_own = side_start_call(down, state, gate, side_gain, wide_query[layer], wide_kv[layer])
        side_other = flipped(side_own)
        weights = (side_proj[layer], side_gain2[layer : layer + 1], side_inner[layer], side_outer[layer])
        side_mixed, side_lse, after = side_attend(first, side_q, side_own, side_other, table, joined, *weights)
        side_saved.append(
            (joined, side_mixed, weights, side_q, side_own, side_other, side_lse, gate, side_gain, down, state, out_low)
        )
        state = after
    backbone_out = moved(out_low)
    side_out = state

    grad_side = cotangent
    ddowns, sums = [None, None], [None, None]
    for layer in (1, 0):
        joined, side_mixed, weights, side_q, side_own, side_other, side_lse, gate, side_gain, down, prior, low = (
            side_saved[layer]
        )
        djoined, dq, dkv_own, dkv_other, sums_a = side_back(
            first, grad_side, joined, side_mixed, *weights, spread_sel, side_q, side_own, side_other, table, side_lse
        )
        dkv_got = flipped(dkv_other)
        ddowns[layer], grad_side, sums_b = side_end(
            joined, djoined, dq, dkv_own, dkv_got, gate, side_gain, down, prior,
            back_query[layer], back_kv[layer], gather_sel, low,
        )
        sums[layer] = (sums_a, sums_b)
    summed = sum_gradients(sums[0] + sums[1])

    def to_all(rows):
        partner = flipped(rows)
        sequence = jnp.where(core == 0, jnp.concatenate([rows, partner]), jnp.concatenate([partner, rows]))
        every = lax.all_gather(sequence, "tp", axis=0)
        return jnp.concatenate(
            [lax.dynamic_index_in_dim(every, core + 2 * n, 0, keepdims=False) for n in range(2)]
        )

    side_out = to_all(side_out)
    grad_start = to_all(grad_side)

    grad = jnp.zeros((HALF, WIDTH), F32)
    for layer in (1, 0):
        b, q, own, other, lse, mid, slope, gain_one, gain_two = saved[layer]
        gmid, dmixed = feed_back(
            layer, grad, ddowns[layer], narrowing_weight[layer], mid, gain_two, slope, all_outer, all_inner, all_out
        )
        dq, dkv_own, dkv_other = attend_back(q, own, other, table, lse, dmixed)
        dkv_got = flipped(dkv_other)
        grad = project_back(
            layer, dq, dkv_own, dkv_got, all_qkv, b, gain_one, gmid, F32 if layer == 1 else BF
        )
    grad_inputs = moved(grad).astype(F32)
    return (backbone_out, side_out, grad_inputs, grad_start) + tuple(summed)


def solution(mesh):
    in_specs = (
        P(("batch", "tp"), None),
        P("batch", None),
        P("batch"),
        P(),
        P(),
        P(None, None, "tp"),
        P(None, None, "tp"),
        P(None, None, "tp"),
        P(None, "tp", None),
        P(),
        P(None, None, "tp"),
        P(None, "tp", None),
        P(),
        P(),
        P(),
        P(),
        P(),
        P(),
        P(),
        P(),
        P("batch", None),
    )
    out_specs = (
        P(("batch", "tp"), None),
        P("batch", None),
        P(("batch", "tp"), None),
        P("batch", None),
        P(),
        P(),
        P(),
        P(),
        P(),
        P(),
        P(),
        P(),
    )
    return jax.shard_map(per_device, mesh=mesh, in_specs=in_specs, out_specs=out_specs, check_vma=False)
```

```python
from functools import partial
import math

import jax
import jax.numpy as jnp
import numpy as np
from jax import lax
from jax.experimental import pallas as pl
from jax.experimental.pallas import tpu as pltpu
from jax.sharding import PartitionSpec as P


BF = jnp.bfloat16
F32 = jnp.float32
EPSILON = 1e-06
NEGATIVE = -1e30
HIGHEST = lax.Precision.HIGHEST
MESH = pl.DeviceIdType.MESH
TP = 4
SIDES = 4
HALF = 256
WIDTH = 768
SIDE_W = 96
SIDE_FF = 384
SIDE_SCALE = 1.0 / math.sqrt(8)
GELU_K = math.sqrt(2.0 / math.pi)
VMEM_BYTES = 56 * 1024 * 1024

A_PROJ, A_INNER, A_OUTER, A_SMALL, A_ROWS = 0, 96, 384, 672, 688
B_QKV, B_DOWN, B_SMALL, B_ROWS = 0, 288, 864, 880
LAYER_ROWS = A_ROWS + B_ROWS
SUM_ROWS = 3584


def dot(a, b, ca, cb, precision=None):
    return lax.dot_general(
        a, b, (((ca,), (cb,)), ((), ())), preferred_element_type=F32, precision=precision
    )


def nn(a, b, precision=None):
    return dot(a, b, 1, 0, precision)


def nt(a, b, precision=None):
    return dot(a, b, 1, 1, precision)


def tn(a, b, precision=None):
    return dot(a, b, 0, 0, precision)


def rms_scale(values):
    return lax.rsqrt(jnp.mean(values * values, axis=-1, keepdims=True) + EPSILON)


def rms_back(values, gain_row, grad):
    scale = rms_scale(values)
    scaled = grad * gain_row
    inner = jnp.mean(scaled * values, axis=-1, keepdims=True)
    return scale * scaled - values * (scale * scale * scale * inner)


def gelu_parts(hidden):
    square = hidden * hidden
    tanh = jnp.tanh(GELU_K * hidden * (1.0 + 0.044715 * square))
    plus = 0.5 * (1.0 + tanh)
    slope = plus + (0.5 * GELU_K) * hidden * (1.0 - tanh * tanh) * (1.0 + (3 * 0.044715) * square)
    return hidden * plus, slope


def lane_mask(test):
    lanes = lax.broadcasted_iota(jnp.int32, (HALF, 128), 1)
    return jnp.where(test(lanes), 1.0, 0.0).astype(BF)


def row_block(shape, index_map):
    return pl.BlockSpec(shape, index_map)


def whole(shape):
    return pl.BlockSpec(shape, lambda *_: (0,) * len(shape))


def call(kernel, grid, in_specs, out_specs, out_shape, scratch=(), prefetch=0, flops=0, nbytes=0):
    return pl.pallas_call(
        kernel,
        grid_spec=pltpu.PrefetchScalarGridSpec(
            num_scalar_prefetch=prefetch,
            grid=grid,
            in_specs=in_specs,
            out_specs=out_specs,
            scratch_shapes=scratch,
        ),
        out_shape=out_shape,
        compiler_params=pltpu.CompilerParams(vmem_limit_bytes=VMEM_BYTES),
        cost_estimate=pl.CostEstimate(flops=flops, bytes_accessed=nbytes, transcendentals=0),
    )


def own_block(layer, rows, columns):
    return pl.BlockSpec((1, rows, columns), lambda *_: (layer, 0, 0))


def gathered_block(layer, rows, columns):
    return pl.BlockSpec((1, 1, rows, columns), lambda s, *_: (layer, jnp.maximum(s - 1, 0), 0, 0))


def for_shard(step, body, own_refs, gathered_refs):
    @pl.when(step == 0)
    def _():
        body(*[ref.at[0] for ref in own_refs])

    @pl.when(step > 0)
    def _():
        body(*[ref.at[0, 0] for ref in gathered_refs])


def shape(dims, dtype):
    return jax.ShapeDtypeStruct(dims, dtype)


def gather_kernel(qkv, inner, outer, wo, gq, gi, gu, go, xs, xr, ss, sr, ds, dr, ws, wr):
    x = lax.axis_index("tp")
    b = lax.axis_index("batch")
    c = lax.rem(b, 2)
    z = lax.rem(b // 2, SIDES)
    y = b // (2 * SIDES)
    left, right = {"tp": lax.rem(x + TP - 1, TP)}, {"tp": lax.rem(x + 1, TP)}

    def at(y_now, z_now, c_now):
        return {"batch": (y_now * SIDES + z_now) * 2 + c_now}

    up = (at(lax.rem(y + 1, SIDES), z, c), at(y, lax.rem(z + 1, SIDES), c))
    down = (at(lax.rem(y + SIDES - 1, SIDES), z, c), at(y, lax.rem(z + SIDES - 1, SIDES), c))
    partner = at(y, z, 1 - c)

    barrier = pltpu.get_barrier_semaphore()
    for device in (left, right, up[0], up[1], down[0], down[1], partner):
        pl.semaphore_signal(barrier, inc=1, device_id=device, device_id_type=MESH)
    pl.semaphore_wait(barrier, 7)

    def send(src, dst, send_sem, recv_sem, device):
        return pltpu.make_async_remote_copy(
            src_ref=src,
            dst_ref=dst,
            send_sem=send_sem,
            recv_sem=recv_sem,
            device_id=device,
            device_id_type=MESH,
        )

    def rows(start, count):
        return pl.ds(pl.multiple_of(start, 16), count)

    mine = rows(c * 384, 384)
    blocks = (rows(c * 384 + y * 48, 48), rows(c * 384 + 192 + z * 48, 48))
    back = (
        rows(c * 384 + lax.rem(y + SIDES - 1, SIDES) * 48, 48),
        rows(c * 384 + 192 + lax.rem(z + SIDES - 1, SIDES) * 48, 48),
    )
    ahead = (
        rows(c * 384 + lax.rem(y + 1, SIDES) * 48, 48),
        rows(c * 384 + 192 + lax.rem(z + 1, SIDES) * 48, 48),
    )
    chunks = [(source, target, layer) for layer in range(2) for source, target in ((qkv, gq), (inner, gi), (outer, gu))]
    count = len(chunks)

    def first(k):
        source, target, layer = chunks[k]
        return [
            send(
                source.at[layer, blocks[path]],
                target.at[layer, slot, blocks[path]],
                xs.at[k, path * 2 + slot],
                xr.at[k, path * 2 + slot],
                device,
            )
            for path in range(2)
            for device, slot in ((right, 1), (left, 0))
        ]

    def relay(k):
        _, target, layer = chunks[k]
        y_block, z_block = blocks
        return [
            send(target.at[layer, 1, y_block], target.at[layer, 2, y_block], xs.at[k, 4], xr.at[k, 4], right),
            send(target.at[layer, 0, z_block], target.at[layer, 2, z_block], xs.at[k, 5], xr.at[k, 5], left),
        ]

    def spread(k, part):
        _, target, layer = chunks[k]
        slots = pl.ds(0, 2) if part == 0 else pl.ds(2, 1)
        out = []
        for path in range(2):
            block = target.at[layer, slots, blocks[path]]
            for way, device in enumerate((up[path], down[path])):
                n = part * 4 + path * 2 + way
                out.append(send(block, block, ss.at[k, n], sr.at[k, n], device))
        return out

    def spread_relay(k):
        _, target, layer = chunks[k]
        out = []
        for path in range(2):
            if (k + path) % 2 == 0:
                block, device = target.at[layer, :, back[path]], up[path]
            else:
                block, device = target.at[layer, :, ahead[path]], down[path]
            out.append(send(block, block, ss.at[k, 8 + path], sr.at[k, 8 + path], device))
        return out

    def swap(k):
        _, target, layer = chunks[k]
        block = target.at[layer, :, mine]
        return [send(block, block, ds.at[k], dr.at[k], partner)]

    started = []

    def start(copies):
        for copy in copies:
            copy.start()
        started.extend(copies)
        return copies

    def arrived(copies):
        for copy in copies:
            copy.wait_recv()

    wo_rows = rows(c * 96, 96)
    wo_low, wo_high = rows(c * 96, 48), rows(c * 96 + 48, 48)
    firsts = {0: start(first(0)), 1: start(first(1))}
    relays, spreads, second, last = {}, {}, {}, {}
    for k in range(count):
        arrived(firsts[k])
        relays[k] = start(relay(k))
        spreads[k] = start(spread(k, 0))
        if k + 2 < count:
            firsts[k + 2] = start(first(k + 2))
        elif k + 2 == count:
            wo_first = start([
                send(wo.at[:, wo_rows], go.at[:, 1, wo_rows], ws.at[0], wr.at[0], right),
                send(wo.at[:, wo_rows], go.at[:, 0, wo_rows], ws.at[1], wr.at[1], left),
            ])
        if k >= 1:
            arrived(spreads[k - 1])
            second[k - 1] = start(spread_relay(k - 1))
        arrived(relays[k])
        spreads[k] += start(spread(k, 1))
        if k >= 2:
            arrived(second[k - 2])
            last[k - 2] = start(swap(k - 2))
    arrived(wo_first)
    wo_relay = start([
        send(go.at[:, 1, wo_low], go.at[:, 2, wo_low], ws.at[2], wr.at[2], right),
        send(go.at[:, 0, wo_high], go.at[:, 2, wo_high], ws.at[3], wr.at[3], left),
    ])
    arrived(spreads[count - 1])
    second[count - 1] = start(spread_relay(count - 1))
    arrived(second[count - 2])
    last[count - 2] = start(swap(count - 2))
    arrived(wo_relay)
    wo_block = go.at[:, :, wo_rows]
    wo_last = start([send(wo_block, wo_block, ws.at[4], wr.at[4], partner)])
    arrived(second[count - 1])
    last[count - 1] = start(swap(count - 1))
    for k in range(count):
        arrived(last[k])
    arrived(wo_last)
    for copy in started:
        copy.wait_send()


def gather_weights(qkv, inner, outer, wo):
    layers = qkv.shape[0]
    dma = pltpu.SemaphoreType.DMA
    anywhere = pl.BlockSpec(memory_space=pl.ANY)
    arrays = (qkv, inner, outer, wo)
    return pl.pallas_call(
        gather_kernel,
        out_shape=[shape((layers, TP - 1) + a.shape[1:], a.dtype) for a in arrays],
        in_specs=[anywhere] * 4,
        out_specs=[anywhere] * 4,
        scratch_shapes=[
            dma((6, 6)), dma((6, 6)), dma((6, 10)), dma((6, 10)), dma((6,)), dma((6,)), dma((5,)), dma((5,)),
        ],
        compiler_params=pltpu.CompilerParams(collective_id=0, has_side_effects=True),
    )(*arrays)


def sum_kernel(
    a0, b0, a1, b1, total, packed, from_core, half, from_x, piece, from_y, small, from_z, send_sems, recv_sems,
):
    x = lax.axis_index("tp")
    b = lax.axis_index("batch")
    c = lax.rem(b, 2)
    z = lax.rem(b // 2, SIDES)
    y = b // (2 * SIDES)

    def at(y_now, z_now, c_now):
        return {"batch": (y_now * SIDES + z_now) * 2 + c_now}

    partner = at(y, z, 1 - c)
    x_devices = [{"tp": lax.rem(x + d, TP)} for d in (1, 2, 3)]
    y_devices = [at(lax.rem(y + d, SIDES), z, c) for d in (1, 2, 3)]
    z_devices = [at(y, lax.rem(z + d, SIDES), c) for d in (1, 2, 3)]
    barrier = pltpu.get_barrier_semaphore()
    for device in [partner] + x_devices + y_devices + z_devices:
        pl.semaphore_signal(barrier, inc=1, device_id=device, device_id_type=MESH)

    packed[0:A_ROWS] = a0[...]
    packed[A_ROWS:LAYER_ROWS] = b0[...]
    packed[LAYER_ROWS : LAYER_ROWS + A_ROWS] = a1[...]
    packed[LAYER_ROWS + A_ROWS : 2 * LAYER_ROWS] = b1[...]
    packed[2 * LAYER_ROWS :] = jnp.zeros((SUM_ROWS - 2 * LAYER_ROWS, 128), BF)
    pl.semaphore_wait(barrier, 10)

    def send(n, src, dst, device):
        copy = pltpu.make_async_remote_copy(
            src_ref=src,
            dst_ref=dst,
            send_sem=send_sems.at[n],
            recv_sem=recv_sems.at[n],
            device_id=device,
            device_id_type=MESH,
        )
        copy.start()
        return copy

    def rows(start, count):
        return pl.ds(pl.multiple_of(start, 16), count)

    half_rows, x_rows, y_rows = SUM_ROWS // 2, SUM_ROWS // 8, SUM_ROWS // 32
    copies = [send(0, packed.at[rows((1 - c) * half_rows, half_rows)], from_core, partner)]
    copies[0].wait_recv()
    half[...] = (packed[rows(c * half_rows, half_rows)].astype(F32) + from_core[...].astype(F32)).astype(BF)

    now = [
        send(1 + d, half.at[rows(lax.rem(x + d + 1, TP) * x_rows, x_rows)], from_x.at[d], x_devices[d])
        for d in range(3)
    ]
    for copy in now:
        copy.wait_recv()
    copies += now
    piece[...] = (
        half[rows(x * x_rows, x_rows)].astype(F32)
        + from_x[0].astype(F32)
        + from_x[1].astype(F32)
        + from_x[2].astype(F32)
    ).astype(BF)

    now = [
        send(4 + d, piece.at[rows(lax.rem(y + d + 1, SIDES) * y_rows, y_rows)], from_y.at[d], y_devices[d])
        for d in range(3)
    ]
    for copy in now:
        copy.wait_recv()
    copies += now
    small[...] = (
        piece[rows(y * y_rows, y_rows)].astype(F32)
        + from_y[0].astype(F32)
        + from_y[1].astype(F32)
        + from_y[2].astype(F32)
    ).astype(BF)

    now = [send(7 + d, small, from_z.at[z], z_devices[d]) for d in range(3)]
    from_z[z] = small[...]
    for copy in now:
        copy.wait_recv()
    copies += now
    mine = rows(c * half_rows + x * x_rows + y * y_rows, y_rows)
    total[mine] = (
        from_z[0].astype(F32) + from_z[1].astype(F32) + from_z[2].astype(F32) + from_z[3].astype(F32)
    ).astype(BF)

    now = [send(10 + d, total.at[mine], total.at[mine], y_devices[d]) for d in range(3)]
    for copy in now:
        copy.wait_recv()
    copies += now
    mine = rows(c * half_rows + x * x_rows, x_rows)
    now = [send(13 + d, total.at[mine], total.at[mine], x_devices[d]) for d in range(3)]
    for copy in now:
        copy.wait_recv()
    copies += now
    mine = rows(c * half_rows, half_rows)
    now = [send(16, total.at[mine], total.at[mine], partner)]
    for copy in now:
        copy.wait_recv()
    copies += now
    for copy in copies:
        copy.wait_send()


def unpack_kernel(total, down_out, gate_out, gain1_out, qkv_out, proj_out, gain2_out, inner_out, outer_out):
    for layer in range(2):
        base = layer * LAYER_ROWS

        def part(start, count, base=base):
            return total[base + start : base + start + count].astype(F32)

        proj_out[layer] = part(A_PROJ, 96)[:, :SIDE_W]
        for n in range(3):
            inner_out[layer, :, n * 128 : (n + 1) * 128] = part(A_INNER + n * 96, 96)
            block = part(A_OUTER + n * 96, 128).T
            outer_out[layer, n * 128 : (n + 1) * 128] = block[:, :SIDE_W]
        triple = [part(A_ROWS + B_QKV + n * 96, 96)[:, :SIDE_W] for n in range(3)]
        qkv_out[layer] = jnp.concatenate(triple, axis=1)
        for n in range(6):
            block = part(A_ROWS + B_DOWN + n * 96, 128).T
            down_out[layer, n * 128 : (n + 1) * 128] = block[:, :SIDE_W]
        gain2_out[layer : layer + 1] = part(A_SMALL, 16)[0:1, :SIDE_W]
        rest = part(A_ROWS + B_SMALL, 16)
        gate_out[layer : layer + 1] = rest[0:1, :SIDE_W]
        gain1_out[layer : layer + 1] = rest[1:2, :SIDE_W]


def sum_gradients(parts):
    vmem = pl.BlockSpec(memory_space=pltpu.VMEM)
    dma = pltpu.SemaphoreType.DMA
    total = pl.pallas_call(
        sum_kernel,
        out_shape=shape((SUM_ROWS, 128), BF),
        in_specs=[vmem] * 4,
        out_specs=vmem,
        scratch_shapes=[
            pltpu.VMEM((SUM_ROWS, 128), BF),
            pltpu.VMEM((SUM_ROWS // 2, 128), BF),
            pltpu.VMEM((SUM_ROWS // 2, 128), BF),
            pltpu.VMEM((3, SUM_ROWS // 8, 128), BF),
            pltpu.VMEM((SUM_ROWS // 8, 128), BF),
            pltpu.VMEM((3, SUM_ROWS // 32, 128), BF),
            pltpu.VMEM((SUM_ROWS // 32, 128), BF),
            pltpu.VMEM((4, SUM_ROWS // 32, 128), BF),
            dma((17,)),
            dma((17,)),
        ],
        compiler_params=pltpu.CompilerParams(
            collective_id=1, has_side_effects=True, vmem_limit_bytes=VMEM_BYTES
        ),
    )(*parts)
    outs = [
        shape((2, WIDTH, SIDE_W), F32),
        shape((2, SIDE_W), F32),
        shape((2, SIDE_W), F32),
        shape((2, SIDE_W, 3 * SIDE_W), F32),
        shape((2, SIDE_W, SIDE_W), F32),
        shape((2, SIDE_W), F32),
        shape((2, SIDE_W, SIDE_FF), F32),
        shape((2, SIDE_FF, SIDE_W), F32),
    ]
    return call(
        unpack_kernel, (1,), [whole((SUM_ROWS, 128))], [whole(out.shape) for out in outs], outs, nbytes=4 * 10**6
    )(total)


def table_kernel(place, bias_ref, out, base):
    head = pl.program_id(0)
    core, own_end, other_end = place[1], place[2], place[3]

    @pl.when(head == 0)
    def _():
        rows = lax.broadcasted_iota(jnp.int32, (HALF, HALF), 0)
        columns = lax.broadcasted_iota(jnp.int32, (HALF, HALF), 1)
        reverse = jnp.where(rows + columns == HALF - 1, 1.0, 0.0).astype(BF)
        turned = [nn(bias_ref[:, n * HALF : (n + 1) * HALF], reverse) for n in range(4)]
        base[:, 0, :HALF] = turned[1]
        base[:, 0, HALF:] = turned[2]
        base[:, 1, :HALF] = jnp.where(core == 0, turned[2], turned[0])
        base[:, 1, HALF:] = jnp.where(core == 0, turned[3], turned[1])

    for side, end in enumerate((own_end, other_end)):
        spread = jnp.broadcast_to(base[head, side : side + 1], (HALF, 2 * HALF))
        rolled = pltpu.roll(spread, 0, 1, stride=1, stride_axis=0)[:, :HALF]
        keys = lax.broadcasted_iota(jnp.int32, (HALF, HALF), 0)
        out[0, side * HALF : (side + 1) * HALF] = jnp.where(keys < end, rolled, NEGATIVE).astype(BF)


def table_slot(shard, first):
    turn = lax.rem(shard + TP - first, TP)
    return turn + jnp.where(turn == 2, 1, 0) - jnp.where(turn == 3, 1, 0)


def offset_tables(offset_bias, place):
    heads = offset_bias.shape[0]
    bias = jnp.pad(offset_bias, ((0, 16 - heads), (0, 1)))
    return call(
        table_kernel,
        (heads,),
        [whole((16, 4 * HALF))],
        row_block(
            (1, 2 * HALF, HALF), lambda h, place: (table_slot(lax.div(h, 3), place[0]) * 3 + lax.rem(h, 3), 0, 0)
        ),
        shape((heads, 2 * HALF, HALF), BF),
        [pltpu.VMEM((16, 2, 2 * HALF), F32)],
        prefetch=1,
    )(place, bias)


def project_kernel(layer, b_ref, gain_ref, own_w, gathered_w, q_ref, kv_ref, normed):
    step = pl.program_id(0)

    @pl.when(step == 0)
    def _():
        b = b_ref[...].astype(F32)
        normed[...] = (b * rms_scale(b) * gain_ref[layer : layer + 1].astype(F32)).astype(BF)

    def body(w_ref):
        out = nn(normed[...], w_ref[...])
        q_ref[0] = (out[:, :256] * 0.125).astype(BF)
        kv_ref[0] = out[:, 256:].astype(BF)

    for_shard(step, body, [own_w], [gathered_w])


def project(layer, b, gain, weights):
    return call(
        partial(project_kernel, layer),
        (TP,),
        [
            whole((HALF, WIDTH)),
            whole((2, WIDTH)),
            own_block(layer, WIDTH, 640),
            gathered_block(layer, WIDTH, 640),
        ],
        [row_block((1, HALF, 256), lambda s: (s, 0, 0)), row_block((1, HALF, 384), lambda s: (s, 0, 0))],
        [shape((TP, HALF, 256), BF), shape((TP, HALF, 384), BF)],
        [pltpu.VMEM((HALF, WIDTH), BF)],
        flops=2 * HALF * WIDTH * 2560,
        nbytes=5 * 10**6,
    )(b, gain, *weights)


def head_parts(q, dm=None):
    low = lane_mask(lambda lanes: lanes < 64)
    high = lane_mask(lambda lanes: lanes >= 64)
    queries = [q[:, :128] * low, q[:, :128] * high, q[:, 128:]]
    key_slabs = [slice(0, 128), slice(0, 128), slice(256, 384)]
    value_slabs = [slice(128, 256), slice(128, 256), slice(256, 384)]
    if dm is None:
        return queries, key_slabs, value_slabs
    return queries, key_slabs, value_slabs, [dm[:, :128] * low, dm[:, :128] * high, dm[:, 128:]]


def softmax_parts(scores_own, scores_other):
    top = jnp.maximum(
        jnp.max(scores_own, axis=0, keepdims=True), jnp.max(scores_other, axis=0, keepdims=True)
    )
    exp_own = jnp.exp(scores_own - top)
    exp_other = jnp.exp(scores_other - top)
    total = jnp.sum(exp_own, axis=0, keepdims=True) + jnp.sum(exp_other, axis=0, keepdims=True)
    return exp_own, exp_other, 1.0 / total, top + jnp.log(total)


def attend_kernel(q_ref, own_ref, other_ref, table_ref, mixed_ref, lse_ref):
    queries, key_slabs, value_slabs = head_parts(q_ref[0])
    rows = []
    for j in range(3):
        own, other = own_ref[0, :, key_slabs[j]], other_ref[0, :, key_slabs[j]]
        scores_own = nt(own, queries[j]) + table_ref[j, :HALF].astype(F32)
        scores_other = nt(other, queries[j]) + table_ref[j, HALF:].astype(F32)
        exp_own, exp_other, inverse, lse = softmax_parts(scores_own, scores_other)
        mixed = tn(own_ref[0, :, value_slabs[j]], exp_own.astype(BF)) + tn(
            other_ref[0, :, value_slabs[j]], exp_other.astype(BF)
        )
        rows.append((mixed[:64] if j == 0 else mixed[64:]) * inverse)
        lse_ref[0, j : j + 1] = lse
    mixed_ref[0, :, :128] = jnp.concatenate(rows[:2], axis=0).T.astype(BF)
    third = jnp.concatenate([rows[2], jnp.zeros_like(rows[2])], axis=0).T
    mixed_ref[0, :, 128:] = third[:, :64].astype(BF)


def attend(q, own, other, table):
    return call(
        attend_kernel,
        (TP,),
        [
            row_block((1, HALF, 256), lambda s: (s, 0, 0)),
            row_block((1, HALF, 384), lambda s: (s, 0, 0)),
            row_block((1, HALF, 384), lambda s: (s, 0, 0)),
            row_block((3, 2 * HALF, HALF), lambda s: (s, 0, 0)),
        ],
        [row_block((1, HALF, 192), lambda s: (s, 0, 0)), row_block((1, 8, HALF), lambda s: (s, 0, 0))],
        [shape((TP, HALF, 192), BF), shape((TP, 8, HALF), F32)],
        flops=12 * 4 * 2 * HALF * HALF * 128,
        nbytes=5 * 10**6,
    )(q, own, other, table)


def feed_kernel(
    layer, mixed_ref, b_ref, own_wo, gathered_wo, gain_ref, own_inner, inner_ref, own_outer, outer_ref, narrow_ref,
    mid_ref, slope_ref, out_ref, out_low_ref, down_ref, normed, acc,
):
    step = pl.program_id(0)

    @pl.when(step == 0)
    def _():
        mid = b_ref[...].astype(F32) + nn(mixed_ref[0], own_wo[0])
        for s in range(1, TP):
            mid = mid + nn(mixed_ref[s], gathered_wo[0, s - 1])
        mid_ref[...] = mid
        acc[...] = mid
        normed[...] = (mid * rms_scale(mid) * gain_ref[layer : layer + 1].astype(F32)).astype(BF)

    def body(inner, outer):
        active, slope = gelu_parts(nn(normed[...], inner[...]))
        slope_ref[0] = slope.astype(BF)
        acc[...] += nn(active.astype(BF), outer[...])

    for_shard(step, body, [own_inner, own_outer], [inner_ref, outer_ref])

    @pl.when(step == TP - 1)
    def _():
        out = acc[...]
        low = out.astype(BF)
        out_ref[...] = out
        out_low_ref[...] = low
        down_ref[...] = nn(low, narrow_ref[layer]).astype(BF)


def feed(layer, mixed, b, wo, gain, inner, outer, narrow):
    return call(
        partial(feed_kernel, layer),
        (TP,),
        [
            whole((TP, HALF, 192)),
            whole((HALF, WIDTH)),
            own_block(layer, 192, WIDTH),
            row_block((1, TP - 1, 192, WIDTH), lambda s: (layer, 0, 0, 0)),
            whole((2, WIDTH)),
            own_block(layer, WIDTH, WIDTH),
            gathered_block(layer, WIDTH, WIDTH),
            own_block(layer, WIDTH, WIDTH),
            gathered_block(layer, WIDTH, WIDTH),
            whole((2, WIDTH, SIDE_W)),
        ],
        [
            whole((HALF, WIDTH)),
            row_block((1, HALF, WIDTH), lambda s: (s, 0, 0)),
            whole((HALF, WIDTH)),
            whole((HALF, WIDTH)),
            whole((HALF, SIDE_W)),
        ],
        [
            shape((HALF, WIDTH), F32),
            shape((TP, HALF, WIDTH), BF),
            shape((HALF, WIDTH), F32),
            shape((HALF, WIDTH), BF),
            shape((HALF, SIDE_W), BF),
        ],
        [pltpu.VMEM((HALF, WIDTH), BF), pltpu.VMEM((HALF, WIDTH), F32)],
        flops=2 * HALF * WIDTH * WIDTH * 9,
        nbytes=14 * 10**6,
    )(mixed, b, *wo, gain, *inner, *outer, narrow)


def feed_back_kernel(
    layer, grad_ref, ddown_ref, narrow_ref, mid_ref, gain_ref, slope_ref, own_outer, outer_ref, own_inner, inner_ref,
    own_wo, gathered_wo, gmid_ref, dmixed_ref, grad, grad_low, acc,
):
    step = pl.program_id(0)

    @pl.when(step == 0)
    def _():
        total = nt(ddown_ref[...], narrow_ref[layer])
        if layer == 0:
            total = total + grad_ref[...]
        grad[...] = total
        grad_low[...] = total.astype(BF)
        acc[...] = jnp.zeros_like(acc)

    def body(outer, inner):
        dactive = nt(grad_low[...], outer[...])
        dhidden = (dactive * slope_ref[0].astype(F32)).astype(BF)
        acc[...] += nt(dhidden, inner[...])

    for_shard(step, body, [own_outer, own_inner], [outer_ref, inner_ref])

    @pl.when(step == TP - 1)
    def _():
        gmid = grad[...] + rms_back(mid_ref[...], gain_ref[layer : layer + 1].astype(F32), acc[...])
        gmid_ref[...] = gmid
        low = gmid.astype(BF)
        for s in range(TP):
            wo_ref = own_wo.at[0] if s == 0 else gathered_wo.at[0, s - 1]
            dmixed_ref[s, :, :128] = nt(low, wo_ref[:128]).astype(BF)
            third = jnp.concatenate([jnp.zeros((64, WIDTH), BF), wo_ref[128:]], axis=0)
            dmixed_ref[s, :, 128:] = nt(low, third).astype(BF)


def feed_back(layer, grad, ddown, narrow, mid, gain, slope, outer, inner, wo):
    return call(
        partial(feed_back_kernel, layer),
        (TP,),
        [
            whole(grad.shape),
            whole((HALF, SIDE_W)),
            whole((2, WIDTH, SIDE_W)),
            whole((HALF, WIDTH)),
            whole((2, WIDTH)),
            row_block((1, HALF, WIDTH), lambda s: (s, 0, 0)),
            own_block(layer, WIDTH, WIDTH),
            gathered_block(layer, WIDTH, WIDTH),
            own_block(layer, WIDTH, WIDTH),
            gathered_block(layer, WIDTH, WIDTH),
            own_block(layer, 192, WIDTH),
            row_block((1, TP - 1, 192, WIDTH), lambda s: (layer, 0, 0, 0)),
        ],
        [whole((HALF, WIDTH)), whole((TP, HALF, 256))],
        [shape((HALF, WIDTH), F32), shape((TP, HALF, 256), BF)],
        [pltpu.VMEM((HALF, WIDTH), F32), pltpu.VMEM((HALF, WIDTH), BF), pltpu.VMEM((HALF, WIDTH), F32)],
        flops=2 * HALF * WIDTH * WIDTH * 9,
        nbytes=14 * 10**6,
    )(grad, ddown, narrow, mid, gain, slope, *outer, *inner, *wo)


def score_gradients(scores, lse, dprobs):
    probs = [jnp.exp(s - lse) for s in scores]
    inner = jnp.sum(probs[0] * dprobs[0], axis=0, keepdims=True) + jnp.sum(
        probs[1] * dprobs[1], axis=0, keepdims=True
    )
    dscores = [(p * (d - inner)).astype(BF) for p, d in zip(probs, dprobs)]
    return [p.astype(BF) for p in probs], dscores


def attend_back_kernel(
    q_ref, own_ref, other_ref, table_ref, lse_ref, dmixed_ref, dq_ref, dkv_own_ref, dkv_other_ref
):
    queries, key_slabs, value_slabs, dmixed = head_parts(q_ref[0], dmixed_ref[0])
    halves = (own_ref, other_ref)
    probs, dscores, dq_rows = [], [], []
    for j in range(3):
        keys = [ref[0, :, key_slabs[j]] for ref in halves]
        scores = [
            nt(k, queries[j]) + table_ref[j, n * HALF : (n + 1) * HALF].astype(F32) for n, k in enumerate(keys)
        ]
        dprobs = [nt(ref[0, :, value_slabs[j]], dmixed[j]) for ref in halves]
        p, ds = score_gradients(scores, lse_ref[0, j : j + 1], dprobs)
        probs.append(p)
        dscores.append(ds)
        dq = tn(keys[0], ds[0]) + tn(keys[1], ds[1])
        dq_rows.append(dq[64:] if j == 1 else dq[:64])
    dq_ref[0, :, :128] = (jnp.concatenate(dq_rows[:2], axis=0).T * 0.125).astype(BF)
    third = jnp.concatenate([dq_rows[2], jnp.zeros_like(dq_rows[2])], axis=0)
    dq_ref[0, :, 128:] = (third.T * 0.125).astype(BF)
    right = [
        jnp.concatenate(queries[:2], axis=0),
        jnp.concatenate(dmixed[:2], axis=0),
        jnp.concatenate([queries[2], dmixed[2]], axis=0),
    ]
    for n, ref in enumerate((dkv_own_ref, dkv_other_ref)):
        left = [
            jnp.concatenate([dscores[0][n], dscores[1][n]], axis=1),
            jnp.concatenate([probs[0][n], probs[1][n]], axis=1),
            jnp.concatenate([dscores[2][n], probs[2][n]], axis=1),
        ]
        for m in range(3):
            ref[0, :, m * 128 : (m + 1) * 128] = nn(left[m], right[m]).astype(ref.dtype)


def attend_back(q, own, other, table, lse, dmixed):
    return call(
        attend_back_kernel,
        (TP,),
        [
            row_block((1, HALF, 256), lambda s: (s, 0, 0)),
            row_block((1, HALF, 384), lambda s: (s, 0, 0)),
            row_block((1, HALF, 384), lambda s: (s, 0, 0)),
            row_block((3, 2 * HALF, HALF), lambda s: (s, 0, 0)),
            row_block((1, 8, HALF), lambda s: (s, 0, 0)),
            row_block((1, HALF, 256), lambda s: (s, 0, 0)),
        ],
        [
            row_block((1, HALF, 256), lambda s: (s, 0, 0)),
            row_block((1, HALF, 384), lambda s: (s, 0, 0)),
            row_block((1, HALF, 384), lambda s: (s, 0, 0)),
        ],
        [shape((TP, HALF, 256), BF), shape((TP, HALF, 384), F32), shape((TP, HALF, 384), BF)],
        flops=12 * 10 * 2 * HALF * HALF * 128,
        nbytes=9 * 10**6,
    )(q, own, other, table, lse, dmixed)


def project_back_kernel(layer, dq_ref, own_ref, got_ref, own_w, gathered_w, b_ref, gain_ref, gmid_ref, out_ref, acc):
    step = pl.program_id(0)

    @pl.when(step == 0)
    def _():
        acc[...] = jnp.zeros_like(acc)

    dkv = (own_ref[0] + got_ref[0].astype(F32)).astype(BF)

    def body(w_ref):
        acc[...] += nt(dq_ref[0], w_ref[:, :256]) + nt(dkv, w_ref[:, 256:])

    for_shard(step, body, [own_w], [gathered_w])

    @pl.when(step == TP - 1)
    def _():
        b = b_ref[...].astype(F32)
        out = gmid_ref[...] + rms_back(b, gain_ref[layer : layer + 1].astype(F32), acc[...])
        out_ref[...] = out.astype(out_ref.dtype)


def project_back(layer, dq, dkv_own, dkv_got, weights, b, gain, gmid, out_type):
    return call(
        partial(project_back_kernel, layer),
        (TP,),
        [
            row_block((1, HALF, 256), lambda s: (s, 0, 0)),
            row_block((1, HALF, 384), lambda s: (s, 0, 0)),
            row_block((1, HALF, 384), lambda s: (s, 0, 0)),
            own_block(layer, WIDTH, 640),
            gathered_block(layer, WIDTH, 640),
            whole((HALF, WIDTH)),
            whole((2, WIDTH)),
            whole((HALF, WIDTH)),
        ],
        whole((HALF, WIDTH)),
        shape((HALF, WIDTH), out_type),
        [pltpu.VMEM((HALF, WIDTH), F32)],
        flops=2 * HALF * WIDTH * 2560,
        nbytes=8 * 10**6,
    )(dq, dkv_own, dkv_got, *weights, b, gain, gmid)


def split_pack(values, low_test):
    high = values.astype(BF)
    low = (values - high.astype(F32)).astype(BF)
    mask = lane_mask(low_test)
    return high * (1 - mask) + low * mask


def side_start_kernel(layer, down_ref, prior_ref, gate_ref, gain_ref, wq_ref, wkv_ref, joined_ref, q_ref, kv_ref):
    mix = jax.nn.sigmoid(gate_ref[layer : layer + 1])
    joined = mix * down_ref[...].astype(F32) + (1.0 - mix) * prior_ref[...]
    joined_ref[...] = joined
    normed = joined * rms_scale(joined) * gain_ref[layer : layer + 1]
    q = nn(normed, wq_ref[layer], HIGHEST)
    kv = nn(normed, wkv_ref[layer], HIGHEST)
    for g in range(4):
        lanes = slice(g * 128, (g + 1) * 128)
        q_ref[g] = split_pack(q[:, lanes], lambda n: (n >= 24) & (n < 48))
        kv_ref[g] = split_pack(kv[:, lanes], lambda n: ((n >= 48) & (n < 72)) | (n >= 96))


def side_start_call(layer, down, prior, gate, gain, wq, wkv):
    return call(
        partial(side_start_kernel, layer),
        (1,),
        [
            whole((HALF, SIDE_W)),
            whole((HALF, SIDE_W)),
            whole((2, SIDE_W)),
            whole((2, SIDE_W)),
            whole((2, SIDE_W, 512)),
            whole((2, SIDE_W, 512)),
        ],
        [whole((HALF, SIDE_W)), whole((4, HALF, 128)), whole((4, HALF, 128))],
        [shape((HALF, SIDE_W), F32), shape((4, HALF, 128), BF), shape((4, HALF, 128), BF)],
        flops=6 * 2 * HALF * SIDE_W * 1024,
        nbytes=2 * 10**6,
    )(down, prior, gate, gain, wq, wkv)


def of_head(j, blocks):
    def test(lanes):
        hit = (lanes >= blocks[0] * 24 + j * 8) & (lanes < blocks[0] * 24 + j * 8 + 8)
        for n in blocks[1:]:
            hit = hit | ((lanes >= n * 24 + j * 8) & (lanes < n * 24 + j * 8 + 8))
        return hit

    return lane_mask(test)


def transposed(rows):
    return jnp.concatenate([rows, jnp.zeros((32, rows.shape[1]), rows.dtype)], axis=0).T[:, :SIDE_W]


def side_attend_kernel(
    layer, place, q_ref, own_ref, other_ref, table_ref, joined_ref, proj_ref, gain_ref, inner_ref, outer_ref,
    mixed_ref, lse_ref, out_ref, mixed_rows,
):
    group = pl.program_id(0)
    for j in range(3):
        q = q_ref[0] * of_head(j, (0, 1, 2))
        scores_own = nt(own_ref[0], q) + table_ref[j, :HALF].astype(F32)
        scores_other = nt(other_ref[0], q) + table_ref[j, HALF:].astype(F32)
        exp_own, exp_other, inverse, lse = softmax_parts(scores_own, scores_other)
        mixed = tn(own_ref[0], exp_own.astype(BF)) + tn(other_ref[0], exp_other.astype(BF))
        head = (mixed[72 + j * 8 : 80 + j * 8] + mixed[96 + j * 8 : 104 + j * 8]) * inverse
        mixed_rows[pl.ds(pl.multiple_of(group * 24 + j * 8, 8), 8)] = head
        lse_ref[0, j : j + 1] = lse

    @pl.when(group == 3)
    def _():
        mixed = transposed(mixed_rows[...])
        mixed_ref[...] = mixed
        joined = joined_ref[...] + nn(mixed, proj_ref[0], HIGHEST)
        normed = joined * rms_scale(joined) * gain_ref[layer : layer + 1]
        active, _ = gelu_parts(nn(normed, inner_ref[0], HIGHEST))
        out_ref[...] = joined + nn(active, outer_ref[0], HIGHEST)


def group_table(g, place):
    return (table_slot(g, place[0]), 0, 0)


def side_attend(layer, place, q, own, other, table, joined, proj, gain, inner, outer):
    return call(
        partial(side_attend_kernel, layer),
        (4,),
        [
            row_block((1, HALF, 128), lambda g, place: (g, 0, 0)),
            row_block((1, HALF, 128), lambda g, place: (g, 0, 0)),
            row_block((1, HALF, 128), lambda g, place: (g, 0, 0)),
            row_block((3, 2 * HALF, HALF), group_table),
            whole((HALF, SIDE_W)),
            own_block(layer, SIDE_W, SIDE_W),
            whole((2, SIDE_W)),
            own_block(layer, SIDE_W, SIDE_FF),
            own_block(layer, SIDE_FF, SIDE_W),
        ],
        [whole((HALF, SIDE_W)), row_block((1, 8, HALF), lambda g, place: (g, 0, 0)), whole((HALF, SIDE_W))],
        [shape((HALF, SIDE_W), F32), shape((4, 8, HALF), F32), shape((HALF, SIDE_W), F32)],
        [pltpu.VMEM((SIDE_W, HALF), F32)],
        prefetch=1,
        flops=12 * 4 * 2 * HALF * HALF * 128,
        nbytes=5 * 10**6,
    )(place, q, own, other, table, joined, proj, gain, inner, outer)


def side_back_kernel(
    layer, place, grad_ref, joined_ref, mixed_ref, proj_ref, gain_ref, inner_ref, outer_ref, spread_ref,
    q_ref, own_ref, other_ref, table_ref, lse_ref,
    djoined_ref, dq_ref, dkv_own_ref, dkv_other_ref, sums_ref, dmixed,
):
    group = pl.program_id(0)

    @pl.when(group == 0)
    def _():
        grad = grad_ref[...]
        grad_low = grad.astype(BF)
        mixed = mixed_ref[...]
        gain = gain_ref[layer : layer + 1]
        joined = joined_ref[...] + nn(mixed, proj_ref[0], HIGHEST)
        unit = joined * rms_scale(joined)
        normed = unit * gain
        active, slope = gelu_parts(nn(normed, inner_ref[0], HIGHEST))
        dhidden = (nt(grad_low, outer_ref[0].astype(BF)) * slope).astype(BF)
        dnormed = nt(dhidden, inner_ref[0].astype(BF))
        djoined = grad + rms_back(joined, gain, dnormed)
        djoined_ref[...] = djoined
        djoined_low = djoined.astype(BF)
        dmixed_low = nt(djoined_low, proj_ref[0].astype(BF)).astype(BF)
        for g in range(4):
            dmixed[g] = nn(dmixed_low, spread_ref[:, g * 128 : (g + 1) * 128]).astype(BF)
        sums_ref[...] = jnp.zeros_like(sums_ref)
        sums_ref[A_PROJ : A_PROJ + SIDE_W, :SIDE_W] = tn(mixed.astype(BF), djoined_low).astype(BF)
        inner_sum = tn(normed.astype(BF), dhidden).astype(BF)
        outer_sum = tn(grad_low, active.astype(BF)).astype(BF)
        for n in range(3):
            lanes = slice(n * 128, (n + 1) * 128)
            sums_ref[A_INNER + n * 96 : A_INNER + (n + 1) * 96] = inner_sum[:, lanes]
            sums_ref[A_OUTER + n * 96 : A_OUTER + (n + 1) * 96] = outer_sum[:, lanes]
        gain_sum = jnp.sum(dnormed * unit, axis=0, keepdims=True)
        sums_ref[A_SMALL:A_ROWS, :SIDE_W] = jnp.broadcast_to(gain_sum, (16, SIDE_W)).astype(BF)

    halves = (own_ref[0], other_ref[0])
    left, right = [[], []], []
    for j in range(3):
        q = q_ref[0] * of_head(j, (0, 1, 2))
        dm = dmixed[group] * of_head(j, (3, 4))
        scores = [nt(kv, q) + table_ref[j, n * HALF : (n + 1) * HALF].astype(F32) for n, kv in enumerate(halves)]
        dprobs = [nt(kv, dm) for kv in halves]
        p, ds = score_gradients(scores, lse_ref[0, j : j + 1], dprobs)
        dq = tn(halves[0], ds[0]) + tn(halves[1], ds[1])
        dq_ref[j * 8 : j * 8 + 8] = dq[j * 8 : j * 8 + 8] + dq[48 + j * 8 : 56 + j * 8]
        for n in range(2):
            left[n] += [ds[n], p[n]]
        right += [q_ref[0] * of_head(j, (0,)), dmixed[group] * of_head(j, (3,))]
    right = jnp.concatenate(right, axis=0)
    for n, ref in enumerate((dkv_own_ref, dkv_other_ref)):
        ref[0] = nn(jnp.concatenate(left[n], axis=1), right).astype(ref.dtype)


def side_back(layer, place, grad, joined, mixed, proj, gain, inner, outer, spread, q, own, other, table, lse):
    return call(
        partial(side_back_kernel, layer),
        (4,),
        [
            whole((HALF, SIDE_W)),
            whole((HALF, SIDE_W)),
            whole((HALF, SIDE_W)),
            own_block(layer, SIDE_W, SIDE_W),
            whole((2, SIDE_W)),
            own_block(layer, SIDE_W, SIDE_FF),
            own_block(layer, SIDE_FF, SIDE_W),
            whole((SIDE_W, 512)),
            row_block((1, HALF, 128), lambda g, place: (g, 0, 0)),
            row_block((1, HALF, 128), lambda g, place: (g, 0, 0)),
            row_block((1, HALF, 128), lambda g, place: (g, 0, 0)),
            row_block((3, 2 * HALF, HALF), group_table),
            row_block((1, 8, HALF), lambda g, place: (g, 0, 0)),
        ],
        [
            whole((HALF, SIDE_W)),
            row_block((24, HALF), lambda g, place: (g, 0)),
            row_block((1, HALF, 128), lambda g, place: (g, 0, 0)),
            row_block((1, HALF, 128), lambda g, place: (g, 0, 0)),
            whole((A_ROWS, 128)),
        ],
        [
            shape((HALF, SIDE_W), F32),
            shape((SIDE_W, HALF), F32),
            shape((4, HALF, 128), F32),
            shape((4, HALF, 128), BF),
            shape((A_ROWS, 128), BF),
        ],
        [pltpu.VMEM((4, HALF, 128), BF)],
        prefetch=1,
        flops=12 * 10 * 2 * HALF * HALF * 128,
        nbytes=6 * 10**6,
    )(place, grad, joined, mixed, proj, gain, inner, outer, spread, q, own, other, table, lse)


def side_end_kernel(
    layer, joined_ref, djoined_ref, dq_ref, own_ref, got_ref, gate_ref, gain_ref, down_ref, prior_ref,
    wq_ref, wkv_ref, gather_ref, out_low_ref, ddown_ref, dprior_ref, sums_ref,
):
    joined = joined_ref[...]
    unit = joined * rms_scale(joined)
    gain = gain_ref[layer : layer + 1]
    normed_low = (unit * gain).astype(BF)
    dq = transposed(dq_ref[...]).astype(BF)
    dkv = jnp.zeros((HALF, 256), F32)
    for g in range(4):
        both = (own_ref[g] + got_ref[g].astype(F32)).astype(BF)
        dkv = dkv + nn(both, gather_ref[g * 128 : (g + 1) * 128])
    dkv = dkv.astype(BF)
    dnormed = nt(dq, wq_ref[layer]) + nt(dkv, wkv_ref[layer])
    djoined = djoined_ref[...] + rms_back(joined, gain, dnormed)
    mix = jax.nn.sigmoid(gate_ref[layer : layer + 1])
    down = down_ref[...].astype(F32)
    ddown = (mix * djoined).astype(BF)
    ddown_ref[...] = ddown
    dprior_ref[...] = (1.0 - mix) * djoined
    gate_sum = jnp.sum(djoined * (down - prior_ref[...]), axis=0, keepdims=True) * mix * (1.0 - mix)
    gain_sum = jnp.sum(dnormed * unit, axis=0, keepdims=True)
    sums_ref[...] = jnp.zeros_like(sums_ref)
    sums_ref[B_QKV : B_QKV + 96, :SIDE_W] = (tn(normed_low, dq) * SIDE_SCALE).astype(BF)
    kv_sum = tn(normed_low, dkv).astype(BF)
    sums_ref[B_QKV + 96 : B_QKV + 192] = kv_sum[:, :128]
    sums_ref[B_QKV + 192 : B_QKV + 288] = kv_sum[:, 128:]
    down_sum = tn(ddown, out_low_ref[...]).astype(BF)
    for n in range(6):
        sums_ref[B_DOWN + n * 96 : B_DOWN + (n + 1) * 96] = down_sum[:, n * 128 : (n + 1) * 128]
    row = lax.broadcasted_iota(jnp.int32, (16, SIDE_W), 0)
    sums_ref[B_SMALL:B_ROWS, :SIDE_W] = jnp.where(row == 0, gate_sum, gain_sum).astype(BF)


def side_end(layer, joined, djoined, dq, dkv_own, dkv_got, gate, gain, down, prior, wq, wkv, gather, out_low):
    return call(
        partial(side_end_kernel, layer),
        (1,),
        [
            whole((HALF, SIDE_W)),
            whole((HALF, SIDE_W)),
            whole((SIDE_W, HALF)),
            whole((4, HALF, 128)),
            whole((4, HALF, 128)),
            whole((2, SIDE_W)),
            whole((2, SIDE_W)),
            whole((HALF, SIDE_W)),
            whole((HALF, SIDE_W)),
            whole((2, SIDE_W, SIDE_W)),
            whole((2, SIDE_W, 256)),
            whole((512, 256)),
            whole((HALF, WIDTH)),
        ],
        [whole((HALF, SIDE_W)), whole((HALF, SIDE_W)), whole((B_ROWS, 128))],
        [shape((HALF, SIDE_W), BF), shape((HALF, SIDE_W), F32), shape((B_ROWS, 128), BF)],
        flops=2 * HALF * 96 * 2048,
        nbytes=2 * 10**6,
    )(joined, djoined, dq, dkv_own, dkv_got, gate, gain, down, prior, wq, wkv, gather, out_low)


def grouped(blocks):
    out = np.zeros((SIDE_W, 512), np.float32)
    for column in range(SIDE_W):
        for block in blocks:
            out[column, column // 24 * 128 + block * 24 + column % 24] = 1.0
    return out


def place_columns(target, source, start):
    out = np.zeros((3 * SIDE_W, target.shape[1]), np.float32)
    out[start : start + SIDE_W] = target
    return out + source


WIDE_QUERY = place_columns(grouped((0, 1, 2)), 0.0, 0)
WIDE_KV = place_columns(grouped((3, 4)), place_columns(grouped((0, 1, 2)), 0.0, SIDE_W), 2 * SIDE_W)
SPREAD = grouped((3, 4))
COMPACT = np.zeros((512, 256), np.float32)
COMPACT[:, :SIDE_W] = grouped((0,)).T
COMPACT[:, 128 : 128 + SIDE_W] = grouped((3,)).T


def side_weights_kernel(w_ref, wide_query_ref, wide_kv_ref, query_out, kv_out, back_query, back_kv):
    for layer in range(2):
        weight = w_ref[layer]
        query_out[layer] = nn(weight, wide_query_ref[...], HIGHEST) * SIDE_SCALE
        kv_out[layer] = nn(weight, wide_kv_ref[...], HIGHEST)
        back_query[layer] = (weight[:, :SIDE_W] * SIDE_SCALE).astype(BF)
        zero = jnp.zeros((SIDE_W, 32), F32)
        back_kv[layer] = jnp.concatenate(
            [weight[:, SIDE_W : 2 * SIDE_W], zero, weight[:, 2 * SIDE_W :], zero], axis=1
        ).astype(BF)


def side_weights(side_qkv):
    dims = [((2, SIDE_W, 512), F32), ((2, SIDE_W, 512), F32), ((2, SIDE_W, SIDE_W), BF), ((2, SIDE_W, 256), BF)]
    return call(
        side_weights_kernel,
        (1,),
        [whole((2, SIDE_W, 3 * SIDE_W)), whole((3 * SIDE_W, 512)), whole((3 * SIDE_W, 512))],
        [whole(d) for d, _ in dims],
        [shape(*d) for d in dims],
        nbytes=2 * 10**6,
    )(side_qkv, WIDE_QUERY, WIDE_KV)


def permutations(batch_size):
    move, flip = [], []
    for b in range(batch_size):
        core = b % 2
        flip.append((b, b - core + 1 - core))
        for x in range(TP):
            if x % 2 == core:
                target = b * TP + x
            elif core == 1:
                target = (b - 1) * TP + x + 1
            else:
                target = (b + 1) * TP + x - 1
            move.append((b * TP + x, target))
    return move, flip


def per_device(
    inputs, side_start, lengths, offset_bias, gain_attn, w_query, w_key, w_value, w_out, gain_ffn, w_inner,
    w_outer, narrowing_weight, gate_logit, side_gain1, side_qkv, side_proj, side_gain2, side_inner, side_outer,
    side_cotangent,
):
    x = lax.axis_index("tp")
    core = lax.rem(lax.axis_index("batch"), 2)
    move, flip = permutations(lax.axis_size("batch"))

    def moved(rows):
        return lax.ppermute(rows, ("batch", "tp"), move)

    def flipped(rows):
        return lax.ppermute(rows, "batch", flip)

    joined_qkv = jnp.concatenate(
        [
            w_query,
            jnp.zeros(w_query.shape[:2] + (64,), BF),
            w_key[..., :128],
            w_value[..., :128],
            w_key[..., 128:],
            w_value[..., 128:],
        ],
        axis=-1,
    )
    owned = (joined_qkv, w_inner, w_outer, w_out)
    all_qkv, all_inner, all_outer, all_out = zip(owned, gather_weights(*owned))
    wide_query, wide_kv, back_query, back_kv = side_weights(side_qkv)
    spread_sel, compact_sel = jnp.asarray(SPREAD, BF), jnp.asarray(COMPACT, BF)

    start = lax.div(x, 2) * (2 * HALF)

    def side_rows(half):
        return jnp.concatenate(
            [
                lax.dynamic_slice_in_dim(side_start, start + half * HALF, HALF, 0),
                lax.dynamic_slice_in_dim(side_cotangent, start + half * HALF, HALF, 0),
                jnp.broadcast_to(lax.dynamic_slice_in_dim(lengths, lax.div(x, 2), 1, 0).astype(F32), (8, SIDE_W)),
            ]
        )

    got = flipped(side_rows(1 - core))
    here = jnp.where(lax.rem(x, 2) == core, side_rows(core), got)
    state, cotangent, length = here[:HALF], here[HALF : 2 * HALF], here[2 * HALF, 0].astype(jnp.int32)
    place = jnp.stack([x, core, length - core * HALF, length - (1 - core) * HALF])
    table = offset_tables(offset_bias, place)

    b = moved(inputs)
    saved, side_saved = [], []
    for layer in range(2):
        q, own = project(layer, b, gain_attn, all_qkv)
        other = flipped(own)
        mixed, lse = attend(q, own, other, table)
        mid, slope, out, out_low, down = feed(
            layer, mixed, b, all_out, gain_ffn, all_inner, all_outer, narrowing_weight
        )
        saved.append((b, q, own, other, lse, mid, slope))
        b = out
        joined, side_q, side_own = side_start_call(layer, down, state, gate_logit, side_gain1, wide_query, wide_kv)
        side_other = flipped(side_own)
        weights = (side_proj, side_gain2, side_inner, side_outer)
        side_mixed, side_lse, after = side_attend(
            layer, place, side_q, side_own, side_other, table, joined, *weights
        )
        side_saved.append((joined, side_mixed, side_q, side_own, side_other, side_lse, down, state, out_low))
        state = after
    backbone_out = moved(out_low)
    side_out = state

    grad_side = cotangent
    ddowns, sums = [None, None], [None, None]
    for layer in (1, 0):
        joined, side_mixed, side_q, side_own, side_other, side_lse, down, prior, low = side_saved[layer]
        djoined, dq, dkv_own, dkv_other, sums_a = side_back(
            layer, place, grad_side, joined, side_mixed, *weights, spread_sel, side_q, side_own, side_other, table,
            side_lse,
        )
        dkv_got = flipped(dkv_other)
        ddowns[layer], grad_side, sums_b = side_end(
            layer, joined, djoined, dq, dkv_own, dkv_got, gate_logit, side_gain1, down, prior,
            back_query, back_kv, compact_sel, low,
        )
        sums[layer] = (sums_a, sums_b)
    summed = sum_gradients(sums[0] + sums[1])

    def to_all(rows):
        partner = flipped(rows)
        sequence = jnp.where(core == 0, jnp.concatenate([rows, partner]), jnp.concatenate([partner, rows]))
        far, after, before = (lax.ppermute(sequence, "tp", [(n, (n + d) % TP) for n in range(TP)]) for d in (2, 1, 3))
        turn = lax.rem(x + TP - core, TP)
        low = jnp.where(turn == 0, sequence, jnp.where(turn == 1, after, jnp.where(turn == 2, far, before)))
        high = jnp.where(turn == 0, far, jnp.where(turn == 1, before, jnp.where(turn == 2, sequence, after)))
        return jnp.concatenate([low, high])

    side_out = to_all(side_out)
    grad_start = to_all(grad_side)

    grad = jnp.zeros((8, 128), F32)
    for layer in (1, 0):
        b, q, own, other, lse, mid, slope = saved[layer]
        gmid, dmixed = feed_back(
            layer, grad, ddowns[layer], narrowing_weight, mid, gain_ffn, slope, all_outer, all_inner, all_out
        )
        dq, dkv_own, dkv_other = attend_back(q, own, other, table, lse, dmixed)
        dkv_got = flipped(dkv_other)
        grad = project_back(
            layer, dq, dkv_own, dkv_got, all_qkv, b, gain_attn, gmid, F32 if layer == 1 else BF
        )
    grad_inputs = moved(grad).astype(F32)
    return (backbone_out, side_out, grad_inputs, grad_start) + tuple(summed)


def solution(mesh):
    in_specs = (
        P(("batch", "tp"), None),
        P("batch", None),
        P("batch"),
        P(),
        P(),
        P(None, None, "tp"),
        P(None, None, "tp"),
        P(None, None, "tp"),
        P(None, "tp", None),
        P(),
        P(None, None, "tp"),
        P(None, "tp", None),
        P(),
        P(),
        P(),
        P(),
        P(),
        P(),
        P(),
        P(),
        P("batch", None),
    )
    out_specs = (
        P(("batch", "tp"), None),
        P("batch", None),
        P(("batch", "tp"), None),
        P("batch", None),
        P(),
        P(),
        P(),
        P(),
        P(),
        P(),
        P(),
        P(),
    )
    return jax.shard_map(per_device, mesh=mesh, in_specs=in_specs, out_specs=out_specs, check_vma=False)
```

```python
from functools import partial
import math

import jax
import jax.numpy as jnp
from jax import lax
from jax.experimental import pallas as pl
from jax.experimental.pallas import tpu as pltpu
from jax.sharding import PartitionSpec as P


BF = jnp.bfloat16
F32 = jnp.float32
EPSILON = 1e-06
NEGATIVE = -1e30
HIGHEST = lax.Precision.HIGHEST
MESH = pl.DeviceIdType.MESH
TP = 4
SIDES = 4
HALF = 256
WIDTH = 768
SIDE_W = 96
SIDE_FF = 384
SIDE_SCALE = 1.0 / math.sqrt(8)
GELU_K = math.sqrt(2.0 / math.pi)
VMEM_BYTES = 63 * 1024 * 1024

A_PROJ, A_INNER, A_OUTER, A_SMALL, A_ROWS = 0, 96, 384, 672, 688
B_QKV, B_DOWN, B_SMALL, B_ROWS = 0, 288, 864, 880
LAYER_ROWS = A_ROWS + B_ROWS
SUM_ROWS = 3584


def dot(a, b, ca, cb, precision=None):
    return lax.dot_general(
        a, b, (((ca,), (cb,)), ((), ())), preferred_element_type=F32, precision=precision
    )


def nn(a, b, precision=None):
    return dot(a, b, 1, 0, precision)


def nt(a, b, precision=None):
    return dot(a, b, 1, 1, precision)


def tn(a, b, precision=None):
    return dot(a, b, 0, 0, precision)


def rms_scale(values):
    return lax.rsqrt(jnp.mean(values * values, axis=-1, keepdims=True) + EPSILON)


def rms_back(values, gain_row, grad):
    scale = rms_scale(values)
    scaled = grad * gain_row
    inner = jnp.mean(scaled * values, axis=-1, keepdims=True)
    return scale * scaled - values * (scale * scale * scale * inner)


def gelu_parts(hidden):
    square = hidden * hidden
    tanh = jnp.tanh(GELU_K * hidden * (1.0 + 0.044715 * square))
    plus = 0.5 * (1.0 + tanh)
    slope = plus + (0.5 * GELU_K) * hidden * (1.0 - tanh * tanh) * (1.0 + (3 * 0.044715) * square)
    return hidden * plus, slope


def lane_mask(test):
    lanes = lax.broadcasted_iota(jnp.int32, (HALF, 128), 1)
    return jnp.where(test(lanes), 1.0, 0.0).astype(BF)


def row_block(shape, index_map):
    return pl.BlockSpec(shape, index_map)


def whole(shape):
    return pl.BlockSpec(shape, lambda *_: (0,) * len(shape))


def call(kernel, grid, in_specs, out_specs, out_shape, scratch=(), prefetch=0, flops=0, nbytes=0):
    return pl.pallas_call(
        kernel,
        grid_spec=pltpu.PrefetchScalarGridSpec(
            num_scalar_prefetch=prefetch,
            grid=grid,
            in_specs=in_specs,
            out_specs=out_specs,
            scratch_shapes=scratch,
        ),
        out_shape=out_shape,
        compiler_params=pltpu.CompilerParams(vmem_limit_bytes=VMEM_BYTES),
        cost_estimate=pl.CostEstimate(flops=flops, bytes_accessed=nbytes, transcendentals=0),
    )


def shape(dims, dtype):
    return jax.ShapeDtypeStruct(dims, dtype)


def unpack_kernel(total, down_out, gate_out, gain1_out, qkv_out, proj_out, gain2_out, inner_out, outer_out):
    for layer in range(2):
        base = layer * LAYER_ROWS

        def part(start, count, base=base):
            return total[base + start : base + start + count].astype(F32)

        proj_out[layer] = part(A_PROJ, 96)[:, :SIDE_W]
        for n in range(3):
            inner_out[layer, :, n * 128 : (n + 1) * 128] = part(A_INNER + n * 96, 96)
            outer_out[layer, :, n * 128 : (n + 1) * 128] = part(A_OUTER + n * 96, 96)
        triple = [part(A_ROWS + B_QKV + n * 96, 96)[:, :SIDE_W] for n in range(3)]
        qkv_out[layer] = jnp.concatenate(triple, axis=1)
        for n in range(6):
            down_out[layer, :, n * 128 : (n + 1) * 128] = part(A_ROWS + B_DOWN + n * 96, 96)
        gain2_out[layer : layer + 1] = part(A_SMALL, 16)[0:1, :SIDE_W]
        rest = part(A_ROWS + B_SMALL, 16)
        gate_out[layer : layer + 1] = rest[0:1, :SIDE_W]
        gain1_out[layer : layer + 1] = rest[1:2, :SIDE_W]


def head_parts(q, dm=None):
    low = lane_mask(lambda lanes: lanes < 64)
    high = lane_mask(lambda lanes: lanes >= 64)
    queries = [q[:, :128] * low, q[:, :128] * high, q[:, 128:]]
    if dm is None:
        return queries
    return queries, [dm[:, :128] * low, dm[:, :128] * high, dm[:, 128:]]


def softmax_parts(scores):
    top = jnp.max(scores, axis=0, keepdims=True)
    exps = jnp.exp(scores - top)
    total = jnp.sum(exps, axis=0, keepdims=True)
    return exps.astype(BF), 1.0 / total, top + jnp.log(total)


def score_gradients(scores, lse, dprobs):
    probs = jnp.exp(scores - lse)
    inner = jnp.sum(probs * dprobs, axis=0, keepdims=True)
    return probs.astype(BF), (probs * (dprobs - inner)).astype(BF)


def split_pack(values, low_test):
    high = values.astype(BF)
    low = (values - high.astype(F32)).astype(BF)
    mask = lane_mask(low_test)
    return high * (1 - mask) + low * mask


def of_head(j, blocks):
    def test(lanes):
        hit = (lanes >= blocks[0] * 24 + j * 8) & (lanes < blocks[0] * 24 + j * 8 + 8)
        for n in blocks[1:]:
            hit = hit | ((lanes >= n * 24 + j * 8) & (lanes < n * 24 + j * 8 + 8))
        return hit

    return lane_mask(test)


def transposed(rows):
    return jnp.concatenate([rows, jnp.zeros((32, rows.shape[1]), rows.dtype)], axis=0).T[:, :SIDE_W]


INPUTS = [
    "inputs", "side_start", "side_cotangent", "lengths", "bias", "gain_attn", "gain_ffn", "w_query", "w_key", "w_value",
    "w_inner", "w_outer", "w_out", "narrow", "gate", "gain1", "gain2", "side_qkv", "proj", "side_inner", "side_outer",
]
FAR = {"inputs", "side_start", "side_cotangent", "w_query", "w_key", "w_value", "w_inner", "w_outer", "w_out"}

OUTPUTS = {
    "backbone_out": ((HALF, WIDTH), BF, True),
    "side_out": ((SIDE_W, 4 * HALF), F32, True),
    "grad_start": ((SIDE_W, 4 * HALF), F32, True),
    "grad": ((HALF, WIDTH), BF, True),
    "total": ((SUM_ROWS, 128), BF, False),
}

BUFFERS = {
    "qkv": ((2, TP, 640, WIDTH), BF),
    "inner": ((2, TP, WIDTH, WIDTH), BF),
    "outer": ((2, TP, WIDTH, WIDTH), BF),
    "out": ((2, TP, 192, WIDTH), BF),
    "tokens": ((HALF, WIDTH), BF),
    "start_own": ((SIDE_W, HALF), F32),
    "start_got": ((SIDE_W, HALF), F32),
    "cot_own": ((SIDE_W, HALF), F32),
    "cot_got": ((SIDE_W, HALF), F32),
    "span_own": ((8, HALF), F32),
    "span_got": ((8, HALF), F32),
    "wide_bias": ((16, 4 * HALF), BF),
    "wide_query": ((2, SIDE_W, 512), F32),
    "wide_kv": ((2, SIDE_W, 512), F32),
    "back_query": ((2, SIDE_W, SIDE_W), BF),
    "back_kv": ((2, SIDE_W, 256), BF),
    "spread": ((SIDE_W, 512), BF),
    "compact": ((512, 256), BF),
    "table": ((12, 2 * HALF, HALF), BF),
    "base": ((16, 2, 2 * HALF), F32),
    "q": ((2, TP, HALF, 256), BF),
    "kv": ((2, TP, 2, HALF, 384), BF),
    "lse": ((2, TP, 8, HALF), F32),
    "mid": ((2, HALF, WIDTH), F32),
    "slope": ((2, TP, HALF, WIDTH), BF),
    "residual": ((HALF, WIDTH), F32),
    "low": ((2, HALF, WIDTH), BF),
    "down": ((2, HALF, SIDE_W), BF),
    "state": ((3, HALF, SIDE_W), F32),
    "joined": ((2, HALF, SIDE_W), F32),
    "side_mixed": ((2, HALF, SIDE_W), F32),
    "side_q": ((2, 4, HALF, 128), BF),
    "side_kv": ((2, 4, 2, HALF, 128), BF),
    "side_lse": ((2, 4, 8, HALF), F32),
    "normed": ((HALF, WIDTH), BF),
    "acc": ((HALF, WIDTH), F32),
    "grad_side": ((3, HALF, SIDE_W), F32),
    "djoined": ((HALF, SIDE_W), F32),
    "side_dmixed": ((4, HALF, 128), BF),
    "side_dq": ((SIDE_W, HALF), F32),
    "side_dkv": ((4, HALF, 128), F32),
    "side_dkv_sent": ((4, HALF, 128), BF),
    "side_dkv_got": ((2, 4, HALF, 128), BF),
    "ddown": ((2, HALF, SIDE_W), BF),
    "upper": ((HALF, WIDTH), F32),
    "dmixed": ((TP, HALF, 256), BF),
    "dq": ((TP, HALF, 256), BF),
    "dkv": ((TP, HALF, 384), F32),
    "dkv_sent": ((TP, HALF, 384), BF),
    "dkv_got": ((2, TP, HALF, 384), BF),
    "packed": ((SUM_ROWS, 128), BF),
    "half_sum": ((SUM_ROWS // 2, 128), BF),
    "from_x": ((3, SUM_ROWS // 8, 128), BF),
    "piece": ((SUM_ROWS // 8, 128), BF),
    "from_y": ((3, SUM_ROWS // 32, 128), BF),
    "small": ((SUM_ROWS // 32, 128), BF),
    "from_z": ((4, SUM_ROWS // 32, 128), BF),
}

SEMAPHORES = {
    "load": (12,),
    "early_s": (4,),
    "early_r": (4,),
    "x_s": (6, 6),
    "x_r": (6, 6),
    "yz_s": (6, 12),
    "yz_r": (6, 12),
    "core_s": (6,),
    "core_r": (6,),
    "out_s": (10,),
    "out_r": (10,),
    "kv_s": (2, TP),
    "kv_r": (2, TP),
    "side_kv_s": (2, 4),
    "side_kv_r": (2, 4),
    "dkv_s": (2, TP),
    "dkv_r": (2, TP),
    "side_dkv_s": (2, 4),
    "side_dkv_r": (2, 4),
    "sum_s": (17,),
    "sum_r": (17,),
    "all_s": (2, 4),
    "all_r": (2, 4),
    "all_own": (2,),
    "back_s": (2,),
    "back_r": (2,),
    "back_own": (2,),
}


class Refs:
    def __init__(self, names, refs):
        self.__dict__.update(zip(names, refs))


def rows(start, count):
    return pl.ds(pl.multiple_of(start, 16), count)


def network_kernel(*refs):
    r = Refs(INPUTS + list(OUTPUTS) + list(BUFFERS) + list(SEMAPHORES), refs)
    x = lax.axis_index("tp")
    b = lax.axis_index("batch")
    c = lax.rem(b, 2)
    z = lax.rem(b // 2, SIDES)
    y = b // (2 * SIDES)
    parity = lax.rem(x, 2)
    stays = parity == c
    sequence = lax.div(x, 2)

    def chip(y_now, z_now, c_now):
        return (y_now * SIDES + z_now) * 2 + c_now

    left, right = {"tp": lax.rem(x + TP - 1, TP)}, {"tp": lax.rem(x + 1, TP)}
    x_devices = [{"tp": lax.rem(x + d, TP)} for d in (1, 2, 3)]
    y_devices = [{"batch": chip(lax.rem(y + d, SIDES), z, c)} for d in (1, 2, 3)]
    z_devices = [{"batch": chip(y, lax.rem(z + d, SIDES), c)} for d in (1, 2, 3)]
    up, down = (y_devices[0], z_devices[0]), (y_devices[2], z_devices[2])
    partner = {"batch": chip(y, z, 1 - c)}
    across = {"tp": x + 1 - 2 * parity, "batch": chip(y, z, 1 - c)}

    pending = []

    def remote(src, dst, send_sem, recv_sem, device):
        return pltpu.make_async_remote_copy(
            src_ref=src, dst_ref=dst, send_sem=send_sem, recv_sem=recv_sem, device_id=device, device_id_type=MESH
        )

    def start(copies):
        for copy in copies:
            copy.start()
            pending.append(copy.wait_send)
        return copies

    def arrived(copies):
        for copy in copies:
            copy.wait_recv()

    def load(n, source, target):
        copy = pltpu.make_async_copy(source, target, r.load.at[n])
        copy.start()
        return copy

    own_lanes = pl.ds(pl.multiple_of(sequence * (2 * HALF) + c * HALF, HALF), HALF)
    sent_lanes = pl.ds(pl.multiple_of(sequence * (2 * HALF) + (1 - c) * HALF, HALF), HALF)
    qkv_loads = [
        load(n, source.at[:, low:high], r.qkv.at[:, 0, place : place + high - low])
        for n, (source, low, high, place) in enumerate((
            (r.w_query, 0, 128, 0),
            (r.w_key, 0, 128, 128),
            (r.w_value, 0, 128, 256),
            (r.w_key, 128, 192, 384),
            (r.w_value, 128, 192, 448),
            (r.w_query, 128, 192, 512),
        ))
    ]
    side_loads = [
        load(6, r.side_start.at[:, own_lanes], r.start_own),
        load(7, r.side_cotangent.at[:, own_lanes], r.cot_own),
    ]
    weight_loads = [
        load(8, r.w_out, r.out.at[:, 0]),
        load(9, r.w_inner, r.inner.at[:, 0]),
        load(10, r.w_outer, r.outer.at[:, 0]),
    ]
    r.span_own[...] = jnp.full((8, HALF), r.lengths[sequence].astype(F32))
    r.qkv[:, :, 576:] = jnp.zeros((2, TP, 64, WIDTH), BF)

    barrier = pltpu.get_barrier_semaphore()
    line = [{"tp": lax.rem(x + d, TP), "batch": chip(y, z, core)} for d in (1, 2, 3) for core in (0, 1)]
    for device in [partner] + line + y_devices + z_devices:
        pl.semaphore_signal(barrier, inc=1, device_id=device, device_id_type=MESH)
    pl.semaphore_wait(barrier, 13)

    chunks = [chunk for layer in range(2) for chunk in ((r.qkv, layer), (r.inner, layer), (r.outer, layer))]

    def place(k):
        core_rows = 256 if k % 3 == 0 else 384
        low = c * core_rows
        part = core_rows // 8
        return (
            rows(low, core_rows),
            (rows(low + y * part, part), rows(low + core_rows // 2 + z * part, part)),
        )

    direct = {"W": (r.out, 192, 0, 0), "Q": (r.qkv, 64, 512, 5)}
    flying = {}

    def first(k):
        target, layer = chunks[k]
        _, blocks = place(k)
        return [
            remote(
                target.at[layer, 0, blocks[path]],
                target.at[layer, slot, blocks[path]],
                r.x_s.at[k, path * 2 + slot - 1],
                r.x_r.at[k, path * 2 + slot - 1],
                device,
            )
            for path in range(2)
            for device, slot in ((right, 2), (left, 1))
        ]

    def relay(k):
        target, layer = chunks[k]
        _, (y_block, z_block) = place(k)
        return [
            remote(target.at[layer, 2, y_block], target.at[layer, 3, y_block], r.x_s.at[k, 4], r.x_r.at[k, 4], right),
            remote(target.at[layer, 1, z_block], target.at[layer, 3, z_block], r.x_s.at[k, 5], r.x_r.at[k, 5], left),
        ]

    def spread(k, part):
        target, layer = chunks[k]
        _, blocks = place(k)
        slots = pl.ds(1, 2) if part == 0 else pl.ds(3, 1)
        out = []
        for path in range(2):
            block = target.at[layer, slots, blocks[path]]
            for way, device in enumerate((up[path], down[path])):
                n = part * 4 + path * 2 + way
                out.append(remote(block, block, r.yz_s.at[k, n], r.yz_r.at[k, n], device))
        return out

    def spread_relay(k):
        target, layer = chunks[k]
        out = []
        for path in range(2):
            part = 32 if k % 3 == 0 else 48
            cut = 32 if part == 48 and (k + path) % 2 == 0 else 16
            for n, (step, device, low, high) in enumerate(
                ((SIDES - 1, up[path], 0, cut), (1, down[path], cut, part))
            ):
                start_row = c * part * 8 + path * part * 4 + lax.rem((y, z)[path] + step, SIDES) * part
                block = target.at[layer, pl.ds(1, 3), rows(start_row + low, high - low)]
                m = 8 + path * 2 + n
                out.append(remote(block, block, r.yz_s.at[k, m], r.yz_r.at[k, m], device))
        return out

    def swap(k):
        target, layer = chunks[k]
        mine, _ = place(k)
        block = target.at[layer, pl.ds(1, 3), mine]
        return [remote(block, block, r.core_s.at[k], r.core_r.at[k], partner)]

    def straight(kind, step):
        target, count, base, sem = direct[kind]
        base = base + c * (count // 2)
        mine, low, high = rows(base, count // 2), rows(base, count // 4), rows(base + count // 4, count // 4)

        def go(n, source_slot, target_slot, block, device):
            return remote(
                target.at[:, source_slot, block], target.at[:, target_slot, block],
                r.out_s.at[sem + n], r.out_r.at[sem + n], device,
            )

        if step == "A":
            return [go(0, 0, 2, mine, right), go(1, 0, 1, mine, left)]
        if step == "B":
            return [go(2, 2, 3, low, right), go(3, 1, 3, high, left)]
        return [go(4, pl.ds(1, 3), pl.ds(1, 3), mine, partner)]

    def gather(steps):
        for step in steps.split():
            kind, k = step[0], step[1:]
            if kind in direct:
                if k != "A":
                    arrived(flying[kind])
                flying[kind] = start(straight(kind, k)) if k != "F" else []
                continue
            k = int(k)
            if kind == "A":
                flying["A", k] = start(first(k))
            elif kind == "B":
                arrived(flying["A", k])
                flying["B", k] = start(relay(k))
                flying["S", k] = start(spread(k, 0))
            elif kind == "C":
                arrived(flying["B", k])
                flying["S", k] += start(spread(k, 1))
            elif kind == "D":
                arrived(flying["S", k])
                flying["D", k] = start(spread_relay(k))
            elif kind == "E":
                arrived(flying["D", k])
                flying["E", k] = start(swap(k))
            else:
                arrived(flying["E", k])

    early = [
        remote(r.span_own, r.span_got, r.early_s.at[0], r.early_r.at[0], partner),
        remote(r.side_start.at[:, sent_lanes], r.start_got, r.early_s.at[1], r.early_r.at[1], partner),
        remote(r.side_cotangent.at[:, sent_lanes], r.cot_got, r.early_s.at[2], r.early_r.at[2], partner),
    ]
    tokens_here = pltpu.make_async_copy(r.inputs, r.tokens, r.load.at[11])
    tokens_over = remote(r.inputs, r.tokens, r.early_s.at[3], r.early_r.at[3], across)

    for copy in qkv_loads:
        copy.wait()
    gather("A0")
    gather("QA")
    for copy in weight_loads:
        copy.wait()
    gather("A1")
    start(early)

    @pl.when(stays)
    def _():
        tokens_here.start()

    @pl.when(jnp.logical_not(stays))
    def _():
        tokens_over.start()

    def table_slot(shard):
        turn = lax.rem(shard + TP - x, TP)
        return turn + jnp.where(turn == 2, 1, 0) - jnp.where(turn == 3, 1, 0)

    def make_base():
        row = lax.broadcasted_iota(jnp.int32, (HALF, HALF), 0)
        column = lax.broadcasted_iota(jnp.int32, (HALF, HALF), 1)
        reverse = jnp.where(row + column == HALF - 1, 1.0, 0.0).astype(BF)
        r.wide_bias[...] = jnp.zeros_like(r.wide_bias)
        r.wide_bias[:12, : 4 * HALF - 1] = r.bias[...]
        turned = [nn(r.wide_bias[:, n * HALF : (n + 1) * HALF], reverse) for n in range(4)]
        r.base[:, 0, :HALF] = turned[1]
        r.base[:, 0, HALF:] = turned[2]
        r.base[:, 1, :HALF] = jnp.where(c == 0, turned[2], turned[0])
        r.base[:, 1, HALF:] = jnp.where(c == 0, turned[3], turned[1])

    def make_table(low, high):
        row = lax.broadcasted_iota(jnp.int32, (HALF, HALF), 0)
        length = jnp.where(stays, r.span_own[0:1], r.span_got[0:1])
        place = row.astype(F32)

        def one(head, carry):
            slot = table_slot(lax.div(head, 3)) * 3 + lax.rem(head, 3)
            for side in range(2):
                first_key = (c if side == 0 else 1 - c) * HALF
                spread_row = jnp.broadcast_to(r.base[head, side : side + 1], (HALF, 2 * HALF))
                rolled = pltpu.roll(spread_row, 0, 1, stride=1, stride_axis=0)[:, :HALF]
                counts = place + first_key.astype(F32) < length
                r.table[slot, side * HALF : (side + 1) * HALF] = jnp.where(counts, rolled, NEGATIVE).astype(BF)
            return carry

        lax.fori_loop(low, high, one, 0)

    def lay_out_side():
        row = lax.broadcasted_iota(jnp.int32, (SIDE_W, 128), 0)
        lane = lax.broadcasted_iota(jnp.int32, (SIDE_W, 128), 1)
        wide_row = lax.broadcasted_iota(jnp.int32, (128, 128), 0)
        wide_lane = lax.broadcasted_iota(jnp.int32, (128, 128), 1)

        def ones(test):
            return jnp.where(test, 1.0, 0.0)

        thrice = lane - jnp.where(lane >= 24, 24, 0) - jnp.where(lane >= 48, 24, 0)
        twice = lane - 72 - jnp.where(lane >= 96, 24, 0)
        for g in range(4):
            lanes = slice(g * 128, (g + 1) * 128)
            to_keys = ones((row == thrice + g * 24) & (lane < 72))
            to_values = ones((row == twice + g * 24) & (lane >= 72) & (lane < 120))
            r.spread[:, lanes] = to_values.astype(BF)
            r.compact[lanes, :128] = ones((wide_row < 24) & (wide_lane == wide_row + g * 24)).astype(BF)
            r.compact[lanes, 128:] = ones(
                (wide_row >= 72) & (wide_row < 96) & (wide_lane == wide_row - 72 + g * 24)
            ).astype(BF)
            for layer in range(2):
                weight = r.side_qkv[layer]
                query, key, value = weight[:, :96], weight[:, 96:192], weight[:, 192:]
                r.wide_query[layer, :, lanes] = nn(query, to_keys, HIGHEST) * SIDE_SCALE
                r.wide_kv[layer, :, lanes] = nn(key, to_keys, HIGHEST) + nn(value, to_values, HIGHEST)
        for layer in range(2):
            weight = r.side_qkv[layer]
            r.back_query[layer] = (weight[:, :96] * SIDE_SCALE).astype(BF)
            r.back_kv[layer] = jnp.zeros((SIDE_W, 256), BF)
            r.back_kv[layer, :, :96] = weight[:, 96:192].astype(BF)
            r.back_kv[layer, :, 128:224] = weight[:, 192:].astype(BF)

    def project(layer, residual):
        r.normed[...] = (residual * rms_scale(residual) * r.gain_attn[layer : layer + 1].astype(F32)).astype(BF)

        def one(s, carry):
            out = nt(r.normed[...], r.qkv[layer, s])
            r.kv[layer, s, 0] = out[:, 128:512].astype(BF)
            kv_copy(layer, s).start()
            r.q[layer, s, :, :128] = (out[:, :128] * 0.125).astype(BF)
            r.q[layer, s, :, 128:] = (out[:, 512:] * 0.125).astype(BF)
            return carry

        lax.fori_loop(0, TP, one, 0)
        pending.append(lambda: wait_sends(lambda s: kv_copy(layer, s)))

    def kv_copy(layer, s):
        return remote(r.kv.at[layer, s, 0], r.kv.at[layer, s, 1], r.kv_s.at[layer, s], r.kv_r.at[layer, s], partner)

    def wait_sends(copy_of):
        def one(s, carry):
            copy_of(s).wait_send()
            return carry

        lax.fori_loop(0, 4, one, 0)

    def slab(layer, s, n):
        return r.kv[layer, s, :, :, n * 128 : (n + 1) * 128].reshape(2 * HALF, 128)

    def attend(layer):
        def one(s, carry):
            kv_copy(layer, s).wait_recv()
            queries = head_parts(r.q[layer, s])
            keys, values = [slab(layer, s, 0), slab(layer, s, 2)], [slab(layer, s, 1), slab(layer, s, 2)]
            scores = [nt(keys[j // 2], queries[j]) + r.table[s * 3 + j].astype(F32) for j in range(3)]
            parts = [softmax_parts(score) for score in scores]
            heads = [tn(values[j // 2], parts[j][0]) for j in range(3)]
            heads = [(heads[j][:64] if j == 0 else heads[j][64:]) * parts[j][1] for j in range(3)]
            for j in range(3):
                r.lse[layer, s, j : j + 1] = parts[j][2]
            r.dq[s, :, :128] = jnp.concatenate(heads[:2], axis=0).T.astype(BF)
            third = jnp.concatenate([heads[2], jnp.zeros_like(heads[2])], axis=0).T
            r.dq[s, :, 128:192] = third[:, :64].astype(BF)
            return carry

        lax.fori_loop(0, TP, one, 0)

    def feed(layer, residual):
        middle = residual
        for s in range(TP):
            middle = middle + nn(r.dq[s, :, :192], r.out[layer, s])
        r.mid[layer] = middle
        r.acc[...] = middle
        r.normed[...] = (middle * rms_scale(middle) * r.gain_ffn[layer : layer + 1].astype(F32)).astype(BF)

        def one(s, carry):
            active, slope = gelu_parts(nn(r.normed[...], r.inner[layer, s]))
            r.slope[layer, s] = slope.astype(BF)
            r.acc[...] += nn(active.astype(BF), r.outer[layer, s])
            return carry

        lax.fori_loop(0, TP, one, 0)
        out = r.acc[...]
        low = out.astype(BF)
        if layer == 0:
            r.residual[...] = out
        r.low[layer] = low
        r.down[layer] = nt(low, r.narrow[layer]).astype(BF)

    def side_kv_copy(layer, g):
        return remote(
            r.side_kv.at[layer, g, 0], r.side_kv.at[layer, g, 1],
            r.side_kv_s.at[layer, g], r.side_kv_r.at[layer, g], partner,
        )

    def side_begin(layer):
        mix = jax.nn.sigmoid(r.gate[layer : layer + 1])
        joined = mix * r.down[layer].astype(F32) + (1.0 - mix) * r.state[layer]
        r.joined[layer] = joined
        normed = joined * rms_scale(joined) * r.gain1[layer : layer + 1]
        kv = nn(normed, r.wide_kv[layer], HIGHEST)
        for g in range(4):
            r.side_kv[layer, g, 0] = split_pack(
                kv[:, g * 128 : (g + 1) * 128], lambda n: ((n >= 48) & (n < 72)) | (n >= 96)
            )
            side_kv_copy(layer, g).start()
        q = nn(normed, r.wide_query[layer], HIGHEST)
        for g in range(4):
            r.side_q[layer, g] = split_pack(q[:, g * 128 : (g + 1) * 128], lambda n: (n >= 24) & (n < 48))
        pending.append(lambda: wait_sends(lambda g: side_kv_copy(layer, g)))

    def side_attend(layer):
        def one(g, carry):
            side_kv_copy(layer, g).wait_recv()
            kv = r.side_kv[layer, g].reshape(2 * HALF, 128)
            q = r.side_q[layer, g]
            slot = table_slot(g) * 3
            scores = [nt(kv, q * of_head(j, (0, 1, 2))) + r.table[slot + j].astype(F32) for j in range(3)]
            parts = [softmax_parts(score) for score in scores]
            heads = [tn(kv, parts[j][0]) for j in range(3)]
            for j in range(3):
                both = heads[j][72 + j * 8 : 80 + j * 8] + heads[j][96 + j * 8 : 104 + j * 8]
                r.side_dq[pl.ds(pl.multiple_of(g * 24 + j * 8, 8), 8)] = both * parts[j][1]
                r.side_lse[layer, g, j : j + 1] = parts[j][2]
            return carry

        lax.fori_loop(0, 4, one, 0)
        mixed = transposed(r.side_dq[...])
        r.side_mixed[layer] = mixed
        joined = r.joined[layer] + nn(mixed, r.proj[layer], HIGHEST)
        normed = joined * rms_scale(joined) * r.gain2[layer : layer + 1]
        active, _ = gelu_parts(nn(normed, r.side_inner[layer], HIGHEST))
        r.state[layer + 1] = joined + nt(active, r.side_outer[layer], HIGHEST)

    def side_dkv_copy(layer, g):
        return remote(
            r.side_dkv_sent.at[g], r.side_dkv_got.at[layer, g],
            r.side_dkv_s.at[layer, g], r.side_dkv_r.at[layer, g], partner,
        )

    def side_back(layer):
        base = layer * LAYER_ROWS
        grad = r.grad_side[layer + 1]
        grad_low = grad.astype(BF)
        mixed = r.side_mixed[layer]
        gain = r.gain2[layer : layer + 1]
        joined = r.joined[layer] + nn(mixed, r.proj[layer], HIGHEST)
        unit = joined * rms_scale(joined)
        normed = unit * gain
        active, slope = gelu_parts(nn(normed, r.side_inner[layer], HIGHEST))
        dhidden = (nn(grad_low, r.side_outer[layer].astype(BF)) * slope).astype(BF)
        dnormed = nt(dhidden, r.side_inner[layer].astype(BF))
        djoined = grad + rms_back(joined, gain, dnormed)
        r.djoined[...] = djoined
        djoined_low = djoined.astype(BF)
        dmixed_low = nt(djoined_low, r.proj[layer].astype(BF)).astype(BF)
        for g in range(4):
            r.side_dmixed[g] = nn(dmixed_low, r.spread[:, g * 128 : (g + 1) * 128]).astype(BF)
        r.packed[base + A_PROJ : base + A_PROJ + SIDE_W, :SIDE_W] = tn(mixed.astype(BF), djoined_low).astype(BF)
        inner_sum = tn(normed.astype(BF), dhidden).astype(BF)
        outer_sum = tn(grad_low, active.astype(BF)).astype(BF)
        for n in range(3):
            lanes = slice(n * 128, (n + 1) * 128)
            r.packed[base + A_INNER + n * 96 : base + A_INNER + (n + 1) * 96] = inner_sum[:, lanes]
            r.packed[base + A_OUTER + n * 96 : base + A_OUTER + (n + 1) * 96] = outer_sum[:, lanes]
        gain_sum = jnp.sum(dnormed * unit, axis=0, keepdims=True)
        r.packed[base + A_SMALL : base + A_ROWS, :SIDE_W] = jnp.broadcast_to(gain_sum, (16, SIDE_W)).astype(BF)

        if layer == 0:
            wait_sends(lambda g: side_dkv_copy(1, g))

        def one(g, carry):
            kv = r.side_kv[layer, g].reshape(2 * HALF, 128)
            q, dm = r.side_q[layer, g], r.side_dmixed[g]
            slot = table_slot(g) * 3
            scores = [nt(kv, q * of_head(j, (0, 1, 2))) + r.table[slot + j].astype(F32) for j in range(3)]
            dprobs = [nt(kv, dm * of_head(j, (3, 4))) for j in range(3)]
            left, right_parts = [], []
            for j in range(3):
                p, ds = score_gradients(scores[j], r.side_lse[layer, g, j : j + 1], dprobs[j])
                dq = tn(kv, ds)
                r.side_dq[pl.ds(pl.multiple_of(g * 24 + j * 8, 8), 8)] = (
                    dq[j * 8 : j * 8 + 8] + dq[48 + j * 8 : 56 + j * 8]
                )
                left += [ds, p]
                right_parts += [q * of_head(j, (0,)), dm * of_head(j, (3,))]
            dkv = nn(jnp.concatenate(left, axis=1), jnp.concatenate(right_parts, axis=0))
            r.side_dkv_sent[g] = dkv[HALF:].astype(BF)
            side_dkv_copy(layer, g).start()
            r.side_dkv[g] = dkv[:HALF]
            return carry

        lax.fori_loop(0, 4, one, 0)
        if layer == 0:
            pending.append(lambda: wait_sends(lambda g: side_dkv_copy(layer, g)))

    def side_end(layer):
        base = layer * LAYER_ROWS + A_ROWS
        joined = r.joined[layer]
        gain = r.gain1[layer : layer + 1]
        unit = joined * rms_scale(joined)
        normed_low = (unit * gain).astype(BF)
        dq = transposed(r.side_dq[...]).astype(BF)
        dkv = jnp.zeros((HALF, 256), F32)
        for g in range(4):
            side_dkv_copy(layer, g).wait_recv()
            both = (r.side_dkv[g] + r.side_dkv_got[layer, g].astype(F32)).astype(BF)
            dkv = dkv + nn(both, r.compact[g * 128 : (g + 1) * 128])
        dkv = dkv.astype(BF)
        dnormed = nt(dq, r.back_query[layer]) + nt(dkv, r.back_kv[layer])
        djoined = r.djoined[...] + rms_back(joined, gain, dnormed)
        mix = jax.nn.sigmoid(r.gate[layer : layer + 1])
        ddown = (mix * djoined).astype(BF)
        r.ddown[layer] = ddown
        r.grad_side[layer] = (1.0 - mix) * djoined
        change = r.down[layer].astype(F32) - r.state[layer]
        gate_sum = jnp.sum(djoined * change, axis=0, keepdims=True) * mix * (1.0 - mix)
        gain_sum = jnp.sum(dnormed * unit, axis=0, keepdims=True)
        r.packed[base + B_QKV : base + B_QKV + 96, :SIDE_W] = (tn(normed_low, dq) * SIDE_SCALE).astype(BF)
        kv_sum = tn(normed_low, dkv).astype(BF)
        r.packed[base + B_QKV + 96 : base + B_QKV + 192] = kv_sum[:, :128]
        r.packed[base + B_QKV + 192 : base + B_QKV + 288] = kv_sum[:, 128:]
        down_sum = tn(ddown, r.low[layer]).astype(BF)
        for n in range(6):
            r.packed[base + B_DOWN + n * 96 : base + B_DOWN + (n + 1) * 96] = down_sum[:, n * 128 : (n + 1) * 128]
        row = lax.broadcasted_iota(jnp.int32, (16, SIDE_W), 0)
        r.packed[base + B_SMALL : base + B_ROWS, :SIDE_W] = jnp.where(row == 0, gate_sum, gain_sum).astype(BF)

    def feed_back(layer):
        upper = nn(r.ddown[layer], r.narrow[layer])
        if layer == 0:
            upper = upper + r.upper[...]
        r.upper[...] = upper
        r.normed[...] = upper.astype(BF)
        r.acc[...] = jnp.zeros_like(r.acc)

        def one(s, carry):
            dactive = nt(r.normed[...], r.outer[layer, s])
            dhidden = (dactive * r.slope[layer, s].astype(F32)).astype(BF)
            r.acc[...] += nt(dhidden, r.inner[layer, s])
            return carry

        lax.fori_loop(0, TP, one, 0)
        middle = r.upper[...] + rms_back(r.mid[layer], r.gain_ffn[layer : layer + 1].astype(F32), r.acc[...])
        r.upper[...] = middle
        low = middle.astype(BF)
        for s in range(TP):
            r.dmixed[s, :, :128] = nt(low, r.out[layer, s, :128]).astype(BF)
            third = jnp.concatenate([jnp.zeros((64, WIDTH), BF), r.out[layer, s, 128:]], axis=0)
            r.dmixed[s, :, 128:] = nt(low, third).astype(BF)

    def dkv_copy(layer, s):
        return remote(
            r.dkv_sent.at[s], r.dkv_got.at[layer, s], r.dkv_s.at[layer, s], r.dkv_r.at[layer, s], partner
        )

    def attend_back(layer):
        if layer == 0:
            wait_sends(lambda s: dkv_copy(1, s))

        def one(s, carry):
            queries, dmixed = head_parts(r.q[layer, s], r.dmixed[s])
            keys, values = [slab(layer, s, 0), slab(layer, s, 2)], [slab(layer, s, 1), slab(layer, s, 2)]
            scores = [nt(keys[j // 2], queries[j]) + r.table[s * 3 + j].astype(F32) for j in range(3)]
            dprobs = [nt(values[j // 2], dmixed[j]) for j in range(3)]
            probs, dscores, dq_rows = [], [], []
            for j in range(3):
                p, ds = score_gradients(scores[j], r.lse[layer, s, j : j + 1], dprobs[j])
                probs.append(p)
                dscores.append(ds)
                dq = tn(keys[j // 2], ds)
                dq_rows.append(dq[64:] if j == 1 else dq[:64])
            pairs = [
                (dscores[:2], queries[:2]),
                (probs[:2], dmixed[:2]),
                ([dscores[2], probs[2]], [queries[2], dmixed[2]]),
            ]
            for m, (left, other) in enumerate(pairs):
                lanes = slice(m * 128, (m + 1) * 128)
                dkv = nn(jnp.concatenate(left, axis=1), jnp.concatenate(other, axis=0))
                r.dkv_sent[s, :, lanes] = dkv[HALF:].astype(BF)
                r.dkv[s, :, lanes] = dkv[:HALF]
            dkv_copy(layer, s).start()
            r.dq[s, :, :128] = (jnp.concatenate(dq_rows[:2], axis=0).T * 0.125).astype(BF)
            third = jnp.concatenate([dq_rows[2], jnp.zeros_like(dq_rows[2])], axis=0)
            r.dq[s, :, 128:] = (third.T * 0.125).astype(BF)
            return carry

        lax.fori_loop(0, TP, one, 0)
        if layer == 0:
            pending.append(lambda: wait_sends(lambda s: dkv_copy(layer, s)))

    def project_back(layer, residual):
        r.acc[...] = jnp.zeros_like(r.acc)

        def one(s, carry):
            dkv_copy(layer, s).wait_recv()
            dkv = (r.dkv[s] + r.dkv_got[layer, s].astype(F32)).astype(BF)
            left = jnp.concatenate([r.dq[s, :, :128], dkv, r.dq[s, :, 128:]], axis=1)
            r.acc[...] += nn(left, r.qkv[layer, s])
            return carry

        lax.fori_loop(0, TP, one, 0)
        return r.upper[...] + rms_back(residual, r.gain_attn[layer : layer + 1].astype(F32), r.acc[...])

    half_rows, x_rows, y_rows = SUM_ROWS // 2, SUM_ROWS // 8, SUM_ROWS // 32
    summing = {}

    def sum_step(step):
        def send(n, src, dst, device):
            return remote(src, dst, r.sum_s.at[n], r.sum_r.at[n], device)

        if step > 0:
            arrived(summing[step - 1])
        if step == 0:
            copies = [send(0, r.packed.at[rows((1 - c) * half_rows, half_rows)], r.half_sum, partner)]
        elif step == 1:
            r.half_sum[...] = (
                r.packed[rows(c * half_rows, half_rows)].astype(F32) + r.half_sum[...].astype(F32)
            ).astype(BF)
            copies = [
                send(1 + d, r.half_sum.at[rows(lax.rem(x + d + 1, TP) * x_rows, x_rows)], r.from_x.at[d], x_devices[d])
                for d in range(3)
            ]
        elif step == 2:
            r.piece[...] = (
                r.half_sum[rows(x * x_rows, x_rows)].astype(F32)
                + r.from_x[0].astype(F32)
                + r.from_x[1].astype(F32)
                + r.from_x[2].astype(F32)
            ).astype(BF)
            copies = [
                send(4 + d, r.piece.at[rows(lax.rem(y + d + 1, SIDES) * y_rows, y_rows)], r.from_y.at[d], y_devices[d])
                for d in range(3)
            ]
        elif step == 3:
            r.small[...] = (
                r.piece[rows(y * y_rows, y_rows)].astype(F32)
                + r.from_y[0].astype(F32)
                + r.from_y[1].astype(F32)
                + r.from_y[2].astype(F32)
            ).astype(BF)
            copies = [send(7 + d, r.small, r.from_z.at[z], z_devices[d]) for d in range(3)]
            r.from_z[z] = r.small[...]
        elif step == 4:
            block = rows(c * half_rows + x * x_rows + y * y_rows, y_rows)
            parts = [r.from_z[n].astype(F32) for n in range(4)]
            r.total[block] = (parts[0] + parts[1] + parts[2] + parts[3]).astype(BF)
            copies = [send(10 + d, r.total.at[block], r.total.at[block], y_devices[d]) for d in range(3)]
        elif step == 5:
            block = rows(c * half_rows + x * x_rows, x_rows)
            copies = [send(13 + d, r.total.at[block], r.total.at[block], x_devices[d]) for d in range(3)]
        elif step == 6:
            block = rows(c * half_rows, half_rows)
            copies = [send(16, r.total.at[block], r.total.at[block], partner)]
        else:
            copies = []
        summing[step] = start(copies)

    def to_all(n, source, target):
        place_here = sequence * 2 + c
        turned_rows = jnp.concatenate([source, jnp.zeros((HALF, 32), F32)], axis=1).T[:SIDE_W]
        source = (r.start_own, r.cot_own)[n]
        source[...] = turned_rows
        block = target.at[:, pl.ds(pl.multiple_of(place_here * HALF, HALF), HALF)]
        for d in range(1, TP):
            device = {"tp": lax.rem(x + d, TP), "batch": chip(y, z, parity)}
            start([remote(source, block, r.all_s.at[n, d], r.all_r.at[n, place_here], device)])
        here = pltpu.make_async_copy(source, block, r.all_own.at[n])
        over = remote(source, block, r.all_s.at[n, 0], r.all_r.at[n, place_here], partner)

        @pl.when(stays)
        def _():
            here.start()

        @pl.when(jnp.logical_not(stays))
        def _():
            over.start()

        def finish():
            for m in range(4):
                piece = target.at[:, m * HALF : (m + 1) * HALF]
                own = stays & (place_here == m)
                got = remote(source, piece, r.all_s.at[n, 0], r.all_r.at[n, m], partner)

                @pl.when(jnp.logical_not(own))
                def _():
                    got.wait_recv()

            @pl.when(stays)
            def _():
                here.wait()

            @pl.when(jnp.logical_not(stays))
            def _():
                over.wait_send()

        pending.append(finish)

    def give_back(n, source, target):
        here = pltpu.make_async_copy(source, target, r.back_own.at[n])
        over = remote(source, target, r.back_s.at[n], r.back_r.at[n], across)

        @pl.when(stays)
        def _():
            here.start()

        @pl.when(jnp.logical_not(stays))
        def _():
            over.start()

        def finish():
            @pl.when(stays)
            def _():
                here.wait()

            @pl.when(jnp.logical_not(stays))
            def _():
                over.wait()

        pending.append(finish)

    make_base()
    arrived(early)
    make_table(0, 6)
    gather("B0 A2 WA QB")
    make_table(6, 12)
    gather("B1 A3 C0")
    r.packed[...] = jnp.zeros_like(r.packed)
    lay_out_side()
    gather("B2 A4 D0 WB QE QF C1 B3 A5 E0 C2 D1")
    for copy in side_loads:
        copy.wait()
    r.state[0] = transposed(jnp.where(stays, r.start_own[...], r.start_got[...]))
    r.grad_side[2] = transposed(jnp.where(stays, r.cot_own[...], r.cot_got[...]))

    @pl.when(stays)
    def _():
        tokens_here.wait()

    @pl.when(jnp.logical_not(stays))
    def _():
        tokens_over.wait()

    gather("F0")
    project(0, r.tokens[...].astype(F32))
    gather("B4 D2 WE")
    attend(0)
    gather("C3 E1 WF B5 C4 E2 D3 C5 F1 F2")
    feed(0, r.tokens[...].astype(F32))
    gather("D4 E3 D5")
    side_begin(0)
    side_attend(0)
    gather("F3 E4")
    project(1, r.residual[...])
    gather("E5")
    attend(1)
    gather("F4 F5")
    feed(1, r.residual[...])
    give_back(0, r.low.at[1], r.backbone_out)
    side_begin(1)
    side_attend(1)
    to_all(0, r.state[2], r.side_out)
    side_back(1)
    side_end(1)
    side_back(0)
    side_end(0)
    to_all(1, r.grad_side[0], r.grad_start)
    sum_step(0)
    feed_back(1)
    sum_step(1)
    attend_back(1)
    sum_step(2)
    r.upper[...] = project_back(1, r.residual[...])
    sum_step(3)
    feed_back(0)
    sum_step(4)
    attend_back(0)
    sum_step(5)
    r.normed[...] = project_back(0, r.tokens[...].astype(F32)).astype(BF)
    give_back(1, r.normed, r.grad)
    sum_step(6)
    sum_step(7)
    for finish in pending:
        finish()


def network(arrays):
    anywhere, vmem = pl.BlockSpec(memory_space=pl.ANY), pl.BlockSpec(memory_space=pltpu.VMEM)
    smem = pl.BlockSpec(memory_space=pltpu.SMEM)
    dma = pltpu.SemaphoreType.DMA
    return pl.pallas_call(
        network_kernel,
        out_shape=[shape(dims, dtype) for dims, dtype, _ in OUTPUTS.values()],
        in_specs=[smem if name == "lengths" else anywhere if name in FAR else vmem for name in INPUTS],
        out_specs=[anywhere if far else vmem for _, _, far in OUTPUTS.values()],
        scratch_shapes=[pltpu.VMEM(dims, dtype) for dims, dtype in BUFFERS.values()]
        + [dma(dims) for dims in SEMAPHORES.values()],
        compiler_params=pltpu.CompilerParams(
            collective_id=0, has_side_effects=True, vmem_limit_bytes=VMEM_BYTES
        ),
    )(*[arrays[name] for name in INPUTS])


def per_device(
    inputs, side_start, lengths, offset_bias, gain_attn, w_query, w_key, w_value, w_out, gain_ffn, w_inner,
    w_outer, narrowing_weight, gate_logit, side_gain1, side_qkv, side_proj, side_gain2, side_inner, side_outer,
    side_cotangent,
):
    def turned(array):
        return jnp.swapaxes(array, -1, -2)

    arrays = dict(
        inputs=inputs,
        side_start=turned(side_start),
        side_cotangent=turned(side_cotangent),
        lengths=lengths,
        bias=offset_bias,
        gain_attn=gain_attn,
        gain_ffn=gain_ffn,
        w_query=turned(w_query),
        w_key=turned(w_key),
        w_value=turned(w_value),
        w_inner=w_inner,
        w_outer=w_outer,
        w_out=w_out,
        narrow=turned(narrowing_weight),
        gate=gate_logit,
        gain1=side_gain1,
        gain2=side_gain2,
        side_qkv=side_qkv,
        proj=side_proj,
        side_inner=side_inner,
        side_outer=turned(side_outer),
    )
    backbone_out, side_out, grad_start, grad, total = network(arrays)
    outs = [
        shape((2, SIDE_W, WIDTH), F32),
        shape((2, SIDE_W), F32),
        shape((2, SIDE_W), F32),
        shape((2, SIDE_W, 3 * SIDE_W), F32),
        shape((2, SIDE_W, SIDE_W), F32),
        shape((2, SIDE_W), F32),
        shape((2, SIDE_W, SIDE_FF), F32),
        shape((2, SIDE_W, SIDE_FF), F32),
    ]
    summed = call(
        unpack_kernel, (1,), [whole((SUM_ROWS, 128))], [whole(out.shape) for out in outs], outs, nbytes=4 * 10**6
    )(total)
    down, *small, outer = summed
    return (backbone_out, turned(side_out), grad.astype(F32), turned(grad_start), turned(down), *small, turned(outer))


def solution(mesh):
    in_specs = (
        P(("batch", "tp"), None),
        P("batch", None),
        P("batch"),
        P(),
        P(),
        P(None, None, "tp"),
        P(None, None, "tp"),
        P(None, None, "tp"),
        P(None, "tp", None),
        P(),
        P(None, None, "tp"),
        P(None, "tp", None),
        P(),
        P(),
        P(),
        P(),
        P(),
        P(),
        P(),
        P(),
        P("batch", None),
    )
    out_specs = (
        P(("batch", "tp"), None),
        P("batch", None),
        P(("batch", "tp"), None),
        P("batch", None),
        P(),
        P(),
        P(),
        P(),
        P(),
        P(),
        P(),
        P(),
    )
    return jax.shard_map(per_device, mesh=mesh, in_specs=in_specs, out_specs=out_specs, check_vma=False)
```

```python
from functools import partial
import math

import jax
import jax.numpy as jnp
from jax import lax
from jax.experimental import pallas as pl
from jax.experimental.pallas import tpu as pltpu
from jax.sharding import PartitionSpec as P


BF = jnp.bfloat16
F32 = jnp.float32
EPSILON = 1e-06
NEGATIVE = -1e30
HIGHEST = lax.Precision.HIGHEST
MESH = pl.DeviceIdType.MESH
TP = 4
SIDES = 4
HALF = 256
WIDTH = 768
SIDE_W = 96
SIDE_FF = 384
SIDE_SCALE = 1.0 / math.sqrt(8)
GELU_K = math.sqrt(2.0 / math.pi)
VMEM_BYTES = 63 * 1024 * 1024

A_PROJ, A_INNER, A_OUTER, B_QKV, B_DOWN, LAYER_ROWS = 0, 96, 384, 672, 960, 1536


def dot(a, b, ca, cb, precision=None):
    return lax.dot_general(
        a, b, (((ca,), (cb,)), ((), ())), preferred_element_type=F32, precision=precision
    )


def nn(a, b, precision=None):
    return dot(a, b, 1, 0, precision)


def nt(a, b, precision=None):
    return dot(a, b, 1, 1, precision)


def tn(a, b, precision=None):
    return dot(a, b, 0, 0, precision)


def rms_scale(values):
    return lax.rsqrt(jnp.mean(values * values, axis=-1, keepdims=True) + EPSILON)


def rms_back(values, gain_row, grad):
    scale = rms_scale(values)
    scaled = grad * gain_row
    inner = jnp.mean(scaled * values, axis=-1, keepdims=True)
    return scale * scaled - values * (scale * scale * scale * inner)


def gelu_parts(hidden):
    square = hidden * hidden
    tanh = jnp.tanh(GELU_K * hidden * (1.0 + 0.044715 * square))
    plus = 0.5 * (1.0 + tanh)
    slope = plus + (0.5 * GELU_K) * hidden * (1.0 - tanh * tanh) * (1.0 + (3 * 0.044715) * square)
    return hidden * plus, slope


def lane_mask(test):
    lanes = lax.broadcasted_iota(jnp.int32, (HALF, 128), 1)
    return jnp.where(test(lanes), 1.0, 0.0).astype(BF)


def row_block(shape, index_map):
    return pl.BlockSpec(shape, index_map)


def whole(shape):
    return pl.BlockSpec(shape, lambda *_: (0,) * len(shape))


def call(kernel, grid, in_specs, out_specs, out_shape, scratch=(), prefetch=0, flops=0, nbytes=0):
    return pl.pallas_call(
        kernel,
        grid_spec=pltpu.PrefetchScalarGridSpec(
            num_scalar_prefetch=prefetch,
            grid=grid,
            in_specs=in_specs,
            out_specs=out_specs,
            scratch_shapes=scratch,
        ),
        out_shape=out_shape,
        compiler_params=pltpu.CompilerParams(vmem_limit_bytes=VMEM_BYTES),
        cost_estimate=pl.CostEstimate(flops=flops, bytes_accessed=nbytes, transcendentals=0),
    )


def shape(dims, dtype):
    return jax.ShapeDtypeStruct(dims, dtype)


def results_kernel(
    out_in, side_in, start_in, grad_in, total,
    out, side, grad, start, down_out, gate_out, gain1_out, qkv_out, proj_out, gain2_out, inner_out, outer_out,
):
    out[...] = out_in[...]
    side[...] = side_in[...]
    start[...] = start_in[...]
    grad[...] = grad_in[...].astype(F32)
    for layer in range(2):

        def part(first, count, layer=layer):
            return total[layer, first : first + count].astype(F32)

        proj = part(A_PROJ, 96)
        proj_out[layer] = proj[:, :SIDE_W]
        small = jnp.concatenate([proj, jnp.zeros((32, 128), F32)], axis=0).T[96:104]
        gate_out[layer : layer + 1] = small[0:1, :SIDE_W]
        gain1_out[layer : layer + 1] = small[1:2, :SIDE_W]
        gain2_out[layer : layer + 1] = small[2:3, :SIDE_W]
        for n in range(3):
            lanes = slice(n * 128, (n + 1) * 128)
            inner_out[layer, :, lanes] = part(A_INNER + n * 96, 96)
            outer_out[layer, :, lanes] = part(A_OUTER + n * 96, 96)
        triple = [part(B_QKV + n * 96, 96)[:, :SIDE_W] for n in range(3)]
        qkv_out[layer] = jnp.concatenate(triple, axis=1)
        for n in range(6):
            down_out[layer, :, n * 128 : (n + 1) * 128] = part(B_DOWN + n * 96, 96)


def head_parts(q, dm=None):
    low = lane_mask(lambda lanes: lanes < 64)
    high = lane_mask(lambda lanes: lanes >= 64)
    queries = [q[:, :128] * low, q[:, :128] * high, q[:, 128:]]
    if dm is None:
        return queries
    return queries, [dm[:, :128] * low, dm[:, :128] * high, dm[:, 128:]]


def softmax_parts(scores):
    top = jnp.max(scores, axis=0, keepdims=True)
    exps = jnp.exp(scores - top)
    total = jnp.sum(exps, axis=0, keepdims=True)
    return exps.astype(BF), 1.0 / total, top + jnp.log(total)


def score_gradients(scores, lse, dprobs):
    probs = jnp.exp(scores - lse)
    inner = jnp.sum(probs * dprobs, axis=0, keepdims=True)
    return probs.astype(BF), (probs * (dprobs - inner)).astype(BF)


def split_pack(values, low_test):
    high = values.astype(BF)
    low = (values - high.astype(F32)).astype(BF)
    mask = lane_mask(low_test)
    return high * (1 - mask) + low * mask


def of_head(j, blocks):
    def test(lanes):
        hit = (lanes >= blocks[0] * 24 + j * 8) & (lanes < blocks[0] * 24 + j * 8 + 8)
        for n in blocks[1:]:
            hit = hit | ((lanes >= n * 24 + j * 8) & (lanes < n * 24 + j * 8 + 8))
        return hit

    return lane_mask(test)


def transposed(rows):
    return jnp.concatenate([rows, jnp.zeros((32, rows.shape[1]), rows.dtype)], axis=0).T[:, :SIDE_W]


INPUTS = [
    "inputs", "side_start", "side_cotangent", "lengths", "bias", "gain_attn", "gain_ffn", "w_query", "w_key", "w_value",
    "w_inner", "w_outer", "w_out", "narrow", "gate", "gain1", "gain2", "side_qkv", "proj", "side_inner", "side_outer",
]
SMALL = {
    "bias": ((12, 4 * HALF - 1), BF),
    "gain_attn": ((2, WIDTH), BF),
    "gain_ffn": ((2, WIDTH), BF),
    "narrow": ((2, SIDE_W, WIDTH), BF),
    "gate": ((2, SIDE_W), F32),
    "gain1": ((2, SIDE_W), F32),
    "gain2": ((2, SIDE_W), F32),
    "side_qkv": ((2, SIDE_W, 3 * SIDE_W), F32),
    "proj": ((2, SIDE_W, SIDE_W), F32),
    "side_inner": ((2, SIDE_W, SIDE_FF), F32),
    "side_outer": ((2, SIDE_W, SIDE_FF), F32),
}

OUTPUTS = {
    "backbone_out": ((HALF, WIDTH), BF, True),
    "side_out": ((SIDE_W, 4 * HALF), F32, True),
    "grad_start": ((SIDE_W, 4 * HALF), F32, True),
    "grad": ((HALF, WIDTH), BF, True),
    "total": ((2, LAYER_ROWS, 128), BF, False),
}

BUFFERS = {
    "qkv": ((2, TP, 576, WIDTH), BF),
    "inner": ((2, TP, WIDTH, WIDTH), BF),
    "outer": ((2, TP, WIDTH, WIDTH), BF),
    "out": ((2, TP, 192, WIDTH), BF),
    "tokens": ((HALF, WIDTH), BF),
    "start_own": ((SIDE_W, HALF), F32),
    "start_got": ((SIDE_W, HALF), F32),
    "cot_own": ((SIDE_W, HALF), F32),
    "cot_got": ((SIDE_W, HALF), F32),
    "span_own": ((8, HALF), F32),
    "span_got": ((8, HALF), F32),
    "wide_bias": ((16, 4 * HALF), BF),
    "wide_query": ((2, SIDE_W, 512), F32),
    "wide_kv": ((2, SIDE_W, 512), F32),
    "back_query": ((2, SIDE_W, SIDE_W), BF),
    "back_kv": ((2, SIDE_W, 256), BF),
    "table": ((12, 2 * HALF, HALF), BF),
    "q": ((2, TP, HALF, 256), BF),
    "kv": ((2, TP, 2, HALF, 384), BF),
    "lse": ((2, TP, 8, HALF), F32),
    "mid": ((2, HALF, WIDTH), F32),
    "slope": ((2, TP, HALF, WIDTH), BF),
    "residual": ((HALF, WIDTH), F32),
    "low": ((2, HALF, WIDTH), BF),
    "down": ((2, HALF, SIDE_W), BF),
    "state": ((3, HALF, SIDE_W), F32),
    "joined": ((2, HALF, SIDE_W), F32),
    "side_mixed": ((2, HALF, SIDE_W), F32),
    "side_q": ((2, 4, HALF, 128), BF),
    "side_kv": ((2, 4, 2, HALF, 128), BF),
    "side_lse": ((2, 4, 8, HALF), F32),
    "normed": ((HALF, WIDTH), BF),
    "acc": ((HALF, WIDTH), F32),
    "grad_side": ((3, HALF, SIDE_W), F32),
    "djoined": ((HALF, SIDE_W), F32),
    "side_dmixed": ((4, HALF, 128), BF),
    "side_dq": ((SIDE_W, HALF), F32),
    "side_dkv": ((4, HALF, 128), F32),
    "side_dkv_sent": ((4, HALF, 128), BF),
    "side_dkv_got": ((2, 4, HALF, 128), BF),
    "ddown": ((2, HALF, SIDE_W), BF),
    "upper": ((HALF, WIDTH), F32),
    "dmixed": ((TP, HALF, 256), BF),
    "dq": ((TP, HALF, 256), BF),
    "dkv": ((TP, HALF, 384), F32),
    "dkv_sent": ((TP, HALF, 384), BF),
    "dkv_got": ((2, TP, HALF, 384), BF),
    "gain2_sum": ((1, SIDE_W), F32),
    "packed": ((2, LAYER_ROWS, 128), BF),
    "half_sum": ((2, LAYER_ROWS // 2, 128), BF),
    "from_x": ((2, 3, LAYER_ROWS // 8, 128), BF),
    "piece": ((2, LAYER_ROWS // 8, 128), BF),
    "from_y": ((2, 3, LAYER_ROWS // 32, 128), BF),
    "small": ((2, LAYER_ROWS // 32, 128), BF),
    "from_z": ((2, 4, LAYER_ROWS // 32, 128), BF),
}

SEMAPHORES = {
    "load": (12 + 11,),
    "early_s": (4,),
    "early_r": (4,),
    "x_s": (6, 6),
    "x_r": (6, 6),
    "yz_s": (6, 12),
    "yz_r": (6, 12),
    "core_s": (6,),
    "core_r": (6,),
    "out_s": (20,),
    "out_r": (20,),
    "kv_s": (2, TP),
    "kv_r": (2, TP),
    "side_kv_s": (2, 4),
    "side_kv_r": (2, 4),
    "dkv_s": (2, TP),
    "dkv_r": (2, TP),
    "side_dkv_s": (2, 4),
    "side_dkv_r": (2, 4),
    "sum_s": (2, 17),
    "sum_r": (2, 17),
    "all_s": (2, 4),
    "all_r": (2, 4),
    "all_own": (2,),
    "back_s": (2,),
    "back_r": (2,),
    "back_own": (2,),
}


class Refs:
    def __init__(self, names, refs):
        self.__dict__.update(zip(names, refs))


def rows(start, count):
    return pl.ds(pl.multiple_of(start, 16), count)


def network_kernel(*refs):
    given = ["given_" + name if name in SMALL else name for name in INPUTS]
    r = Refs(given + list(OUTPUTS) + list(BUFFERS) + list(SMALL) + list(SEMAPHORES), refs)
    x = lax.axis_index("tp")
    b = lax.axis_index("batch")
    c = lax.rem(b, 2)
    z = lax.rem(b // 2, SIDES)
    y = b // (2 * SIDES)
    parity = lax.rem(x, 2)
    stays = parity == c
    sequence = lax.div(x, 2)

    def chip(y_now, z_now, c_now):
        return (y_now * SIDES + z_now) * 2 + c_now

    left, right = {"tp": lax.rem(x + TP - 1, TP)}, {"tp": lax.rem(x + 1, TP)}
    x_devices = [{"tp": lax.rem(x + d, TP)} for d in (1, 2, 3)]
    y_devices = [{"batch": chip(lax.rem(y + d, SIDES), z, c)} for d in (1, 2, 3)]
    z_devices = [{"batch": chip(y, lax.rem(z + d, SIDES), c)} for d in (1, 2, 3)]
    up, down = (y_devices[0], z_devices[0]), (y_devices[2], z_devices[2])
    partner = {"batch": chip(y, z, 1 - c)}
    across = {"tp": x + 1 - 2 * parity, "batch": chip(y, z, 1 - c)}

    pending = []

    def remote(src, dst, send_sem, recv_sem, device):
        return pltpu.make_async_remote_copy(
            src_ref=src, dst_ref=dst, send_sem=send_sem, recv_sem=recv_sem, device_id=device, device_id_type=MESH
        )

    def start(copies):
        for copy in copies:
            copy.start()
            pending.append(copy.wait_send)
        return copies

    def arrived(copies):
        for copy in copies:
            copy.wait_recv()

    def load(n, source, target):
        copy = pltpu.make_async_copy(source, target, r.load.at[n])
        copy.start()
        return copy

    own_lanes = pl.ds(pl.multiple_of(sequence * (2 * HALF) + c * HALF, HALF), HALF)
    sent_lanes = pl.ds(pl.multiple_of(sequence * (2 * HALF) + (1 - c) * HALF, HALF), HALF)
    qkv_loads = [
        load(n, source.at[:, low:high], r.qkv.at[:, 0, place : place + high - low])
        for n, (source, low, high, place) in enumerate((
            (r.w_query, 0, 128, 0),
            (r.w_key, 0, 128, 128),
            (r.w_value, 0, 128, 256),
            (r.w_key, 128, 192, 384),
            (r.w_value, 128, 192, 448),
            (r.w_query, 128, 192, 512),
        ))
    ]
    side_loads = [
        load(6, r.side_start.at[:, own_lanes], r.start_own),
        load(7, r.side_cotangent.at[:, own_lanes], r.cot_own),
    ]
    weight_loads = [
        load(8, r.w_out, r.out.at[:, 0]),
        load(9, r.w_inner, r.inner.at[:, 0]),
        load(10, r.w_outer, r.outer.at[:, 0]),
    ]
    small_loads = [
        load(12 + n, getattr(r, "given_" + name), getattr(r, name)) for n, name in enumerate(SMALL)
    ]
    r.span_own[...] = jnp.full((8, HALF), r.lengths[sequence].astype(F32))
    r.q[:, :, :, 192:] = jnp.zeros((2, TP, HALF, 64), BF)

    barrier = pltpu.get_barrier_semaphore()
    line = [{"tp": lax.rem(x + d, TP), "batch": chip(y, z, core)} for d in (1, 2, 3) for core in (0, 1)]
    for device in [partner] + line + y_devices + z_devices:
        pl.semaphore_signal(barrier, inc=1, device_id=device, device_id_type=MESH)
    pl.semaphore_wait(barrier, 13)

    chunks = [
        chunk
        for layer in range(2)
        for chunk in (
            (r.qkv.at[layer, 0], r.qkv, layer),
            (r.w_inner.at[layer], r.inner, layer),
            (r.w_outer.at[layer], r.outer, layer),
        )
    ]

    def place(k):
        core_rows = 256 if k % 3 == 0 else 384
        low = c * core_rows
        part = core_rows // 8
        return (
            rows(low, core_rows),
            (rows(low + y * part, part), rows(low + core_rows // 2 + z * part, part)),
        )

    direct = {
        "V": (r.w_out.at[0], r.out.at[0], 192, 0, 0),
        "W": (r.w_out.at[1], r.out.at[1], 192, 0, 5),
        "Q": (r.qkv.at[0, 0], r.qkv.at[0], 64, 512, 10),
        "R": (r.qkv.at[1, 0], r.qkv.at[1], 64, 512, 15),
    }
    flying = {}

    def first(k):
        source, target, layer = chunks[k]
        _, blocks = place(k)
        return [
            remote(
                source.at[blocks[path]],
                target.at[layer, slot, blocks[path]],
                r.x_s.at[k, path * 2 + slot - 1],
                r.x_r.at[k, path * 2 + slot - 1],
                device,
            )
            for path in range(2)
            for device, slot in ((right, 2), (left, 1))
        ]

    def relay(k):
        _, target, layer = chunks[k]
        _, (y_block, z_block) = place(k)
        return [
            remote(target.at[layer, 2, y_block], target.at[layer, 3, y_block], r.x_s.at[k, 4], r.x_r.at[k, 4], right),
            remote(target.at[layer, 1, z_block], target.at[layer, 3, z_block], r.x_s.at[k, 5], r.x_r.at[k, 5], left),
        ]

    def spread(k, part):
        _, target, layer = chunks[k]
        _, blocks = place(k)
        slots = pl.ds(1, 2) if part == 0 else pl.ds(3, 1)
        out = []
        for path in range(2):
            block = target.at[layer, slots, blocks[path]]
            for way, device in enumerate((up[path], down[path])):
                n = part * 4 + path * 2 + way
                out.append(remote(block, block, r.yz_s.at[k, n], r.yz_r.at[k, n], device))
        return out

    def spread_relay(k):
        _, target, layer = chunks[k]
        out = []
        for path in range(2):
            part = 32 if k % 3 == 0 else 48
            cut = 32 if part == 48 and (k + path) % 2 == 0 else 16
            for n, (step, device, low, high) in enumerate(
                ((SIDES - 1, up[path], 0, cut), (1, down[path], cut, part))
            ):
                start_row = c * part * 8 + path * part * 4 + lax.rem((y, z)[path] + step, SIDES) * part
                block = target.at[layer, pl.ds(1, 3), rows(start_row + low, high - low)]
                m = 8 + path * 2 + n
                out.append(remote(block, block, r.yz_s.at[k, m], r.yz_r.at[k, m], device))
        return out

    def swap(k):
        _, target, layer = chunks[k]
        mine, _ = place(k)
        block = target.at[layer, pl.ds(1, 3), mine]
        return [remote(block, block, r.core_s.at[k], r.core_r.at[k], partner)]

    def straight(kind, step):
        source, target, count, base, sem = direct[kind]
        base = base + c * (count // 2)
        mine, low, high = rows(base, count // 2), rows(base, count // 4), rows(base + count // 4, count // 4)

        def go(n, block_from, block_to, device):
            return remote(block_from, block_to, r.out_s.at[sem + n], r.out_r.at[sem + n], device)

        if step == "A":
            return [
                go(0, source.at[mine], target.at[2, mine], right),
                go(1, source.at[mine], target.at[1, mine], left),
            ]
        if step == "B":
            return [
                go(2, target.at[2, low], target.at[3, low], right),
                go(3, target.at[1, high], target.at[3, high], left),
            ]
        block = target.at[pl.ds(1, 3), mine]
        return [go(4, block, block, partner)]

    def gather(*steps):
        for step in steps:
            kind, k = step[0], step[1:]
            if kind in direct:
                if k != "A":
                    arrived(flying[kind])
                flying[kind] = start(straight(kind, k)) if k != "F" else []
                continue
            k = int(k)
            if kind == "A":
                flying["A", k] = start(first(k))
            elif kind == "B":
                arrived(flying["A", k])
                flying["B", k] = start(relay(k))
                flying["S", k] = start(spread(k, 0))
            elif kind == "C":
                arrived(flying["B", k])
                flying["S", k] += start(spread(k, 1))
            elif kind == "D":
                arrived(flying["S", k])
                flying["D", k] = start(spread_relay(k))
            elif kind == "E":
                arrived(flying["D", k])
                flying["E", k] = start(swap(k))
            else:
                arrived(flying["E", k])

    early = [
        remote(r.span_own, r.span_got, r.early_s.at[0], r.early_r.at[0], partner),
        remote(r.side_start.at[:, sent_lanes], r.start_got, r.early_s.at[1], r.early_r.at[1], partner),
        remote(r.side_cotangent.at[:, sent_lanes], r.cot_got, r.early_s.at[2], r.early_r.at[2], partner),
    ]
    tokens_here = pltpu.make_async_copy(r.inputs, r.tokens, r.load.at[11])
    tokens_over = remote(r.inputs, r.tokens, r.early_s.at[3], r.early_r.at[3], across)

    for copy in qkv_loads:
        copy.wait()
    gather("A0")
    gather("QA")
    gather("A1")
    start(early)

    def table_slot(shard):
        turn = lax.rem(shard + TP - x, TP)
        return turn + jnp.where(turn == 2, 1, 0) - jnp.where(turn == 3, 1, 0)

    def make_base():
        row = lax.broadcasted_iota(jnp.int32, (HALF, HALF), 0)
        column = lax.broadcasted_iota(jnp.int32, (HALF, HALF), 1)
        reverse = jnp.where(row + column == HALF - 1, 1.0, 0.0).astype(BF)
        r.wide_bias[...] = jnp.zeros_like(r.wide_bias)
        r.wide_bias[:12, : 4 * HALF - 1] = r.bias[...]
        turned = [nn(r.wide_bias[:, n * HALF : (n + 1) * HALF], reverse) for n in range(4)]
        other = [jnp.where(c == 0, turned[n + 2], turned[n]) for n in range(2)]
        for head in range(12):
            one = slice(head, head + 1)
            r.acc[16 * head : 16 * head + 1, :HALF] = turned[1][one]
            r.acc[16 * head : 16 * head + 1, HALF : 2 * HALF] = turned[2][one]
            r.acc[16 * head + 8 : 16 * head + 9, :HALF] = other[0][one]
            r.acc[16 * head + 8 : 16 * head + 9, HALF : 2 * HALF] = other[1][one]

    def make_table(low, high):
        row = lax.broadcasted_iota(jnp.int32, (HALF, HALF), 0)
        length = jnp.where(stays, r.span_own[0:1], r.span_got[0:1])
        place = row.astype(F32)

        def one(head, carry):
            slot = table_slot(lax.div(head, 3)) * 3 + lax.rem(head, 3)
            for side in range(2):
                first_key = (c if side == 0 else 1 - c) * HALF
                spread_row = jnp.broadcast_to(
                    r.acc[pl.ds(head * 16 + side * 8, 1), : 2 * HALF], (HALF, 2 * HALF)
                )
                rolled = pltpu.roll(spread_row, 0, 1, stride=1, stride_axis=0)[:, :HALF]
                counts = place + first_key.astype(F32) < length
                r.table[slot, side * HALF : (side + 1) * HALF] = jnp.where(counts, rolled, NEGATIVE).astype(BF)
            return carry

        lax.fori_loop(low, high, one, 0)

    def ones(test):
        return jnp.where(test, 1.0, 0.0)

    def to_lanes(g):
        row = lax.broadcasted_iota(jnp.int32, (SIDE_W, 128), 0)
        lane = lax.broadcasted_iota(jnp.int32, (SIDE_W, 128), 1)
        thrice = lane - jnp.where(lane >= 24, 24, 0) - jnp.where(lane >= 48, 24, 0)
        twice = lane - 72 - jnp.where(lane >= 96, 24, 0)
        keys = ones((row == thrice + g * 24) & (lane < 72))
        return keys, ones((row == twice + g * 24) & (lane >= 72) & (lane < 120))

    def from_lanes(g):
        row = lax.broadcasted_iota(jnp.int32, (128, 128), 0)
        column = lax.broadcasted_iota(jnp.int32, (128, 128), 1)
        keys = ones((row < 24) & (column == row + g * 24))
        values = ones((row >= 72) & (row < 96) & (column == row - 72 + g * 24))
        return jnp.concatenate([keys, values], axis=1).astype(BF)

    def lay_out_side():
        for g in range(4):
            lanes = slice(g * 128, (g + 1) * 128)
            to_keys, to_values = to_lanes(g)
            for layer in range(2):
                weight = r.side_qkv[layer]
                query, key, value = weight[:, :96], weight[:, 96:192], weight[:, 192:]
                r.wide_query[layer, :, lanes] = nn(query, to_keys, HIGHEST) * SIDE_SCALE
                r.wide_kv[layer, :, lanes] = nn(key, to_keys, HIGHEST) + nn(value, to_values, HIGHEST)
        for layer in range(2):
            weight = r.side_qkv[layer]
            r.back_query[layer] = (weight[:, :96] * SIDE_SCALE).astype(BF)
            r.back_kv[layer] = jnp.zeros((SIDE_W, 256), BF)
            r.back_kv[layer, :, :96] = weight[:, 96:192].astype(BF)
            r.back_kv[layer, :, 128:224] = weight[:, 192:].astype(BF)

    def loop(low, high, *bodies):
        def one(s, carry):
            for body in bodies:
                body(s)
            return carry

        lax.fori_loop(low, high, one, 0)

    def project_begin(layer, residual):
        r.normed[...] = (residual * rms_scale(residual) * r.gain_attn[layer : layer + 1].astype(F32)).astype(BF)
        pending.append(lambda: wait_sends(lambda s: kv_copy(layer, s)))

    def project_one(layer):
        def one(s):
            out = nt(r.normed[...], r.qkv[layer, s])
            r.kv[layer, s, 0] = out[:, 128:512].astype(BF)
            kv_copy(layer, s).start()
            r.q[layer, s, :, :128] = (out[:, :128] * 0.125).astype(BF)
            r.q[layer, s, :, 128:192] = (out[:, 512:] * 0.125).astype(BF)

        return one

    def kv_copy(layer, s):
        return remote(r.kv.at[layer, s, 0], r.kv.at[layer, s, 1], r.kv_s.at[layer, s], r.kv_r.at[layer, s], partner)

    def wait_sends(copy_of):
        def one(s, carry):
            copy_of(s).wait_send()
            return carry

        lax.fori_loop(0, 4, one, 0)

    def slab(layer, s, n):
        return r.kv[layer, s, :, :, n * 128 : (n + 1) * 128].reshape(2 * HALF, 128)

    def attend_one(layer):
        def one(s):
            kv_copy(layer, s).wait_recv()
            queries = head_parts(r.q[layer, s])
            keys, values = [slab(layer, s, 0), slab(layer, s, 2)], [slab(layer, s, 1), slab(layer, s, 2)]
            scores = [nt(keys[j // 2], queries[j]) + r.table[s * 3 + j].astype(F32) for j in range(3)]
            parts = [softmax_parts(score) for score in scores]
            heads = [tn(values[j // 2], parts[j][0]) for j in range(3)]
            heads = [(heads[j][:64] if j == 0 else heads[j][64:]) * parts[j][1] for j in range(3)]
            for j in range(3):
                r.lse[layer, s, j : j + 1] = parts[j][2]
            r.dq[s, :, :128] = jnp.concatenate(heads[:2], axis=0).T.astype(BF)
            third = jnp.concatenate([heads[2], jnp.zeros_like(heads[2])], axis=0).T
            r.dq[s, :, 128:192] = third[:, :64].astype(BF)

        return one

    def feed_begin(layer, residual):
        middle = residual
        for s in range(TP):
            middle = middle + nn(r.dq[s, :, :192], r.out[layer, s])
        r.mid[layer] = middle
        r.acc[...] = middle
        r.normed[...] = (middle * rms_scale(middle) * r.gain_ffn[layer : layer + 1].astype(F32)).astype(BF)

    def feed_one(layer):
        def one(s):
            active, slope = gelu_parts(nn(r.normed[...], r.inner[layer, s]))
            r.slope[layer, s] = slope.astype(BF)
            r.acc[...] += nn(active.astype(BF), r.outer[layer, s])

        return one

    def hidden_one(layer):
        def one(s):
            active, slope = gelu_parts(nn(r.normed[...], r.inner[layer, s]))
            r.slope[layer, s] = slope.astype(BF)
            r.dkv_got[0, s] = active[:, :384].astype(BF)
            r.dkv_got[1, s] = active[:, 384:].astype(BF)

        return one

    def outer_one(layer):
        def one(s):
            active = jnp.concatenate([r.dkv_got[0, s], r.dkv_got[1, s]], axis=1)
            r.acc[...] += nn(active, r.outer[layer, s])

        return one

    def feed_finish(layer):
        out = r.acc[...]
        low = out.astype(BF)
        if layer == 0:
            r.residual[...] = out
        r.low[layer] = low
        r.down[layer] = nt(low, r.narrow[layer]).astype(BF)

    def side_kv_copy(layer, g):
        return remote(
            r.side_kv.at[layer, g, 0], r.side_kv.at[layer, g, 1],
            r.side_kv_s.at[layer, g], r.side_kv_r.at[layer, g], partner,
        )

    def side_begin(layer):
        mix = jax.nn.sigmoid(r.gate[layer : layer + 1])
        joined = mix * r.down[layer].astype(F32) + (1.0 - mix) * r.state[layer]
        r.joined[layer] = joined
        normed = joined * rms_scale(joined) * r.gain1[layer : layer + 1]
        kv = nn(normed, r.wide_kv[layer], HIGHEST)
        for g in range(4):
            r.side_kv[layer, g, 0] = split_pack(
                kv[:, g * 128 : (g + 1) * 128], lambda n: ((n >= 48) & (n < 72)) | (n >= 96)
            )
            side_kv_copy(layer, g).start()
        q = nn(normed, r.wide_query[layer], HIGHEST)
        for g in range(4):
            r.side_q[layer, g] = split_pack(q[:, g * 128 : (g + 1) * 128], lambda n: (n >= 24) & (n < 48))
        pending.append(lambda: wait_sends(lambda g: side_kv_copy(layer, g)))

    def side_attend_one(layer):
        def one(g):
            side_kv_copy(layer, g).wait_recv()
            kv = r.side_kv[layer, g].reshape(2 * HALF, 128)
            q = r.side_q[layer, g]
            slot = table_slot(g) * 3
            scores = [nt(kv, q * of_head(j, (0, 1, 2))) + r.table[slot + j].astype(F32) for j in range(3)]
            parts = [softmax_parts(score) for score in scores]
            heads = [tn(kv, parts[j][0]) for j in range(3)]
            for j in range(3):
                both = heads[j][72 + j * 8 : 80 + j * 8] + heads[j][96 + j * 8 : 104 + j * 8]
                r.side_dq[pl.ds(pl.multiple_of(g * 24 + j * 8, 8), 8)] = both * parts[j][1]
                r.side_lse[layer, g, j : j + 1] = parts[j][2]

        return one

    def side_attend_finish(layer):
        mixed = transposed(r.side_dq[...])
        r.side_mixed[layer] = mixed
        joined = r.joined[layer] + nn(mixed, r.proj[layer], HIGHEST)
        normed = joined * rms_scale(joined) * r.gain2[layer : layer + 1]
        active, _ = gelu_parts(nn(normed, r.side_inner[layer], HIGHEST))
        r.state[layer + 1] = joined + nt(active, r.side_outer[layer], HIGHEST)

    def side_dkv_copy(layer, g):
        return remote(
            r.side_dkv_sent.at[g], r.side_dkv_got.at[layer, g],
            r.side_dkv_s.at[layer, g], r.side_dkv_r.at[layer, g], partner,
        )

    def side_back_begin(layer):
        grad = r.grad_side[layer + 1]
        grad_low = grad.astype(BF)
        mixed = r.side_mixed[layer]
        gain = r.gain2[layer : layer + 1]
        joined = r.joined[layer] + nn(mixed, r.proj[layer], HIGHEST)
        unit = joined * rms_scale(joined)
        normed = unit * gain
        active, slope = gelu_parts(nn(normed, r.side_inner[layer], HIGHEST))
        dhidden = (nn(grad_low, r.side_outer[layer].astype(BF)) * slope).astype(BF)
        dnormed = nt(dhidden, r.side_inner[layer].astype(BF))
        djoined = grad + rms_back(joined, gain, dnormed)
        r.djoined[...] = djoined
        djoined_low = djoined.astype(BF)
        dmixed_low = nt(djoined_low, r.proj[layer].astype(BF)).astype(BF)
        for g in range(4):
            r.side_dmixed[g] = nn(dmixed_low, to_lanes(g)[1].astype(BF)).astype(BF)
        r.packed[layer, A_PROJ : A_PROJ + SIDE_W, :SIDE_W] = tn(mixed.astype(BF), djoined_low).astype(BF)
        inner_sum = tn(normed.astype(BF), dhidden).astype(BF)
        outer_sum = tn(grad_low, active.astype(BF)).astype(BF)
        for n in range(3):
            lanes = slice(n * 128, (n + 1) * 128)
            r.packed[layer, A_INNER + n * 96 : A_INNER + (n + 1) * 96] = inner_sum[:, lanes]
            r.packed[layer, A_OUTER + n * 96 : A_OUTER + (n + 1) * 96] = outer_sum[:, lanes]
        r.gain2_sum[...] = jnp.sum(dnormed * unit, axis=0, keepdims=True)
        if layer == 0:
            wait_sends(lambda g: side_dkv_copy(1, g))

    def side_back_one(layer):
        def one(g):
            kv = r.side_kv[layer, g].reshape(2 * HALF, 128)
            q, dm = r.side_q[layer, g], r.side_dmixed[g]
            slot = table_slot(g) * 3
            scores = [nt(kv, q * of_head(j, (0, 1, 2))) + r.table[slot + j].astype(F32) for j in range(3)]
            dprobs = [nt(kv, dm * of_head(j, (3, 4))) for j in range(3)]
            left, right_parts = [], []
            for j in range(3):
                p, ds = score_gradients(scores[j], r.side_lse[layer, g, j : j + 1], dprobs[j])
                dq = tn(kv, ds)
                r.side_dq[pl.ds(pl.multiple_of(g * 24 + j * 8, 8), 8)] = (
                    dq[j * 8 : j * 8 + 8] + dq[48 + j * 8 : 56 + j * 8]
                )
                left += [ds, p]
                right_parts += [q * of_head(j, (0,)), dm * of_head(j, (3,))]
            dkv = nn(jnp.concatenate(left, axis=1), jnp.concatenate(right_parts, axis=0))
            r.side_dkv_sent[g] = dkv[HALF:].astype(BF)
            side_dkv_copy(layer, g).start()
            r.side_dkv[g] = dkv[:HALF]

        if layer == 0:
            pending.append(lambda: wait_sends(lambda g: side_dkv_copy(layer, g)))
        return one

    def side_end(layer):
        joined = r.joined[layer]
        gain = r.gain1[layer : layer + 1]
        unit = joined * rms_scale(joined)
        normed_low = (unit * gain).astype(BF)
        dq = transposed(r.side_dq[...]).astype(BF)
        dkv = jnp.zeros((HALF, 256), F32)
        for g in range(4):
            side_dkv_copy(layer, g).wait_recv()
            both = (r.side_dkv[g] + r.side_dkv_got[layer, g].astype(F32)).astype(BF)
            dkv = dkv + nn(both, from_lanes(g))
        dkv = dkv.astype(BF)
        dnormed = nt(dq, r.back_query[layer]) + nt(dkv, r.back_kv[layer])
        djoined = r.djoined[...] + rms_back(joined, gain, dnormed)
        mix = jax.nn.sigmoid(r.gate[layer : layer + 1])
        ddown = (mix * djoined).astype(BF)
        r.ddown[layer] = ddown
        r.grad_side[layer] = (1.0 - mix) * djoined
        change = r.down[layer].astype(F32) - r.state[layer]
        gate_sum = jnp.sum(djoined * change, axis=0, keepdims=True) * mix * (1.0 - mix)
        gain_sum = jnp.sum(dnormed * unit, axis=0, keepdims=True)
        r.packed[layer, B_QKV : B_QKV + 96, :SIDE_W] = (tn(normed_low, dq) * SIDE_SCALE).astype(BF)
        kv_sum = tn(normed_low, dkv).astype(BF)
        r.packed[layer, B_QKV + 96 : B_QKV + 192] = kv_sum[:, :128]
        r.packed[layer, B_QKV + 192 : B_QKV + 288] = kv_sum[:, 128:]
        down_sum = tn(ddown, r.low[layer]).astype(BF)
        for n in range(6):
            r.packed[layer, B_DOWN + n * 96 : B_DOWN + (n + 1) * 96] = down_sum[:, n * 128 : (n + 1) * 128]
        zeros = jnp.zeros((SIDE_W, SIDE_W), F32)
        small = jnp.concatenate([zeros, gate_sum, gain_sum, r.gain2_sum[...], jnp.zeros((29, SIDE_W), F32)], axis=0)
        small = jnp.concatenate([small, jnp.zeros((128, 32), F32)], axis=1).T[:SIDE_W]
        block = r.packed[layer, A_PROJ : A_PROJ + SIDE_W].astype(F32)
        r.packed[layer, A_PROJ : A_PROJ + SIDE_W] = (block + small).astype(BF)

    def feed_back_begin(layer):
        upper = nn(r.ddown[layer], r.narrow[layer])
        if layer == 0:
            upper = upper + r.upper[...]
        r.upper[...] = upper
        r.normed[...] = upper.astype(BF)
        r.acc[...] = jnp.zeros_like(r.acc)

    def feed_back_one(layer):
        def one(s):
            dactive = nt(r.normed[...], r.outer[layer, s])
            dhidden = (dactive * r.slope[layer, s].astype(F32)).astype(BF)
            r.acc[...] += nt(dhidden, r.inner[layer, s])

        return one

    def feed_back_finish(layer):
        middle = r.upper[...] + rms_back(r.mid[layer], r.gain_ffn[layer : layer + 1].astype(F32), r.acc[...])
        r.upper[...] = middle
        low = middle.astype(BF)
        for s in range(TP):
            r.dmixed[s, :, :128] = nt(low, r.out[layer, s, :128]).astype(BF)
            third = jnp.concatenate([jnp.zeros((64, WIDTH), BF), r.out[layer, s, 128:]], axis=0)
            r.dmixed[s, :, 128:] = nt(low, third).astype(BF)

    def dkv_copy(layer, s):
        return remote(
            r.dkv_sent.at[s], r.dkv_got.at[layer, s], r.dkv_s.at[layer, s], r.dkv_r.at[layer, s], partner
        )

    def attend_back_one(layer):
        def one(s):
            queries, dmixed = head_parts(r.q[layer, s], r.dmixed[s])
            keys, values = [slab(layer, s, 0), slab(layer, s, 2)], [slab(layer, s, 1), slab(layer, s, 2)]
            scores = [nt(keys[j // 2], queries[j]) + r.table[s * 3 + j].astype(F32) for j in range(3)]
            dprobs = [nt(values[j // 2], dmixed[j]) for j in range(3)]
            probs, dscores, dq_rows = [], [], []
            for j in range(3):
                p, ds = score_gradients(scores[j], r.lse[layer, s, j : j + 1], dprobs[j])
                probs.append(p)
                dscores.append(ds)
                dq = tn(keys[j // 2], ds)
                dq_rows.append(dq[64:] if j == 1 else dq[:64])
            pairs = [
                (dscores[:2], queries[:2]),
                (probs[:2], dmixed[:2]),
                ([dscores[2], probs[2]], [queries[2], dmixed[2]]),
            ]
            for m, (left, other) in enumerate(pairs):
                lanes = slice(m * 128, (m + 1) * 128)
                dkv = nn(jnp.concatenate(left, axis=1), jnp.concatenate(other, axis=0))
                r.dkv_sent[s, :, lanes] = dkv[HALF:].astype(BF)
                r.dkv[s, :, lanes] = dkv[:HALF]
            dkv_copy(layer, s).start()
            r.dq[s, :, :128] = (jnp.concatenate(dq_rows[:2], axis=0).T * 0.125).astype(BF)
            third = jnp.concatenate([dq_rows[2], jnp.zeros_like(dq_rows[2])], axis=0)
            r.dq[s, :, 128:] = (third.T * 0.125).astype(BF)

        return one

    def project_back(layer, residual):
        r.acc[...] = jnp.zeros_like(r.acc)

        def one(s, carry):
            dkv_copy(layer, s).wait_recv()
            dkv = (r.dkv[s] + r.dkv_got[layer, s].astype(F32)).astype(BF)
            left = jnp.concatenate([r.dq[s, :, :128], dkv, r.dq[s, :, 128:192]], axis=1)
            r.acc[...] += nn(left, r.qkv[layer, s])
            return carry

        lax.fori_loop(0, TP, one, 0)
        return r.upper[...] + rms_back(residual, r.gain_attn[layer : layer + 1].astype(F32), r.acc[...])

    half_rows, x_rows, y_rows = LAYER_ROWS // 2, LAYER_ROWS // 8, LAYER_ROWS // 32
    summing = {}

    def sum_step(layer, step):
        def send(n, src, dst, device):
            return remote(src, dst, r.sum_s.at[layer, n], r.sum_r.at[layer, n], device)

        if step > 0:
            arrived(summing[layer, step - 1])
        if step == 0:
            copies = [send(0, r.packed.at[layer, rows((1 - c) * half_rows, half_rows)], r.half_sum.at[layer], partner)]
        elif step == 1:
            r.half_sum[layer] = (
                r.packed[layer, rows(c * half_rows, half_rows)].astype(F32) + r.half_sum[layer].astype(F32)
            ).astype(BF)
            copies = [
                send(1 + d, r.half_sum.at[layer, rows(lax.rem(x + d + 1, TP) * x_rows, x_rows)], r.from_x.at[layer, d], x_devices[d])
                for d in range(3)
            ]
        elif step == 2:
            r.piece[layer] = (
                r.half_sum[layer, rows(x * x_rows, x_rows)].astype(F32)
                + r.from_x[layer, 0].astype(F32)
                + r.from_x[layer, 1].astype(F32)
                + r.from_x[layer, 2].astype(F32)
            ).astype(BF)
            copies = [
                send(4 + d, r.piece.at[layer, rows(lax.rem(y + d + 1, SIDES) * y_rows, y_rows)], r.from_y.at[layer, d], y_devices[d])
                for d in range(3)
            ]
        elif step == 3:
            r.small[layer] = (
                r.piece[layer, rows(y * y_rows, y_rows)].astype(F32)
                + r.from_y[layer, 0].astype(F32)
                + r.from_y[layer, 1].astype(F32)
                + r.from_y[layer, 2].astype(F32)
            ).astype(BF)
            copies = [send(7 + d, r.small.at[layer], r.from_z.at[layer, z], z_devices[d]) for d in range(3)]
            r.from_z[layer, z] = r.small[layer]
        elif step == 4:
            block = rows(c * half_rows + x * x_rows + y * y_rows, y_rows)
            parts = [r.from_z[layer, n].astype(F32) for n in range(4)]
            r.total[layer, block] = (parts[0] + parts[1] + parts[2] + parts[3]).astype(BF)
            copies = [send(10 + d, r.total.at[layer, block], r.total.at[layer, block], y_devices[d]) for d in range(3)]
        elif step == 5:
            block = rows(c * half_rows + x * x_rows, x_rows)
            copies = [send(13 + d, r.total.at[layer, block], r.total.at[layer, block], x_devices[d]) for d in range(3)]
        elif step == 6:
            block = rows(c * half_rows, half_rows)
            copies = [send(16, r.total.at[layer, block], r.total.at[layer, block], partner)]
        else:
            copies = []
        summing[layer, step] = start(copies)

    def to_all(n, source, target):
        place_here = sequence * 2 + c
        turned_rows = jnp.concatenate([source, jnp.zeros((HALF, 32), F32)], axis=1).T[:SIDE_W]
        source = (r.start_own, r.cot_own)[n]
        source[...] = turned_rows
        block = target.at[:, pl.ds(pl.multiple_of(place_here * HALF, HALF), HALF)]
        for d in range(1, TP):
            device = {"tp": lax.rem(x + d, TP), "batch": chip(y, z, parity)}
            start([remote(source, block, r.all_s.at[n, d], r.all_r.at[n, place_here], device)])
        here = pltpu.make_async_copy(source, block, r.all_own.at[n])
        over = remote(source, block, r.all_s.at[n, 0], r.all_r.at[n, place_here], partner)

        @pl.when(stays)
        def _():
            here.start()

        @pl.when(jnp.logical_not(stays))
        def _():
            over.start()

        def finish():
            for m in range(4):
                piece = target.at[:, m * HALF : (m + 1) * HALF]
                own = stays & (place_here == m)
                got = remote(source, piece, r.all_s.at[n, 0], r.all_r.at[n, m], partner)

                @pl.when(jnp.logical_not(own))
                def _():
                    got.wait_recv()

            @pl.when(stays)
            def _():
                here.wait()

            @pl.when(jnp.logical_not(stays))
            def _():
                over.wait_send()

        pending.append(finish)

    def give_back(n, source, target):
        here = pltpu.make_async_copy(source, target, r.back_own.at[n])
        over = remote(source, target, r.back_s.at[n], r.back_r.at[n], across)

        @pl.when(stays)
        def _():
            here.start()

        @pl.when(jnp.logical_not(stays))
        def _():
            over.start()

        def finish():
            @pl.when(stays)
            def _():
                here.wait()

            @pl.when(jnp.logical_not(stays))
            def _():
                over.wait()

        pending.append(finish)

    arrived(early)
    for copy in small_loads:
        copy.wait()
    make_base()
    make_table(0, 6)
    make_table(6, 12)
    r.packed[...] = jnp.zeros_like(r.packed)
    lay_out_side()
    gather("B0", "A2", "QB", "B1", "A3", "C0")

    @pl.when(stays)
    def _():
        tokens_here.start()

    @pl.when(jnp.logical_not(stays))
    def _():
        tokens_over.start()

    gather("B2", "A4", "VA", "RA", "QE", "C1", "QF", "D0", "B3", "A5", "C2", "D1", "B4", "E0", "VB", "F0", "RB", "D2")
    for copy in side_loads + weight_loads:
        copy.wait()
    r.state[0] = transposed(jnp.where(stays, r.start_own[...], r.start_got[...]))
    r.grad_side[2] = transposed(jnp.where(stays, r.cot_own[...], r.cot_got[...]))

    @pl.when(stays)
    def _():
        tokens_here.wait()

    @pl.when(jnp.logical_not(stays))
    def _():
        tokens_over.wait()

    project_begin(0, r.tokens[...].astype(F32))
    project_one(0)(0)
    gather("C3")
    loop(1, 4, project_one(0))
    gather("E1")
    loop(0, 2, attend_one(0))
    gather("B5", "WA")
    attend_one(0)(2)
    gather("C4")
    attend_one(0)(3)
    gather("VE", "F1", "RE", "E2", "D3", "VF", "C5", "RF")
    feed_begin(0, r.tokens[...].astype(F32))
    gather("WB", "F2")
    feed_one(0)(0)
    gather("D4")
    feed_one(0)(1)
    gather("E3")
    loop(2, 4, feed_one(0))
    gather("D5", "WE")
    feed_finish(0)
    project_begin(1, r.residual[...])
    side_begin(0)
    gather("F3")
    project_one(1)(0)
    gather("E4", "WF")
    loop(1, 4, project_one(1))
    loop(0, 2, attend_one(1), side_attend_one(0))
    gather("E5", "F4")
    loop(2, 4, attend_one(1), side_attend_one(0))
    side_attend_finish(0)
    feed_begin(1, r.residual[...])
    loop(0, 4, hidden_one(1))
    gather("F5")
    loop(0, 4, outer_one(1))
    feed_finish(1)
    give_back(0, r.low.at[1], r.backbone_out)
    side_begin(1)
    loop(0, 4, side_attend_one(1))
    side_attend_finish(1)
    to_all(0, r.state[2], r.side_out)
    side_back_begin(1)
    loop(0, 4, side_back_one(1))
    side_end(1)
    sum_step(1, 0)
    side_back_begin(0)
    sum_step(1, 1)
    feed_back_begin(1)
    loop(0, TP, feed_back_one(1), side_back_one(0))
    sum_step(1, 2)
    side_end(0)
    sum_step(0, 0)
    feed_back_finish(1)
    loop(0, 1, attend_back_one(1))
    sum_step(0, 1)
    sum_step(1, 3)
    loop(1, TP, attend_back_one(1))
    sum_step(1, 4)
    r.upper[...] = project_back(1, r.residual[...])
    sum_step(0, 2)
    feed_back_begin(0)
    loop(0, 2, feed_back_one(0))
    sum_step(0, 3)
    sum_step(1, 5)
    loop(2, TP, feed_back_one(0))
    feed_back_finish(0)
    sum_step(0, 4)
    wait_sends(lambda s: dkv_copy(1, s))
    loop(0, 2, attend_back_one(0))
    sum_step(0, 5)
    sum_step(1, 6)
    loop(2, TP, attend_back_one(0))
    pending.append(lambda: wait_sends(lambda s: dkv_copy(0, s)))
    to_all(1, r.grad_side[0], r.grad_start)
    last = project_back(0, r.tokens[...].astype(F32))
    sum_step(0, 6)
    r.normed[...] = last.astype(BF)
    give_back(1, r.normed, r.grad)
    sum_step(1, 7)
    sum_step(0, 7)
    for finish in pending:
        finish()


def network(arrays):
    anywhere, vmem = pl.BlockSpec(memory_space=pl.ANY), pl.BlockSpec(memory_space=pltpu.VMEM)
    smem = pl.BlockSpec(memory_space=pltpu.SMEM)
    dma = pltpu.SemaphoreType.DMA
    return pl.pallas_call(
        network_kernel,
        out_shape=[shape(dims, dtype) for dims, dtype, _ in OUTPUTS.values()],
        in_specs=[smem if name == "lengths" else anywhere for name in INPUTS],
        out_specs=[anywhere if far else vmem for _, _, far in OUTPUTS.values()],
        scratch_shapes=[pltpu.VMEM(dims, dtype) for dims, dtype in (BUFFERS | SMALL).values()]
        + [dma(dims) for dims in SEMAPHORES.values()],
        compiler_params=pltpu.CompilerParams(
            collective_id=0, has_side_effects=True, vmem_limit_bytes=VMEM_BYTES
        ),
    )(*[arrays[name] for name in INPUTS])


def per_device(
    inputs, side_start, lengths, offset_bias, gain_attn, w_query, w_key, w_value, w_out, gain_ffn, w_inner,
    w_outer, narrowing_weight, gate_logit, side_gain1, side_qkv, side_proj, side_gain2, side_inner, side_outer,
    side_cotangent,
):
    def turned(array):
        return jnp.swapaxes(array, -1, -2)

    arrays = dict(
        inputs=inputs,
        side_start=turned(side_start),
        side_cotangent=turned(side_cotangent),
        lengths=lengths,
        bias=offset_bias,
        gain_attn=gain_attn,
        gain_ffn=gain_ffn,
        w_query=turned(w_query),
        w_key=turned(w_key),
        w_value=turned(w_value),
        w_inner=w_inner,
        w_outer=w_outer,
        w_out=w_out,
        narrow=turned(narrowing_weight),
        gate=gate_logit,
        gain1=side_gain1,
        gain2=side_gain2,
        side_qkv=side_qkv,
        proj=side_proj,
        side_inner=side_inner,
        side_outer=turned(side_outer),
    )
    results = network(arrays)
    outs = [
        shape((HALF, WIDTH), BF),
        shape((SIDE_W, 4 * HALF), F32),
        shape((HALF, WIDTH), F32),
        shape((SIDE_W, 4 * HALF), F32),
        shape((2, SIDE_W, WIDTH), F32),
        shape((2, SIDE_W), F32),
        shape((2, SIDE_W), F32),
        shape((2, SIDE_W, 3 * SIDE_W), F32),
        shape((2, SIDE_W, SIDE_W), F32),
        shape((2, SIDE_W), F32),
        shape((2, SIDE_W, SIDE_FF), F32),
        shape((2, SIDE_W, SIDE_FF), F32),
    ]
    results = call(
        results_kernel,
        (1,),
        [whole(array.shape) for array in results],
        [whole(out.shape) for out in outs],
        outs,
        nbytes=6 * 10**6,
    )(*results)
    backbone_out, side_out, grad, grad_start, down, *small, outer = results
    return (backbone_out, turned(side_out), grad, turned(grad_start), turned(down), *small, turned(outer))


def solution(mesh):
    in_specs = (
        P(("batch", "tp"), None),
        P("batch", None),
        P("batch"),
        P(),
        P(),
        P(None, None, "tp"),
        P(None, None, "tp"),
        P(None, None, "tp"),
        P(None, "tp", None),
        P(),
        P(None, None, "tp"),
        P(None, "tp", None),
        P(),
        P(),
        P(),
        P(),
        P(),
        P(),
        P(),
        P(),
        P("batch", None),
    )
    out_specs = (
        P(("batch", "tp"), None),
        P("batch", None),
        P(("batch", "tp"), None),
        P("batch", None),
        P(),
        P(),
        P(),
        P(),
        P(),
        P(),
        P(),
        P(),
    )
    return jax.shard_map(per_device, mesh=mesh, in_specs=in_specs, out_specs=out_specs, check_vma=False)
```

```python
from functools import partial
import math

import jax
import jax.numpy as jnp
from jax import lax
from jax.experimental import pallas as pl
from jax.experimental.pallas import tpu as pltpu
from jax.sharding import PartitionSpec as P


BF = jnp.bfloat16
F32 = jnp.float32
EPSILON = 1e-06
NEGATIVE = -1e30
HIGHEST = lax.Precision.HIGHEST
MESH = pl.DeviceIdType.MESH
TP = 4
SIDES = 4
HALF = 256
WIDTH = 768
SIDE_W = 96
SIDE_FF = 384
SIDE_SCALE = 1.0 / math.sqrt(8)
GELU_K = math.sqrt(2.0 / math.pi)
VMEM_BYTES = 63 * 1024 * 1024

A_PROJ, A_INNER, A_OUTER, B_QKV, B_DOWN, LAYER_ROWS = 0, 96, 384, 672, 960, 1536


def dot(a, b, ca, cb, precision=None):
    return lax.dot_general(
        a, b, (((ca,), (cb,)), ((), ())), preferred_element_type=F32, precision=precision
    )


def nn(a, b, precision=None):
    return dot(a, b, 1, 0, precision)


def nt(a, b, precision=None):
    return dot(a, b, 1, 1, precision)


def tn(a, b, precision=None):
    return dot(a, b, 0, 0, precision)


def rms_scale(values):
    return lax.rsqrt(jnp.mean(values * values, axis=-1, keepdims=True) + EPSILON)


def rms_back(values, gain_row, grad):
    scale = rms_scale(values)
    scaled = grad * gain_row
    inner = jnp.mean(scaled * values, axis=-1, keepdims=True)
    return scale * scaled - values * (scale * scale * scale * inner)


def gelu_parts(hidden):
    square = hidden * hidden
    tanh = jnp.tanh(GELU_K * hidden * (1.0 + 0.044715 * square))
    plus = 0.5 * (1.0 + tanh)
    slope = plus + (0.5 * GELU_K) * hidden * (1.0 - tanh * tanh) * (1.0 + (3 * 0.044715) * square)
    return hidden * plus, slope


def lane_mask(test):
    lanes = lax.broadcasted_iota(jnp.int32, (HALF, 128), 1)
    return jnp.where(test(lanes), 1.0, 0.0).astype(BF)


def row_block(shape, index_map):
    return pl.BlockSpec(shape, index_map)


def whole(shape):
    return pl.BlockSpec(shape, lambda *_: (0,) * len(shape))


def call(kernel, grid, in_specs, out_specs, out_shape, scratch=(), prefetch=0, flops=0, nbytes=0):
    return pl.pallas_call(
        kernel,
        grid_spec=pltpu.PrefetchScalarGridSpec(
            num_scalar_prefetch=prefetch,
            grid=grid,
            in_specs=in_specs,
            out_specs=out_specs,
            scratch_shapes=scratch,
        ),
        out_shape=out_shape,
        compiler_params=pltpu.CompilerParams(vmem_limit_bytes=VMEM_BYTES),
        cost_estimate=pl.CostEstimate(flops=flops, bytes_accessed=nbytes, transcendentals=0),
    )


def shape(dims, dtype):
    return jax.ShapeDtypeStruct(dims, dtype)


def results_kernel(
    out_in, side_in, start_in, grad_in, total,
    out, side, grad, start, down_out, gate_out, gain1_out, qkv_out, proj_out, gain2_out, inner_out, outer_out,
):
    out[...] = out_in[...]
    side[...] = side_in[...]
    start[...] = start_in[...]
    grad[...] = grad_in[...].astype(F32)
    for layer in range(2):

        def part(first, count, layer=layer):
            return total[layer, first : first + count].astype(F32)

        proj = part(A_PROJ, 96)
        proj_out[layer] = proj[:, :SIDE_W]
        small = jnp.concatenate([proj, jnp.zeros((32, 128), F32)], axis=0).T[96:104]
        gate_out[layer : layer + 1] = small[0:1, :SIDE_W]
        gain1_out[layer : layer + 1] = small[1:2, :SIDE_W]
        gain2_out[layer : layer + 1] = small[2:3, :SIDE_W]
        for n in range(3):
            lanes = slice(n * 128, (n + 1) * 128)
            inner_out[layer, :, lanes] = part(A_INNER + n * 96, 96)
            outer_out[layer, :, lanes] = part(A_OUTER + n * 96, 96)
        triple = [part(B_QKV + n * 96, 96)[:, :SIDE_W] for n in range(3)]
        qkv_out[layer] = jnp.concatenate(triple, axis=1)
        for n in range(6):
            down_out[layer, :, n * 128 : (n + 1) * 128] = part(B_DOWN + n * 96, 96)


def head_parts(q, dm=None):
    low = lane_mask(lambda lanes: lanes < 64)
    high = lane_mask(lambda lanes: lanes >= 64)
    queries = [q[:, :128] * low, q[:, :128] * high, q[:, 128:]]
    if dm is None:
        return queries
    return queries, [dm[:, :128] * low, dm[:, :128] * high, dm[:, 128:]]


def softmax_parts(scores):
    top = jnp.max(scores, axis=0, keepdims=True)
    exps = jnp.exp(scores - top)
    total = jnp.sum(exps, axis=0, keepdims=True)
    return exps.astype(BF), 1.0 / total, top + jnp.log(total)


def score_gradients(scores, lse, dprobs):
    probs = jnp.exp(scores - lse)
    inner = jnp.sum(probs * dprobs, axis=0, keepdims=True)
    return probs.astype(BF), (probs * (dprobs - inner)).astype(BF)


def split_pack(values, low_test):
    high = values.astype(BF)
    low = (values - high.astype(F32)).astype(BF)
    mask = lane_mask(low_test)
    return high * (1 - mask) + low * mask


def of_head(j, blocks):
    def test(lanes):
        hit = (lanes >= blocks[0] * 24 + j * 8) & (lanes < blocks[0] * 24 + j * 8 + 8)
        for n in blocks[1:]:
            hit = hit | ((lanes >= n * 24 + j * 8) & (lanes < n * 24 + j * 8 + 8))
        return hit

    return lane_mask(test)


def parts(values):
    high = values.astype(BF)
    return high, (values - high.astype(F32)).astype(BF)


def fine(product, left, right):
    left_high, left_low = parts(left)
    right_high, right_low = parts(right)
    return product(left_high, right_high) + product(left_low, right_high) + product(left_high, right_low)


def transposed(rows):
    return jnp.concatenate([rows, jnp.zeros((32, rows.shape[1]), rows.dtype)], axis=0).T[:, :SIDE_W]


INPUTS = [
    "inputs", "side_start", "side_cotangent", "lengths", "bias", "gain_attn", "gain_ffn", "w_query", "w_key", "w_value",
    "w_inner", "w_outer", "w_out", "narrow", "gate", "gain1", "gain2", "side_qkv", "proj", "side_inner", "side_outer",
]
SMALL = {
    "bias": ((12, 4 * HALF - 1), BF),
    "gain_attn": ((2, WIDTH), BF),
    "gain_ffn": ((2, WIDTH), BF),
    "narrow": ((2, SIDE_W, WIDTH), BF),
    "gate": ((2, SIDE_W), F32),
    "gain1": ((2, SIDE_W), F32),
    "gain2": ((2, SIDE_W), F32),
    "side_qkv": ((2, SIDE_W, 3 * SIDE_W), F32),
    "proj": ((2, SIDE_W, SIDE_W), F32),
    "side_inner": ((2, SIDE_W, SIDE_FF), F32),
    "side_outer": ((2, SIDE_W, SIDE_FF), F32),
}

OUTPUTS = {
    "backbone_out": ((HALF, WIDTH), BF, True),
    "side_out": ((SIDE_W, 4 * HALF), F32, True),
    "grad_start": ((SIDE_W, 4 * HALF), F32, True),
    "grad": ((HALF, WIDTH), BF, True),
    "total": ((2, LAYER_ROWS, 128), BF, False),
}

BUFFERS = {
    "qkv": ((2, TP, 576, WIDTH), BF),
    "inner": ((2, TP, WIDTH, WIDTH), BF),
    "outer": ((2, TP, WIDTH, WIDTH), BF),
    "out": ((2, TP, 192, WIDTH), BF),
    "tokens": ((HALF, WIDTH), BF),
    "start_own": ((SIDE_W, HALF), F32),
    "start_got": ((SIDE_W, HALF), F32),
    "cot_own": ((SIDE_W, HALF), F32),
    "cot_got": ((SIDE_W, HALF), F32),
    "span_own": ((8, HALF), F32),
    "span_got": ((8, HALF), F32),
    "wide_bias": ((16, 4 * HALF), BF),
    "wide_query": ((2, SIDE_W, 512), F32),
    "wide_kv": ((2, SIDE_W, 512), F32),
    "back_query": ((2, SIDE_W, SIDE_W), BF),
    "back_kv": ((2, SIDE_W, 256), BF),
    "table": ((12, 2 * HALF, HALF), BF),
    "q": ((2, TP, HALF, 256), BF),
    "kv": ((2, TP, 2, HALF, 384), BF),
    "lse": ((2, TP, 8, HALF), F32),
    "mid": ((2, HALF, WIDTH), F32),
    "slope": ((2, TP, HALF, WIDTH), BF),
    "residual": ((HALF, WIDTH), F32),
    "low": ((2, HALF, WIDTH), BF),
    "down": ((2, HALF, SIDE_W), BF),
    "state": ((3, HALF, SIDE_W), F32),
    "joined": ((2, HALF, SIDE_W), F32),
    "side_mixed": ((2, HALF, SIDE_W), F32),
    "side_q": ((2, 4, HALF, 128), BF),
    "side_kv": ((2, 4, 2, HALF, 128), BF),
    "side_lse": ((2, 4, 8, HALF), F32),
    "normed": ((HALF, WIDTH), BF),
    "acc": ((HALF, WIDTH), F32),
    "grad_side": ((3, HALF, SIDE_W), F32),
    "djoined": ((HALF, SIDE_W), F32),
    "side_dmixed": ((4, HALF, 128), BF),
    "side_dq": ((SIDE_W, HALF), F32),
    "side_dkv": ((4, HALF, 128), F32),
    "side_dkv_sent": ((4, HALF, 128), BF),
    "side_dkv_got": ((2, 4, HALF, 128), BF),
    "ddown": ((2, HALF, SIDE_W), BF),
    "upper": ((HALF, WIDTH), F32),
    "dmixed": ((TP, HALF, 256), BF),
    "dq": ((TP, HALF, 256), BF),
    "dkv": ((TP, HALF, 384), F32),
    "dkv_sent": ((TP, HALF, 384), BF),
    "dkv_got": ((2, TP, HALF, 384), BF),
    "gain2_sum": ((1, SIDE_W), F32),
    "packed": ((2, LAYER_ROWS, 128), BF),
    "half_sum": ((2, LAYER_ROWS // 2, 128), BF),
    "from_x": ((2, 3, LAYER_ROWS // 8, 128), BF),
    "piece": ((2, LAYER_ROWS // 8, 128), BF),
    "from_y": ((2, 3, LAYER_ROWS // 32, 128), BF),
    "small": ((2, LAYER_ROWS // 32, 128), BF),
    "from_z": ((2, 4, LAYER_ROWS // 32, 128), BF),
}

SEMAPHORES = {
    "load": (12 + 11,),
    "early_s": (4,),
    "early_r": (4,),
    "x_s": (6, 6),
    "x_r": (6, 6),
    "yz_s": (6, 12),
    "yz_r": (6, 12),
    "core_s": (6,),
    "core_r": (6,),
    "out_s": (20,),
    "out_r": (20,),
    "kv_s": (2, TP),
    "kv_r": (2, TP),
    "side_kv_s": (2, 4),
    "side_kv_r": (2, 4),
    "dkv_s": (2, TP),
    "dkv_r": (2, TP),
    "side_dkv_s": (2, 4),
    "side_dkv_r": (2, 4),
    "sum_s": (2, 17),
    "sum_r": (2, 17),
    "all_s": (2, 4),
    "all_r": (2, 4),
    "all_own": (2,),
    "back_s": (2,),
    "back_r": (2,),
    "back_own": (2,),
}


class Refs:
    def __init__(self, names, refs):
        self.__dict__.update(zip(names, refs))


def rows(start, count):
    return pl.ds(pl.multiple_of(start, 16), count)


def network_kernel(*refs):
    given = ["given_" + name if name in SMALL else name for name in INPUTS]
    r = Refs(given + list(OUTPUTS) + list(BUFFERS) + list(SMALL) + list(SEMAPHORES), refs)
    x = lax.axis_index("tp")
    b = lax.axis_index("batch")
    c = lax.rem(b, 2)
    z = lax.rem(b // 2, SIDES)
    y = b // (2 * SIDES)
    parity = lax.rem(x, 2)
    stays = parity == c
    sequence = lax.div(x, 2)

    def chip(y_now, z_now, c_now):
        return (y_now * SIDES + z_now) * 2 + c_now

    left, right = {"tp": lax.rem(x + TP - 1, TP)}, {"tp": lax.rem(x + 1, TP)}
    x_devices = [{"tp": lax.rem(x + d, TP)} for d in (1, 2, 3)]
    y_devices = [{"batch": chip(lax.rem(y + d, SIDES), z, c)} for d in (1, 2, 3)]
    z_devices = [{"batch": chip(y, lax.rem(z + d, SIDES), c)} for d in (1, 2, 3)]
    up, down = (y_devices[0], z_devices[0]), (y_devices[2], z_devices[2])
    partner = {"batch": chip(y, z, 1 - c)}
    across = {"tp": x + 1 - 2 * parity, "batch": chip(y, z, 1 - c)}

    pending = []

    def remote(src, dst, send_sem, recv_sem, device):
        return pltpu.make_async_remote_copy(
            src_ref=src, dst_ref=dst, send_sem=send_sem, recv_sem=recv_sem, device_id=device, device_id_type=MESH
        )

    def start(copies):
        for copy in copies:
            copy.start()
            pending.append(copy.wait_send)
        return copies

    def arrived(copies):
        for copy in copies:
            copy.wait_recv()

    def load(n, source, target):
        copy = pltpu.make_async_copy(source, target, r.load.at[n])
        copy.start()
        return copy

    own_lanes = pl.ds(pl.multiple_of(sequence * (2 * HALF) + c * HALF, HALF), HALF)
    sent_lanes = pl.ds(pl.multiple_of(sequence * (2 * HALF) + (1 - c) * HALF, HALF), HALF)
    qkv_loads = [
        load(n, source.at[:, low:high], r.qkv.at[:, 0, place : place + high - low])
        for n, (source, low, high, place) in enumerate((
            (r.w_query, 0, 128, 0),
            (r.w_key, 0, 128, 128),
            (r.w_value, 0, 128, 256),
            (r.w_key, 128, 192, 384),
            (r.w_value, 128, 192, 448),
            (r.w_query, 128, 192, 512),
        ))
    ]
    side_loads = [
        load(6, r.side_start.at[:, own_lanes], r.start_own),
        load(7, r.side_cotangent.at[:, own_lanes], r.cot_own),
    ]
    weight_loads = [
        load(8, r.w_out, r.out.at[:, 0]),
        load(9, r.w_inner, r.inner.at[:, 0]),
        load(10, r.w_outer, r.outer.at[:, 0]),
    ]
    small_loads = [
        load(12 + n, getattr(r, "given_" + name), getattr(r, name)) for n, name in enumerate(SMALL)
    ]
    r.span_own[...] = jnp.full((8, HALF), r.lengths[sequence].astype(F32))
    r.q[:, :, :, 192:] = jnp.zeros((2, TP, HALF, 64), BF)

    barrier = pltpu.get_barrier_semaphore()
    line = [{"tp": lax.rem(x + d, TP), "batch": chip(y, z, core)} for d in (1, 2, 3) for core in (0, 1)]
    for device in [partner] + line + y_devices + z_devices:
        pl.semaphore_signal(barrier, inc=1, device_id=device, device_id_type=MESH)
    pl.semaphore_wait(barrier, 13)

    chunks = [
        chunk
        for layer in range(2)
        for chunk in (
            (r.qkv.at[layer, 0], r.qkv, layer),
            (r.w_inner.at[layer], r.inner, layer),
            (r.w_outer.at[layer], r.outer, layer),
        )
    ]

    def place(k):
        core_rows = 256 if k % 3 == 0 else 384
        low = c * core_rows
        part = core_rows // 8
        return (
            rows(low, core_rows),
            (rows(low + y * part, part), rows(low + core_rows // 2 + z * part, part)),
        )

    direct = {
        "V": (r.w_out.at[0], r.out.at[0], 192, 0, 0),
        "W": (r.w_out.at[1], r.out.at[1], 192, 0, 5),
        "Q": (r.qkv.at[0, 0], r.qkv.at[0], 64, 512, 10),
        "R": (r.qkv.at[1, 0], r.qkv.at[1], 64, 512, 15),
    }
    flying = {}

    def first(k):
        source, target, layer = chunks[k]
        _, blocks = place(k)
        return [
            remote(
                source.at[blocks[path]],
                target.at[layer, slot, blocks[path]],
                r.x_s.at[k, path * 2 + slot - 1],
                r.x_r.at[k, path * 2 + slot - 1],
                device,
            )
            for path in range(2)
            for device, slot in ((right, 2), (left, 1))
        ]

    def relay(k):
        _, target, layer = chunks[k]
        _, (y_block, z_block) = place(k)
        return [
            remote(target.at[layer, 2, y_block], target.at[layer, 3, y_block], r.x_s.at[k, 4], r.x_r.at[k, 4], right),
            remote(target.at[layer, 1, z_block], target.at[layer, 3, z_block], r.x_s.at[k, 5], r.x_r.at[k, 5], left),
        ]

    def spread(k, part):
        _, target, layer = chunks[k]
        _, blocks = place(k)
        slots = pl.ds(1, 2) if part == 0 else pl.ds(3, 1)
        out = []
        for path in range(2):
            block = target.at[layer, slots, blocks[path]]
            for way, device in enumerate((up[path], down[path])):
                n = part * 4 + path * 2 + way
                out.append(remote(block, block, r.yz_s.at[k, n], r.yz_r.at[k, n], device))
        return out

    def spread_relay(k):
        _, target, layer = chunks[k]
        out = []
        for path in range(2):
            part = 32 if k % 3 == 0 else 48
            cut = 32 if part == 48 and (k + path) % 2 == 0 else 16
            for n, (step, device, low, high) in enumerate(
                ((SIDES - 1, up[path], 0, cut), (1, down[path], cut, part))
            ):
                start_row = c * part * 8 + path * part * 4 + lax.rem((y, z)[path] + step, SIDES) * part
                block = target.at[layer, pl.ds(1, 3), rows(start_row + low, high - low)]
                m = 8 + path * 2 + n
                out.append(remote(block, block, r.yz_s.at[k, m], r.yz_r.at[k, m], device))
        return out

    def swap(k):
        _, target, layer = chunks[k]
        mine, _ = place(k)
        block = target.at[layer, pl.ds(1, 3), mine]
        return [remote(block, block, r.core_s.at[k], r.core_r.at[k], partner)]

    def straight(kind, step):
        source, target, count, base, sem = direct[kind]
        base = base + c * (count // 2)
        mine, low, high = rows(base, count // 2), rows(base, count // 4), rows(base + count // 4, count // 4)

        def go(n, block_from, block_to, device):
            return remote(block_from, block_to, r.out_s.at[sem + n], r.out_r.at[sem + n], device)

        if step == "A":
            return [
                go(0, source.at[mine], target.at[2, mine], right),
                go(1, source.at[mine], target.at[1, mine], left),
            ]
        if step == "B":
            return [
                go(2, target.at[2, low], target.at[3, low], right),
                go(3, target.at[1, high], target.at[3, high], left),
            ]
        block = target.at[pl.ds(1, 3), mine]
        return [go(4, block, block, partner)]

    def gather(*steps):
        for step in steps:
            kind, k = step[0], step[1:]
            if kind in direct:
                if k != "A":
                    arrived(flying[kind])
                flying[kind] = start(straight(kind, k)) if k != "F" else []
                continue
            k = int(k)
            if kind == "A":
                flying["A", k] = start(first(k))
            elif kind == "B":
                arrived(flying["A", k])
                flying["B", k] = start(relay(k))
                flying["S", k] = start(spread(k, 0))
            elif kind == "C":
                arrived(flying["B", k])
                flying["S", k] += start(spread(k, 1))
            elif kind == "D":
                arrived(flying["S", k])
                flying["D", k] = start(spread_relay(k))
            elif kind == "E":
                arrived(flying["D", k])
                flying["E", k] = start(swap(k))
            else:
                arrived(flying["E", k])

    early = [
        remote(r.span_own, r.span_got, r.early_s.at[0], r.early_r.at[0], partner),
        remote(r.side_start.at[:, sent_lanes], r.start_got, r.early_s.at[1], r.early_r.at[1], partner),
        remote(r.side_cotangent.at[:, sent_lanes], r.cot_got, r.early_s.at[2], r.early_r.at[2], partner),
    ]
    tokens_here = pltpu.make_async_copy(r.inputs, r.tokens, r.load.at[11])
    tokens_over = remote(r.inputs, r.tokens, r.early_s.at[3], r.early_r.at[3], across)

    for copy in qkv_loads:
        copy.wait()
    gather("A0")
    gather("QA")
    gather("A1")
    start(early)

    def table_slot(shard):
        turn = lax.rem(shard + TP - x, TP)
        return turn + jnp.where(turn == 2, 1, 0) - jnp.where(turn == 3, 1, 0)

    def make_base():
        row = lax.broadcasted_iota(jnp.int32, (HALF, HALF), 0)
        column = lax.broadcasted_iota(jnp.int32, (HALF, HALF), 1)
        reverse = jnp.where(row + column == HALF - 1, 1.0, 0.0).astype(BF)
        r.wide_bias[...] = jnp.zeros_like(r.wide_bias)
        r.wide_bias[:12, : 4 * HALF - 1] = r.bias[...]
        turned = [nn(r.wide_bias[:, n * HALF : (n + 1) * HALF], reverse) for n in range(4)]
        other = [jnp.where(c == 0, turned[n + 2], turned[n]) for n in range(2)]
        for head in range(12):
            one = slice(head, head + 1)
            r.acc[16 * head : 16 * head + 1, :HALF] = turned[1][one]
            r.acc[16 * head : 16 * head + 1, HALF : 2 * HALF] = turned[2][one]
            r.acc[16 * head + 8 : 16 * head + 9, :HALF] = other[0][one]
            r.acc[16 * head + 8 : 16 * head + 9, HALF : 2 * HALF] = other[1][one]

    def make_table(low, high):
        row = lax.broadcasted_iota(jnp.int32, (HALF, HALF), 0)
        length = jnp.where(stays, r.span_own[0:1], r.span_got[0:1])
        place = row.astype(F32)

        def one(head, carry):
            slot = table_slot(lax.div(head, 3)) * 3 + lax.rem(head, 3)
            for side in range(2):
                first_key = (c if side == 0 else 1 - c) * HALF
                spread_row = jnp.broadcast_to(
                    r.acc[pl.ds(head * 16 + side * 8, 1), : 2 * HALF], (HALF, 2 * HALF)
                )
                rolled = pltpu.roll(spread_row, 0, 1, stride=1, stride_axis=0)[:, :HALF]
                counts = place + first_key.astype(F32) < length
                r.table[slot, side * HALF : (side + 1) * HALF] = jnp.where(counts, rolled, NEGATIVE).astype(BF)
            return carry

        lax.fori_loop(low, high, one, 0)

    def ones(test):
        return jnp.where(test, 1.0, 0.0)

    def to_lanes(g):
        row = lax.broadcasted_iota(jnp.int32, (SIDE_W, 128), 0)
        lane = lax.broadcasted_iota(jnp.int32, (SIDE_W, 128), 1)
        thrice = lane - jnp.where(lane >= 24, 24, 0) - jnp.where(lane >= 48, 24, 0)
        twice = lane - 72 - jnp.where(lane >= 96, 24, 0)
        keys = ones((row == thrice + g * 24) & (lane < 72))
        return keys, ones((row == twice + g * 24) & (lane >= 72) & (lane < 120))

    def from_lanes(g):
        row = lax.broadcasted_iota(jnp.int32, (128, 128), 0)
        column = lax.broadcasted_iota(jnp.int32, (128, 128), 1)
        keys = ones((row < 24) & (column == row + g * 24))
        values = ones((row >= 72) & (row < 96) & (column == row - 72 + g * 24))
        return jnp.concatenate([keys, values], axis=1).astype(BF)

    def lay_out_side():
        for g in range(4):
            lanes = slice(g * 128, (g + 1) * 128)
            to_keys, to_values = to_lanes(g)
            for layer in range(2):
                weight = r.side_qkv[layer]
                query, key, value = weight[:, :96], weight[:, 96:192], weight[:, 192:]
                r.wide_query[layer, :, lanes] = nn(query, to_keys, HIGHEST) * SIDE_SCALE
                r.wide_kv[layer, :, lanes] = nn(key, to_keys, HIGHEST) + nn(value, to_values, HIGHEST)
        for layer in range(2):
            weight = r.side_qkv[layer]
            r.back_query[layer] = (weight[:, :96] * SIDE_SCALE).astype(BF)
            r.back_kv[layer] = jnp.zeros((SIDE_W, 256), BF)
            r.back_kv[layer, :, :96] = weight[:, 96:192].astype(BF)
            r.back_kv[layer, :, 128:224] = weight[:, 192:].astype(BF)

    def loop(low, high, *bodies):
        def one(s, carry):
            for body in bodies:
                body(s)
            return carry

        lax.fori_loop(low, high, one, 0)

    def project_begin(layer, residual):
        r.normed[...] = (residual * rms_scale(residual) * r.gain_attn[layer : layer + 1].astype(F32)).astype(BF)
        pending.append(lambda: wait_sends(lambda s: kv_copy(layer, s)))

    def project_one(layer):
        def one(s):
            out = nt(r.normed[...], r.qkv[layer, s])
            r.kv[layer, s, 0] = out[:, 128:512].astype(BF)
            kv_copy(layer, s).start()
            r.q[layer, s, :, :128] = (out[:, :128] * 0.125).astype(BF)
            r.q[layer, s, :, 128:192] = (out[:, 512:] * 0.125).astype(BF)

        return one

    def kv_copy(layer, s):
        return remote(r.kv.at[layer, s, 0], r.kv.at[layer, s, 1], r.kv_s.at[layer, s], r.kv_r.at[layer, s], partner)

    def wait_sends(copy_of):
        def one(s, carry):
            copy_of(s).wait_send()
            return carry

        lax.fori_loop(0, 4, one, 0)

    def slab(layer, s, n):
        return r.kv[layer, s, :, :, n * 128 : (n + 1) * 128].reshape(2 * HALF, 128)

    def attend_one(layer):
        def one(s):
            kv_copy(layer, s).wait_recv()
            queries = head_parts(r.q[layer, s])
            keys, values = [slab(layer, s, 0), slab(layer, s, 2)], [slab(layer, s, 1), slab(layer, s, 2)]
            scores = [nt(keys[j // 2], queries[j]) + r.table[s * 3 + j].astype(F32) for j in range(3)]
            parts = [softmax_parts(score) for score in scores]
            heads = [tn(values[j // 2], parts[j][0]) for j in range(3)]
            heads = [(heads[j][:64] if j == 0 else heads[j][64:]) * parts[j][1] for j in range(3)]
            for j in range(3):
                r.lse[layer, s, j : j + 1] = parts[j][2]
            r.dq[s, :, :128] = jnp.concatenate(heads[:2], axis=0).T.astype(BF)
            third = jnp.concatenate([heads[2], jnp.zeros_like(heads[2])], axis=0).T
            r.dq[s, :, 128:192] = third[:, :64].astype(BF)

        return one

    def feed_begin(layer, residual):
        middle = residual
        for s in range(TP):
            middle = middle + nn(r.dq[s, :, :192], r.out[layer, s])
        r.mid[layer] = middle
        r.acc[...] = middle
        r.normed[...] = (middle * rms_scale(middle) * r.gain_ffn[layer : layer + 1].astype(F32)).astype(BF)

    def feed_one(layer):
        def one(s):
            active, slope = gelu_parts(nn(r.normed[...], r.inner[layer, s]))
            r.slope[layer, s] = slope.astype(BF)
            r.acc[...] += nn(active.astype(BF), r.outer[layer, s])

        return one

    def hidden_one(layer):
        def one(s):
            active, slope = gelu_parts(nn(r.normed[...], r.inner[layer, s]))
            r.slope[layer, s] = slope.astype(BF)
            r.dkv_got[0, s] = active[:, :384].astype(BF)
            r.dkv_got[1, s] = active[:, 384:].astype(BF)

        return one

    def outer_one(layer):
        def one(s):
            active = jnp.concatenate([r.dkv_got[0, s], r.dkv_got[1, s]], axis=1)
            r.acc[...] += nn(active, r.outer[layer, s])

        return one

    def feed_finish(layer):
        out = r.acc[...]
        low = out.astype(BF)
        if layer == 0:
            r.residual[...] = out
        r.low[layer] = low
        r.down[layer] = nt(low, r.narrow[layer]).astype(BF)

    def side_kv_copy(layer, g):
        return remote(
            r.side_kv.at[layer, g, 0], r.side_kv.at[layer, g, 1],
            r.side_kv_s.at[layer, g], r.side_kv_r.at[layer, g], partner,
        )

    def side_begin(layer):
        mix = jax.nn.sigmoid(r.gate[layer : layer + 1])
        joined = mix * r.down[layer].astype(F32) + (1.0 - mix) * r.state[layer]
        r.joined[layer] = joined
        normed = joined * rms_scale(joined) * r.gain1[layer : layer + 1]
        kv = fine(nn, normed, r.wide_kv[layer])
        for g in range(4):
            r.side_kv[layer, g, 0] = split_pack(
                kv[:, g * 128 : (g + 1) * 128], lambda n: ((n >= 48) & (n < 72)) | (n >= 96)
            )
            side_kv_copy(layer, g).start()
        q = fine(nn, normed, r.wide_query[layer])
        for g in range(4):
            r.side_q[layer, g] = split_pack(q[:, g * 128 : (g + 1) * 128], lambda n: (n >= 24) & (n < 48))
        pending.append(lambda: wait_sends(lambda g: side_kv_copy(layer, g)))

    def side_attend_one(layer):
        def one(g):
            side_kv_copy(layer, g).wait_recv()
            kv = r.side_kv[layer, g].reshape(2 * HALF, 128)
            q = r.side_q[layer, g]
            slot = table_slot(g) * 3
            scores = [nt(kv, q * of_head(j, (0, 1, 2))) + r.table[slot + j].astype(F32) for j in range(3)]
            parts = [softmax_parts(score) for score in scores]
            heads = [tn(kv, parts[j][0]) for j in range(3)]
            for j in range(3):
                both = heads[j][72 + j * 8 : 80 + j * 8] + heads[j][96 + j * 8 : 104 + j * 8]
                r.side_dq[pl.ds(pl.multiple_of(g * 24 + j * 8, 8), 8)] = both * parts[j][1]
                r.side_lse[layer, g, j : j + 1] = parts[j][2]

        return one

    def side_attend_finish(layer):
        mixed = transposed(r.side_dq[...])
        r.side_mixed[layer] = mixed
        kept = side_second(layer, mixed)
        joined, _, _, active, _ = kept
        r.state[layer + 1] = joined + fine(nt, active, r.side_outer[layer])
        return kept

    def side_second(layer, mixed):
        joined = r.joined[layer] + fine(nn, mixed, r.proj[layer])
        unit = joined * rms_scale(joined)
        normed = unit * r.gain2[layer : layer + 1]
        return (joined, unit, normed) + gelu_parts(fine(nn, normed, r.side_inner[layer]))

    def side_dkv_copy(layer, g):
        return remote(
            r.side_dkv_sent.at[g], r.side_dkv_got.at[layer, g],
            r.side_dkv_s.at[layer, g], r.side_dkv_r.at[layer, g], partner,
        )

    def side_back_begin(layer, kept=None):
        grad = r.grad_side[layer + 1]
        grad_low = grad.astype(BF)
        mixed = r.side_mixed[layer]
        gain = r.gain2[layer : layer + 1]
        joined, unit, normed, active, slope = kept or side_second(layer, mixed)
        dhidden = (nn(grad_low, r.side_outer[layer].astype(BF)) * slope).astype(BF)
        dnormed = nt(dhidden, r.side_inner[layer].astype(BF))
        djoined = grad + rms_back(joined, gain, dnormed)
        r.djoined[...] = djoined
        djoined_low = djoined.astype(BF)
        dmixed_low = nt(djoined_low, r.proj[layer].astype(BF)).astype(BF)
        for g in range(4):
            r.side_dmixed[g] = nn(dmixed_low, to_lanes(g)[1].astype(BF)).astype(BF)
        r.packed[layer, A_PROJ : A_PROJ + SIDE_W, :SIDE_W] = tn(mixed.astype(BF), djoined_low).astype(BF)
        inner_sum = tn(normed.astype(BF), dhidden).astype(BF)
        outer_sum = tn(grad_low, active.astype(BF)).astype(BF)
        for n in range(3):
            lanes = slice(n * 128, (n + 1) * 128)
            r.packed[layer, A_INNER + n * 96 : A_INNER + (n + 1) * 96] = inner_sum[:, lanes]
            r.packed[layer, A_OUTER + n * 96 : A_OUTER + (n + 1) * 96] = outer_sum[:, lanes]
        r.gain2_sum[...] = jnp.sum(dnormed * unit, axis=0, keepdims=True)
        if layer == 0:
            wait_sends(lambda g: side_dkv_copy(1, g))

    def side_back_one(layer):
        def one(g):
            kv = r.side_kv[layer, g].reshape(2 * HALF, 128)
            q, dm = r.side_q[layer, g], r.side_dmixed[g]
            slot = table_slot(g) * 3
            scores = [nt(kv, q * of_head(j, (0, 1, 2))) + r.table[slot + j].astype(F32) for j in range(3)]
            dprobs = [nt(kv, dm * of_head(j, (3, 4))) for j in range(3)]
            left, right_parts = [], []
            for j in range(3):
                p, ds = score_gradients(scores[j], r.side_lse[layer, g, j : j + 1], dprobs[j])
                dq = tn(kv, ds)
                r.side_dq[pl.ds(pl.multiple_of(g * 24 + j * 8, 8), 8)] = (
                    dq[j * 8 : j * 8 + 8] + dq[48 + j * 8 : 56 + j * 8]
                )
                left += [ds, p]
                right_parts += [q * of_head(j, (0,)), dm * of_head(j, (3,))]
            dkv = nn(jnp.concatenate(left, axis=1), jnp.concatenate(right_parts, axis=0))
            r.side_dkv_sent[g] = dkv[HALF:].astype(BF)
            side_dkv_copy(layer, g).start()
            r.side_dkv[g] = dkv[:HALF]

        if layer == 0:
            pending.append(lambda: wait_sends(lambda g: side_dkv_copy(layer, g)))
        return one

    def side_end(layer):
        joined = r.joined[layer]
        gain = r.gain1[layer : layer + 1]
        unit = joined * rms_scale(joined)
        normed_low = (unit * gain).astype(BF)
        dq = transposed(r.side_dq[...]).astype(BF)
        dkv = jnp.zeros((HALF, 256), F32)
        for g in range(4):
            side_dkv_copy(layer, g).wait_recv()
            both = (r.side_dkv[g] + r.side_dkv_got[layer, g].astype(F32)).astype(BF)
            dkv = dkv + nn(both, from_lanes(g))
        dkv = dkv.astype(BF)
        dnormed = nt(dq, r.back_query[layer]) + nt(dkv, r.back_kv[layer])
        djoined = r.djoined[...] + rms_back(joined, gain, dnormed)
        mix = jax.nn.sigmoid(r.gate[layer : layer + 1])
        ddown = (mix * djoined).astype(BF)
        r.ddown[layer] = ddown
        r.grad_side[layer] = (1.0 - mix) * djoined
        change = r.down[layer].astype(F32) - r.state[layer]
        gate_sum = jnp.sum(djoined * change, axis=0, keepdims=True) * mix * (1.0 - mix)
        gain_sum = jnp.sum(dnormed * unit, axis=0, keepdims=True)
        r.packed[layer, B_QKV : B_QKV + 96, :SIDE_W] = (tn(normed_low, dq) * SIDE_SCALE).astype(BF)
        kv_sum = tn(normed_low, dkv).astype(BF)
        r.packed[layer, B_QKV + 96 : B_QKV + 192] = kv_sum[:, :128]
        r.packed[layer, B_QKV + 192 : B_QKV + 288] = kv_sum[:, 128:]
        down_sum = tn(ddown, r.low[layer]).astype(BF)
        for n in range(6):
            r.packed[layer, B_DOWN + n * 96 : B_DOWN + (n + 1) * 96] = down_sum[:, n * 128 : (n + 1) * 128]
        zeros = jnp.zeros((SIDE_W, SIDE_W), F32)
        small = jnp.concatenate([zeros, gate_sum, gain_sum, r.gain2_sum[...], jnp.zeros((29, SIDE_W), F32)], axis=0)
        small = jnp.concatenate([small, jnp.zeros((128, 32), F32)], axis=1).T[:SIDE_W]
        block = r.packed[layer, A_PROJ : A_PROJ + SIDE_W].astype(F32)
        r.packed[layer, A_PROJ : A_PROJ + SIDE_W] = (block + small).astype(BF)

    def feed_back_begin(layer):
        upper = nn(r.ddown[layer], r.narrow[layer])
        if layer == 0:
            upper = upper + r.upper[...]
        r.upper[...] = upper
        r.normed[...] = upper.astype(BF)
        r.acc[...] = jnp.zeros_like(r.acc)

    def feed_back_one(layer):
        def one(s):
            dactive = nt(r.normed[...], r.outer[layer, s])
            dhidden = (dactive * r.slope[layer, s].astype(F32)).astype(BF)
            r.acc[...] += nt(dhidden, r.inner[layer, s])

        return one

    def feed_back_finish(layer):
        middle = r.upper[...] + rms_back(r.mid[layer], r.gain_ffn[layer : layer + 1].astype(F32), r.acc[...])
        r.upper[...] = middle
        low = middle.astype(BF)
        for s in range(TP):
            r.dmixed[s, :, :128] = nt(low, r.out[layer, s, :128]).astype(BF)
            third = jnp.concatenate([jnp.zeros((64, WIDTH), BF), r.out[layer, s, 128:]], axis=0)
            r.dmixed[s, :, 128:] = nt(low, third).astype(BF)

    def dkv_copy(layer, s):
        return remote(
            r.dkv_sent.at[s], r.dkv_got.at[layer, s], r.dkv_s.at[layer, s], r.dkv_r.at[layer, s], partner
        )

    def attend_back_one(layer):
        def one(s):
            queries, dmixed = head_parts(r.q[layer, s], r.dmixed[s])
            keys, values = [slab(layer, s, 0), slab(layer, s, 2)], [slab(layer, s, 1), slab(layer, s, 2)]
            scores = [nt(keys[j // 2], queries[j]) + r.table[s * 3 + j].astype(F32) for j in range(3)]
            dprobs = [nt(values[j // 2], dmixed[j]) for j in range(3)]
            probs, dscores, dq_rows = [], [], []
            for j in range(3):
                p, ds = score_gradients(scores[j], r.lse[layer, s, j : j + 1], dprobs[j])
                probs.append(p)
                dscores.append(ds)
                dq = tn(keys[j // 2], ds)
                dq_rows.append(dq[64:] if j == 1 else dq[:64])
            pairs = [
                (dscores[:2], queries[:2]),
                (probs[:2], dmixed[:2]),
                ([dscores[2], probs[2]], [queries[2], dmixed[2]]),
            ]
            for m, (left, other) in enumerate(pairs):
                lanes = slice(m * 128, (m + 1) * 128)
                dkv = nn(jnp.concatenate(left, axis=1), jnp.concatenate(other, axis=0))
                r.dkv_sent[s, :, lanes] = dkv[HALF:].astype(BF)
                r.dkv[s, :, lanes] = dkv[:HALF]
            dkv_copy(layer, s).start()
            r.dq[s, :, :128] = (jnp.concatenate(dq_rows[:2], axis=0).T * 0.125).astype(BF)
            third = jnp.concatenate([dq_rows[2], jnp.zeros_like(dq_rows[2])], axis=0)
            r.dq[s, :, 128:] = (third.T * 0.125).astype(BF)

        return one

    def project_back(layer, residual):
        r.acc[...] = jnp.zeros_like(r.acc)

        def one(s, carry):
            dkv_copy(layer, s).wait_recv()
            dkv = (r.dkv[s] + r.dkv_got[layer, s].astype(F32)).astype(BF)
            left = jnp.concatenate([r.dq[s, :, :128], dkv, r.dq[s, :, 128:192]], axis=1)
            r.acc[...] += nn(left, r.qkv[layer, s])
            return carry

        lax.fori_loop(0, TP, one, 0)
        return r.upper[...] + rms_back(residual, r.gain_attn[layer : layer + 1].astype(F32), r.acc[...])

    half_rows, x_rows, y_rows = LAYER_ROWS // 2, LAYER_ROWS // 8, LAYER_ROWS // 32
    summing = {}

    def sum_step(layer, step):
        def send(n, src, dst, device):
            return remote(src, dst, r.sum_s.at[layer, n], r.sum_r.at[layer, n], device)

        if step > 0:
            arrived(summing[layer, step - 1])
        if step == 0:
            copies = [send(0, r.packed.at[layer, rows((1 - c) * half_rows, half_rows)], r.half_sum.at[layer], partner)]
        elif step == 1:
            r.half_sum[layer] = (
                r.packed[layer, rows(c * half_rows, half_rows)].astype(F32) + r.half_sum[layer].astype(F32)
            ).astype(BF)
            copies = [
                send(1 + d, r.half_sum.at[layer, rows(lax.rem(x + d + 1, TP) * x_rows, x_rows)], r.from_x.at[layer, d], x_devices[d])
                for d in range(3)
            ]
        elif step == 2:
            r.piece[layer] = (
                r.half_sum[layer, rows(x * x_rows, x_rows)].astype(F32)
                + r.from_x[layer, 0].astype(F32)
                + r.from_x[layer, 1].astype(F32)
                + r.from_x[layer, 2].astype(F32)
            ).astype(BF)
            copies = [
                send(4 + d, r.piece.at[layer, rows(lax.rem(y + d + 1, SIDES) * y_rows, y_rows)], r.from_y.at[layer, d], y_devices[d])
                for d in range(3)
            ]
        elif step == 3:
            r.small[layer] = (
                r.piece[layer, rows(y * y_rows, y_rows)].astype(F32)
                + r.from_y[layer, 0].astype(F32)
                + r.from_y[layer, 1].astype(F32)
                + r.from_y[layer, 2].astype(F32)
            ).astype(BF)
            copies = [send(7 + d, r.small.at[layer], r.from_z.at[layer, z], z_devices[d]) for d in range(3)]
            r.from_z[layer, z] = r.small[layer]
        elif step == 4:
            block = rows(c * half_rows + x * x_rows + y * y_rows, y_rows)
            parts = [r.from_z[layer, n].astype(F32) for n in range(4)]
            r.total[layer, block] = (parts[0] + parts[1] + parts[2] + parts[3]).astype(BF)
            copies = [send(10 + d, r.total.at[layer, block], r.total.at[layer, block], y_devices[d]) for d in range(3)]
        elif step == 5:
            block = rows(c * half_rows + x * x_rows, x_rows)
            copies = [send(13 + d, r.total.at[layer, block], r.total.at[layer, block], x_devices[d]) for d in range(3)]
        elif step == 6:
            block = rows(c * half_rows, half_rows)
            copies = [send(16, r.total.at[layer, block], r.total.at[layer, block], partner)]
        else:
            copies = []
        summing[layer, step] = start(copies)

    def to_all(n, source, target):
        place_here = sequence * 2 + c
        turned_rows = jnp.concatenate([source, jnp.zeros((HALF, 32), F32)], axis=1).T[:SIDE_W]
        source = (r.start_own, r.cot_own)[n]
        source[...] = turned_rows
        block = target.at[:, pl.ds(pl.multiple_of(place_here * HALF, HALF), HALF)]
        for d in range(1, TP):
            device = {"tp": lax.rem(x + d, TP), "batch": chip(y, z, parity)}
            start([remote(source, block, r.all_s.at[n, d], r.all_r.at[n, place_here], device)])
        here = pltpu.make_async_copy(source, block, r.all_own.at[n])
        over = remote(source, block, r.all_s.at[n, 0], r.all_r.at[n, place_here], partner)

        @pl.when(stays)
        def _():
            here.start()

        @pl.when(jnp.logical_not(stays))
        def _():
            over.start()

        def finish():
            for m in range(4):
                piece = target.at[:, m * HALF : (m + 1) * HALF]
                own = stays & (place_here == m)
                got = remote(source, piece, r.all_s.at[n, 0], r.all_r.at[n, m], partner)

                @pl.when(jnp.logical_not(own))
                def _():
                    got.wait_recv()

            @pl.when(stays)
            def _():
                here.wait()

            @pl.when(jnp.logical_not(stays))
            def _():
                over.wait_send()

        pending.append(finish)

    def give_back(n, source, target):
        here = pltpu.make_async_copy(source, target, r.back_own.at[n])
        over = remote(source, target, r.back_s.at[n], r.back_r.at[n], across)

        @pl.when(stays)
        def _():
            here.start()

        @pl.when(jnp.logical_not(stays))
        def _():
            over.start()

        def finish():
            @pl.when(stays)
            def _():
                here.wait()

            @pl.when(jnp.logical_not(stays))
            def _():
                over.wait()

        pending.append(finish)

    arrived(early)
    for copy in small_loads:
        copy.wait()
    make_base()
    make_table(0, 6)
    make_table(6, 12)
    r.packed[...] = jnp.zeros_like(r.packed)
    lay_out_side()
    gather("B0", "A2", "QB", "B1", "A3", "C0")

    @pl.when(stays)
    def _():
        tokens_here.start()

    @pl.when(jnp.logical_not(stays))
    def _():
        tokens_over.start()

    gather("B2", "A4", "VA", "RA", "QE", "C1", "QF", "D0", "B3", "A5", "C2", "D1", "B4", "E0", "VB", "F0", "RB", "D2")
    for copy in side_loads + weight_loads:
        copy.wait()
    r.state[0] = transposed(jnp.where(stays, r.start_own[...], r.start_got[...]))
    r.grad_side[2] = transposed(jnp.where(stays, r.cot_own[...], r.cot_got[...]))

    @pl.when(stays)
    def _():
        tokens_here.wait()

    @pl.when(jnp.logical_not(stays))
    def _():
        tokens_over.wait()

    project_begin(0, r.tokens[...].astype(F32))
    project_one(0)(0)
    gather("C3")
    loop(1, 4, project_one(0))
    gather("E1")
    loop(0, 2, attend_one(0))
    gather("B5", "WA")
    attend_one(0)(2)
    gather("C4")
    attend_one(0)(3)
    gather("VE", "F1", "RE", "E2", "D3", "VF", "C5", "RF")
    feed_begin(0, r.tokens[...].astype(F32))
    gather("WB", "F2")
    feed_one(0)(0)
    gather("D4")
    feed_one(0)(1)
    gather("E3")
    loop(2, 4, feed_one(0))
    gather("D5", "WE")
    feed_finish(0)
    project_begin(1, r.residual[...])
    side_begin(0)
    gather("F3")
    project_one(1)(0)
    gather("E4", "WF")
    loop(1, 4, project_one(1))
    loop(0, 2, attend_one(1), side_attend_one(0))
    gather("E5", "F4")
    loop(2, 4, attend_one(1), side_attend_one(0))
    side_attend_finish(0)
    feed_begin(1, r.residual[...])
    loop(0, 4, hidden_one(1))
    gather("F5")
    loop(0, 4, outer_one(1))
    feed_finish(1)
    give_back(0, r.low.at[1], r.backbone_out)
    side_begin(1)
    loop(0, 4, side_attend_one(1))
    side_back_begin(1, side_attend_finish(1))
    to_all(0, r.state[2], r.side_out)
    loop(0, 4, side_back_one(1))
    side_end(1)
    sum_step(1, 0)
    side_back_begin(0)
    sum_step(1, 1)
    feed_back_begin(1)
    loop(0, TP, feed_back_one(1), side_back_one(0))
    sum_step(1, 2)
    side_end(0)
    sum_step(0, 0)
    feed_back_finish(1)
    loop(0, 1, attend_back_one(1))
    sum_step(0, 1)
    sum_step(1, 3)
    loop(1, TP, attend_back_one(1))
    sum_step(1, 4)
    r.upper[...] = project_back(1, r.residual[...])
    sum_step(0, 2)
    to_all(1, r.grad_side[0], r.grad_start)
    feed_back_begin(0)
    loop(0, 2, feed_back_one(0))
    sum_step(0, 3)
    sum_step(1, 5)
    loop(2, TP, feed_back_one(0))
    feed_back_finish(0)
    sum_step(0, 4)
    wait_sends(lambda s: dkv_copy(1, s))
    loop(0, 2, attend_back_one(0))
    sum_step(0, 5)
    sum_step(1, 6)
    loop(2, TP, attend_back_one(0))
    pending.append(lambda: wait_sends(lambda s: dkv_copy(0, s)))
    r.normed[...] = project_back(0, r.tokens[...].astype(F32)).astype(BF)
    give_back(1, r.normed, r.grad)
    sum_step(0, 6)
    sum_step(1, 7)
    sum_step(0, 7)
    for finish in pending:
        finish()


def network(arrays):
    anywhere, vmem = pl.BlockSpec(memory_space=pl.ANY), pl.BlockSpec(memory_space=pltpu.VMEM)
    smem = pl.BlockSpec(memory_space=pltpu.SMEM)
    dma = pltpu.SemaphoreType.DMA
    return pl.pallas_call(
        network_kernel,
        out_shape=[shape(dims, dtype) for dims, dtype, _ in OUTPUTS.values()],
        in_specs=[smem if name == "lengths" else anywhere for name in INPUTS],
        out_specs=[anywhere if far else vmem for _, _, far in OUTPUTS.values()],
        scratch_shapes=[pltpu.VMEM(dims, dtype) for dims, dtype in (BUFFERS | SMALL).values()]
        + [dma(dims) for dims in SEMAPHORES.values()],
        compiler_params=pltpu.CompilerParams(
            collective_id=0, has_side_effects=True, vmem_limit_bytes=VMEM_BYTES
        ),
    )(*[arrays[name] for name in INPUTS])


def per_device(
    inputs, side_start, lengths, offset_bias, gain_attn, w_query, w_key, w_value, w_out, gain_ffn, w_inner,
    w_outer, narrowing_weight, gate_logit, side_gain1, side_qkv, side_proj, side_gain2, side_inner, side_outer,
    side_cotangent,
):
    def turned(array):
        return jnp.swapaxes(array, -1, -2)

    arrays = dict(
        inputs=inputs,
        side_start=turned(side_start),
        side_cotangent=turned(side_cotangent),
        lengths=lengths,
        bias=offset_bias,
        gain_attn=gain_attn,
        gain_ffn=gain_ffn,
        w_query=turned(w_query),
        w_key=turned(w_key),
        w_value=turned(w_value),
        w_inner=w_inner,
        w_outer=w_outer,
        w_out=w_out,
        narrow=turned(narrowing_weight),
        gate=gate_logit,
        gain1=side_gain1,
        gain2=side_gain2,
        side_qkv=side_qkv,
        proj=side_proj,
        side_inner=side_inner,
        side_outer=turned(side_outer),
    )
    results = network(arrays)
    outs = [
        shape((HALF, WIDTH), BF),
        shape((SIDE_W, 4 * HALF), F32),
        shape((HALF, WIDTH), F32),
        shape((SIDE_W, 4 * HALF), F32),
        shape((2, SIDE_W, WIDTH), F32),
        shape((2, SIDE_W), F32),
        shape((2, SIDE_W), F32),
        shape((2, SIDE_W, 3 * SIDE_W), F32),
        shape((2, SIDE_W, SIDE_W), F32),
        shape((2, SIDE_W), F32),
        shape((2, SIDE_W, SIDE_FF), F32),
        shape((2, SIDE_W, SIDE_FF), F32),
    ]
    results = call(
        results_kernel,
        (1,),
        [whole(array.shape) for array in results],
        [whole(out.shape) for out in outs],
        outs,
        nbytes=6 * 10**6,
    )(*results)
    backbone_out, side_out, grad, grad_start, down, *small, outer = results
    return (backbone_out, turned(side_out), grad, turned(grad_start), turned(down), *small, turned(outer))


def solution(mesh):
    in_specs = (
        P(("batch", "tp"), None),
        P("batch", None),
        P("batch"),
        P(),
        P(),
        P(None, None, "tp"),
        P(None, None, "tp"),
        P(None, None, "tp"),
        P(None, "tp", None),
        P(),
        P(None, None, "tp"),
        P(None, "tp", None),
        P(),
        P(),
        P(),
        P(),
        P(),
        P(),
        P(),
        P(),
        P("batch", None),
    )
    out_specs = (
        P(("batch", "tp"), None),
        P("batch", None),
        P(("batch", "tp"), None),
        P("batch", None),
        P(),
        P(),
        P(),
        P(),
        P(),
        P(),
        P(),
        P(),
    )
    return jax.shard_map(per_device, mesh=mesh, in_specs=in_specs, out_specs=out_specs, check_vma=False)
```
